256 devices in a mesh: frames: 64 (over z, x, core), mp: 4 (over y).
Axes of the slice: x: 4, y: 4, z: 8, core: 2. Of those that a mesh axis runs over, the one named last changes fastest.
Arguments:
- video_tokens: bfloat16 [64, 256, 1024], P('frames', 'mp'), may hold values from -64 to 64
- grad_output: bfloat16 [64, 256, 1024], P('frames', 'mp'), may hold values from -16 to 16
- spatial_qkv: bfloat16 [3, 1024, 1024], P(None, None, 'mp'), may hold values from -1 to 1
- spatial_out: bfloat16 [1024, 1024], P('mp'), may hold values from -0.1875 to 0.1875
- temporal_qkv: bfloat16 [3, 1024, 1024], P(None, None, 'mp'), may hold values from -1 to 1
- temporal_out: bfloat16 [1024, 1024], P('mp'), may hold values from -0.1875 to 0.1875
- clip_frames: int32 [32], replicated, may hold values from 1 to 4, 64 in all
Outputs:
- grad_tokens: bfloat16 [64, 256, 1024], P('frames', 'mp')
- grad_spatial_qkv: float32 [3, 1024, 1024], P(None, 'frames', 'mp')
- grad_spatial_out: float32 [1024, 1024], P('mp', 'frames')
- grad_temporal_qkv: float32 [3, 1024, 1024], P(None, 'frames', 'mp')
- grad_temporal_out: float32 [1024, 1024], P('mp', 'frames')
The draws below stay inside these ranges and needn't reach their ends.
Inputs may be any that keep to these rules, and one draw needn't show every extreme that they name: `clip_frames`: 32 clip lengths that sum to 64; the longest is exactly 4.
All inputs are finite; a program needn't handle non-finite values.
Results may differ from the reference program's by a relative error of at most 0.015.
Values may be sent and summed in bfloat16 or wider, within the bound.
A program may use at most 128 MiB of HBM per device.

```python
import math
import jax
import jax.numpy as jnp
import numpy as np
from jax import lax

D = 1024
HEADS = 16
HD = 64
P_SIZE = 256
FRAMES = 64
CLIPS = 32
CLIP_MOST = 4


def draw_video_tokens(key, part):
    key = jax.random.fold_in(key, 7)
    k_base, k_cols, k_rows = jax.random.split(key, 3)
    full_shape = (FRAMES, P_SIZE, D)
    base_draw = jnp.clip(jax.random.normal(k_base, full_shape, jnp.float32), -4.0, 4.0)
    col_scale = 0.3 * jnp.exp(jax.random.uniform(k_cols, (D,), jnp.float32, 0.0, math.log(10.0)))
    row_scale = 0.5 * jnp.exp(jax.random.uniform(k_rows, (FRAMES, P_SIZE, 1), jnp.float32, 0.0, math.log(10.0)))
    return (base_draw * col_scale * row_scale).astype(jnp.bfloat16)


def projection_draw(key):
    k_one, k_two, k_three = jax.random.split(key, 3)
    spread = D ** (-0.5)
    queries = jnp.clip(jax.random.normal(k_one, (D, D), jnp.float32), -4.0, 4.0) * spread
    own_keys = jnp.clip(jax.random.normal(k_two, (D, D), jnp.float32), -4.0, 4.0) * spread
    values_part = jnp.clip(jax.random.normal(k_three, (D, D), jnp.float32), -4.0, 4.0) * spread
    keys_part = own_keys
    return jnp.clip(jnp.stack([queries, keys_part, values_part]), -1.0, 1.0).astype(jnp.bfloat16)


def draw_spatial_qkv(key, part):
    key = jax.random.fold_in(key, 19)
    return projection_draw(key)


def draw_temporal_qkv(key, part):
    key = jax.random.fold_in(key, 23)
    return projection_draw(key)


def strengthened(entries, rng, source, target, shards_of, factor):
    def block_of(position):
        return (jnp.arange(entries.shape[position]) // (entries.shape[position] // shards_of)).reshape((-1,) + (1,) * (entries.ndim - 1 - position))

    near = jax.random.permutation(rng, shards_of)[block_of(target)]
    other_side = (block_of(target) + shards_of // 2) % shards_of
    return jnp.where((block_of(source) == near) | (block_of(source) == other_side), factor * entries, entries)


def steps_of(key, shape, cuts, smallest, high):
    def one(axis_at, shards_of):
        heights = jax.random.uniform(jax.random.fold_in(jax.random.fold_in(key, 6), axis_at), (shards_of,), jnp.float32, smallest / len(cuts), high / len(cuts))
        return jnp.repeat(jnp.exp(heights), shape[axis_at] // shards_of).reshape((-1,) + (1,) * (len(shape) - axis_at - 1))

    factor_of = one(*cuts[0])
    for cut in cuts[1:]:
        factor_of = factor_of * one(*cut)
    return factor_of


def profile(amount, total, most, lean):
    portions = [(1 << 20) // math.isqrt(standing ** lean) + 1 for standing in range(2, amount + 1)]
    surplus, holding = total - most - (amount - 1), [1] * (amount - 1)
    while surplus > 0:
        candidates = [i for i in range(amount - 1) if holding[i] < most]
        whole, left = sum([portions[i] for i in candidates]), surplus
        for i in candidates:
            addition = min(most - holding[i], max(1, left * portions[i] // whole), surplus)
            holding[i] = holding[i] + addition
            surplus = surplus - addition
    return np.array([most] + holding)


def uneven_parts(own_key, number_of, total, most, slope):
    if number_of == 2:
        one = jax.random.randint(own_key, (), max(1, total - most), min(most, total - 1) + 1)
        return jnp.stack([one, total - one])
    tallies = jnp.asarray(profile(number_of, total, most, slope), jnp.int32)
    pairs = (number_of - 1) // 2
    source_of, taker = tallies[1:1 + 2 * pairs:2], tallies[2:2 + 2 * pairs:2]
    slack = jnp.minimum(source_of - 1, most - taker)
    moved = jax.random.randint(jax.random.fold_in(own_key, 1), (pairs,), 0, 1 << 20) % (slack + 1)
    tallies = tallies.at[1:1 + 2 * pairs:2].set(source_of - moved).at[2:2 + 2 * pairs:2].set(taker + moved)
    return tallies[jax.random.permutation(jax.random.fold_in(own_key, 2), number_of)]


def gaussian(key, dims, scale, most, cuts=(), held_as=jnp.bfloat16):
    entries = scale * jax.random.normal(key, dims, jnp.float32)
    if cuts:
        entries = entries * steps_of(key, dims, cuts, -0.22, 0.18)
    return jnp.clip(entries, -most, most).astype(held_as)


def noise_with(rng, shape, deviation, limit, shards, heavy, kind=jnp.bfloat16):
    values = deviation * jax.random.normal(rng, shape, jnp.float32)
    if shards:
        values = values * steps_of(rng, shape, shards, -0.22, 0.18)
    return jnp.clip(strengthened(values, jax.random.fold_in(rng, 3), *heavy), -limit, limit).astype(kind)


def setup_inputs(seed: int = 0) -> dict:
    keys = jax.random.split(jax.random.key(seed), 8)
    return {
        "video_tokens": draw_video_tokens(jax.random.fold_in(keys[7], 71), 0),
        "grad_output": noise_with(keys[1], (FRAMES, P_SIZE, D), 1.0, 16.0, ((0, 64), (1, 4)), (0, 2, 64, 4.0)),
        "spatial_qkv": draw_spatial_qkv(jax.random.fold_in(keys[7], 71), 0),
        "spatial_out": gaussian(keys[3], (D, D), D ** -0.5, 0.1875, ((0, 4),)),
        "temporal_qkv": draw_temporal_qkv(jax.random.fold_in(keys[7], 71), 0),
        "temporal_out": gaussian(keys[5], (D, D), D ** -0.5, 0.1875, ((0, 4),)),
        "clip_frames": uneven_parts(keys[6], CLIPS, FRAMES, CLIP_MOST, 2).astype(jnp.int32),
    }


EPS = 1e-06
NEGATIVE = -1e+30

def normed(values_in):
    inv_rms = lax.rsqrt(lax.optimization_barrier(jnp.mean(values_in * values_in, -1, keepdims=True)) + EPS)
    return ((values_in * inv_rms).astype(jnp.bfloat16), inv_rms)

def norm_back(values_in, inv_rms, upstream):
    return inv_rms * (upstream - values_in * (inv_rms * inv_rms) * lax.optimization_barrier(jnp.mean(upstream * values_in, -1, keepdims=True)))

def rounded(tensor):
    return lax.optimization_barrier(tensor.astype(jnp.bfloat16)).astype(jnp.float32)

def probs_of(queries, keys_in, mask_bias):
    scores = jnp.einsum('bld,bmd->blm', queries.astype(jnp.float32), keys_in.astype(jnp.float32))
    scores = scores * queries.shape[-1] ** (-0.5) + mask_bias
    scores = scores - lax.optimization_barrier(jnp.max(scores, -1, keepdims=True))
    expo = jnp.exp(scores)
    return expo / lax.optimization_barrier(jnp.sum(expo, -1, keepdims=True))

def attend(queries, keys_in, values_in, mask_bias):
    probs_f = probs_of(queries, keys_in, mask_bias)
    result = jnp.einsum('blm,bmd->bld', rounded(probs_f), values_in.astype(jnp.float32))
    return result.astype(jnp.bfloat16)

def attend_back(queries, keys_in, values_in, mask_bias, upstream):
    probs_f = probs_of(queries, keys_in, mask_bias)
    up_float = upstream.astype(jnp.float32)
    d_values = jnp.einsum('blm,bld->bmd', rounded(probs_f), up_float)
    d_probs = jnp.einsum('bld,bmd->blm', up_float, values_in.astype(jnp.float32))
    row_delta = lax.optimization_barrier(jnp.sum(probs_f * d_probs, -1, keepdims=True))
    d_scores = rounded(probs_f * (d_probs - row_delta) * queries.shape[-1] ** (-0.5))
    d_queries = jnp.einsum('blm,bmd->bld', d_scores, keys_in.astype(jnp.float32))
    d_keys = jnp.einsum('blm,bld->bmd', d_scores, queries.astype(jnp.float32))
    return (d_queries.astype(jnp.bfloat16), d_keys.astype(jnp.bfloat16), d_values.astype(jnp.bfloat16))

def reference(video_tokens, grad_output, spatial_qkv, spatial_out, temporal_qkv, temporal_out, clip_frames):
    frame_total, patch_total, model_width = video_tokens.shape
    token_total = frame_total * patch_total

    def spatial_heads(flat):
        return flat.reshape(frame_total, patch_total, HEADS, HD).transpose(2, 0, 1, 3)

    def spatial_merge(stacked):
        return stacked.transpose(1, 2, 0, 3).reshape(token_total, model_width)

    def temporal_heads(flat):
        return flat.reshape(frame_total, patch_total, HEADS, HD).transpose(2, 1, 0, 3)

    def temporal_merge(stacked):
        return stacked.transpose(2, 1, 0, 3).reshape(token_total, model_width)

    def project(flat, weights):
        return jnp.stack([jnp.dot(flat, weights[which], preferred_element_type=jnp.float32) for which in range(3)]).astype(jnp.bfloat16)

    def back_project(grads, weights):
        joined = grads.transpose(1, 0, 2).reshape(token_total, 3 * model_width)
        stacked_w = weights.transpose(0, 2, 1).reshape(3 * model_width, model_width)
        return jnp.dot(joined, stacked_w, preferred_element_type=jnp.float32)

    def weight_grads(flat, grads):
        return jnp.stack([jnp.dot(flat.T, grads[which], preferred_element_type=jnp.float32) for which in range(3)])
    no_mask = jnp.zeros((patch_total, patch_total), jnp.float32)
    clip_ends = jnp.cumsum(clip_frames).astype(jnp.int32)
    frame_ids = jnp.arange(frame_total, dtype=jnp.int32)
    clip_ids = lax.optimization_barrier(jnp.sum((frame_ids[:, None] >= clip_ends[None, :]).astype(jnp.int32), axis=1))
    clip_mask = jnp.where(clip_ids[:, None] == clip_ids[None, :], 0.0, NEGATIVE).astype(jnp.float32)
    x_float = video_tokens.astype(jnp.float32)
    normed_x, inv_x = normed(x_float)
    normed_x_flat = normed_x.reshape(token_total, model_width)
    qkv_s = project(normed_x_flat, spatial_qkv)
    heads_s = (spatial_heads(qkv_s[0]), spatial_heads(qkv_s[1]), spatial_heads(qkv_s[2]))
    attn_s = spatial_merge(lax.map(lambda trio: attend(trio[0], trio[1], trio[2], no_mask), heads_s))
    hidden = x_float + jnp.dot(attn_s, spatial_out, preferred_element_type=jnp.float32).reshape(video_tokens.shape)
    normed_h, inv_h = normed(hidden)
    normed_h_flat = normed_h.reshape(token_total, model_width)
    qkv_t = project(normed_h_flat, temporal_qkv)
    heads_t = (temporal_heads(qkv_t[0]), temporal_heads(qkv_t[1]), temporal_heads(qkv_t[2]))
    attn_t = temporal_merge(lax.map(lambda trio: attend(trio[0], trio[1], trio[2], clip_mask), heads_t))
    dy_flat = grad_output.reshape(token_total, model_width)
    grad_temporal_out = jnp.dot(attn_t.T, dy_flat, preferred_element_type=jnp.float32)
    d_attn_t = jnp.dot(dy_flat, temporal_out.T, preferred_element_type=jnp.float32).astype(jnp.bfloat16)
    back_t = lax.map(lambda quad: attend_back(quad[0], quad[1], quad[2], clip_mask, quad[3]), heads_t + (temporal_heads(d_attn_t),))
    d_qkv_t = jnp.stack([temporal_merge(piece) for piece in back_t])
    grad_temporal_qkv = weight_grads(normed_h_flat, d_qkv_t)
    d_normed_h = back_project(d_qkv_t, temporal_qkv).reshape(video_tokens.shape)
    d_hidden = grad_output.astype(jnp.float32) + norm_back(hidden, inv_h, d_normed_h)
    d_hidden_b = d_hidden.astype(jnp.bfloat16).reshape(token_total, model_width)
    grad_spatial_out = jnp.dot(attn_s.T, d_hidden_b, preferred_element_type=jnp.float32)
    d_attn_s = jnp.dot(d_hidden_b, spatial_out.T, preferred_element_type=jnp.float32).astype(jnp.bfloat16)
    back_s = lax.map(lambda quad: attend_back(quad[0], quad[1], quad[2], no_mask, quad[3]), heads_s + (spatial_heads(d_attn_s),))
    d_qkv_s = jnp.stack([spatial_merge(piece) for piece in back_s])
    grad_spatial_qkv = weight_grads(normed_x_flat, d_qkv_s)
    d_normed_x = back_project(d_qkv_s, spatial_qkv).reshape(video_tokens.shape)
    grad_tokens = (d_hidden + norm_back(x_float, inv_x, d_normed_x)).astype(jnp.bfloat16)
    return (grad_tokens, grad_spatial_qkv, grad_spatial_out, grad_temporal_qkv, grad_temporal_out)
```

```python
import jax
import jax.numpy as jnp
from jax import lax
from jax.experimental import pallas as pl
from jax.experimental.pallas import tpu as pltpu
from jax.sharding import PartitionSpec as P

HD = 64
EPS = 1e-06
NEGATIVE = -1e30
FR = 64
MP = 4
XS = 4
ZS = 8
D = 1024
LW = 256
ROWS = 64
HEADS_LOC = 4
MESH = pl.DeviceIdType.MESH
F32 = jnp.float32
BF16 = jnp.bfloat16


def dot(a, b):
    return lax.dot_general(a, b, (((1,), (0,)), ((), ())), preferred_element_type=F32)


def dot_bt(a, b):
    return lax.dot_general(a, b, (((1,), (1,)), ((), ())), preferred_element_type=F32)


def dot_at(a, b):
    return lax.dot_general(a, b, (((0,), (0,)), ((), ())), preferred_element_type=F32)


def head_mask(h):
    lane = lax.broadcasted_iota(jnp.int32, (1, LW), 1)
    return jnp.where(lane // HD == h, 1.0, 0.0).astype(BF16)


def softmax(scores):
    expo = jnp.exp(scores - jnp.max(scores, -1, keepdims=True))
    return expo / jnp.sum(expo, -1, keepdims=True)


def score_grads(probs, d_probs):
    delta = jnp.sum(probs * d_probs, -1, keepdims=True)
    return (probs * (d_probs - delta) * HD ** (-0.5)).astype(BF16)


def norm_back(values_in, inv_rms, upstream):
    mean = jnp.mean(upstream * values_in, -1, keepdims=True)
    return inv_rms * (upstream - values_in * (inv_rms * inv_rms) * mean)


def kernel(
    x_ref, g_ref, cf_row, cf_col, ws_hbm, wos_hbm, wt_hbm, wot_hbm,
    tok_ref, gs_ref, gso_ref, gt_ref, gto_ref,
    ws, wos, wt, wot, xall, gall, nhall, dhall,
    perm, bias, qkvs, probs, attns, dat, hid, dhid,
    rsend, rrecv, a2send, a2recv, tq, dqkv,
    gbuf, grecv1, gsum1, grecv2, gsum2, grecv3,
    w_sem, mp_send, mp_recv, a2_ssem, a2_rsem, c_send, c_recv, x_send, x_recv, z_send, z_recv,
):
    f = lax.axis_index("frames")
    m = lax.axis_index("mp")
    core = lax.rem(f, 2)
    xpos = lax.rem(f // 2, XS)
    zpos = f // (2 * XS)

    def remote(src, dst, ssem, rsem, to_f, to_m):
        return pltpu.make_async_remote_copy(
            src_ref=src, dst_ref=dst, send_sem=ssem, recv_sem=rsem,
            device_id=(to_f, to_m), device_id_type=MESH,
        )

    pending = []

    loads = [
        pltpu.make_async_copy(hbm, vmem, w_sem.at[i])
        for i, (hbm, vmem) in enumerate(
            ((ws_hbm, ws), (wos_hbm, wos), (wot_hbm, wot), (wt_hbm, wt))
        )
    ]
    for load in loads:
        load.start()

    barrier = pltpu.get_barrier_semaphore()

    def greet(step, carry):
        pl.semaphore_signal(
            barrier, inc=1, device_id=(lax.rem(f + step, FR), m), device_id_type=MESH
        )
        return carry

    for k in range(1, MP):
        pl.semaphore_signal(
            barrier, inc=1, device_id=(f, lax.rem(m + k, MP)), device_id_type=MESH
        )
    lax.fori_loop(1, FR, greet, 0)

    def gather_mp(phase, src, buf):
        copies = []
        for k in (1, 3, 2):
            copy = remote(
                src, buf.at[m], mp_send.at[phase, k - 1], mp_recv.at[phase, k - 1],
                f, lax.rem(m + k, MP),
            )
            copy.start()
            copies.append(copy)
        pending.extend(copies)
        return copies

    def scatter_mp(phase, which):
        copies = []
        for k in (1, 3, 2):
            to = lax.rem(m + k, MP)
            copy = remote(
                rsend.at[which, to], rrecv.at[which, k - 1],
                mp_send.at[phase, k - 1], mp_recv.at[phase, k - 1], f, to,
            )
            copy.start()
            copies.append(copy)
        pending.extend(copies)
        return copies

    x = x_ref[...].astype(F32)
    inv_x = lax.rsqrt(jnp.mean(x * x, -1, keepdims=True) + EPS)
    xall[m] = (x * inv_x).astype(BF16)
    gall[m] = g_ref[...]
    pl.semaphore_wait(barrier, FR - 1 + MP - 1)

    ag_x = gather_mp(0, xall.at[m], xall)
    ag_g = gather_mp(1, g_ref, gall)

    row = lax.broadcasted_iota(jnp.int32, (LW, LW), 0)
    col = lax.broadcasted_iota(jnp.int32, (LW, LW), 1)
    source = ((row // 4) % 4) * 64 + (row // 16) * 4 + row % 4
    perm[...] = jnp.where(col == source, 1.0, 0.0).astype(BF16)
    clips = cf_row.shape[1]
    c_row = lax.broadcasted_iota(jnp.int32, (clips, clips), 0)
    c_col = lax.broadcasted_iota(jnp.int32, (clips, clips), 1)
    ends_col = jnp.sum(jnp.where(c_col <= c_row, cf_row[...], 0), axis=1, keepdims=True)
    ends_row = jnp.sum(jnp.where(c_row <= c_col, cf_col[...], 0), axis=0, keepdims=True)
    frame_lane = lax.broadcasted_iota(jnp.int32, (clips, LW), 1) // 4
    frame_sub = lax.broadcasted_iota(jnp.int32, (LW, clips), 0) // 4
    id_lane = jnp.sum(jnp.where(frame_lane >= ends_col, 1, 0), axis=0, keepdims=True)
    id_sub = jnp.sum(jnp.where(frame_sub >= ends_row, 1, 0), axis=1, keepdims=True)
    same = jnp.logical_and(id_lane == id_sub, row % 4 == col % 4)
    bias[...] = jnp.where(same, 0.0, NEGATIVE)

    masks = [head_mask(h) for h in range(HEADS_LOC)]

    loads[0].wait()
    for copy in ag_x:
        copy.wait_recv()
    x_all = xall[...].reshape(LW, D)
    for j in range(3):
        qkvs[j] = dot(x_all, ws[j]).astype(BF16)

    total = jnp.zeros((LW, LW), F32)
    for h in range(HEADS_LOC):
        p = softmax(dot_bt(qkvs[0] * masks[h], qkvs[1]) * HD ** (-0.5))
        probs[h] = p
        total = total + dot(p.astype(BF16), qkvs[2] * masks[h])
    attn = total.astype(BF16)
    attns[...] = attn.reshape(MP, ROWS, LW)

    loads[1].wait()
    for c in range(4):
        cols = pl.ds(c * 256, 256)
        rsend[0, :, :, cols] = dot(attn, wos[:, cols]).astype(BF16).reshape(MP, ROWS, 256)
    rs1 = scatter_mp(2, 0)
    own = dot(attns[m], wos[...])

    loads[2].wait()
    for copy in ag_g:
        copy.wait_recv()
    dat[...] = dot_bt(gall[...].reshape(LW, D), wot[...]).astype(BF16).reshape(MP, ROWS, LW)

    for copy in rs1:
        copy.wait_recv()
    hidden = x_ref[...].astype(F32) + own
    for k in range(3):
        hidden = hidden + rrecv[0, k].astype(F32)
    inv_h = lax.rsqrt(jnp.mean(hidden * hidden, -1, keepdims=True) + EPS)
    hid[...] = hidden
    nhall[m] = (hidden * inv_h).astype(BF16)
    ag_h = gather_mp(3, nhall.at[m], nhall)

    loads[3].wait()

    def exchange_block(which, block):
        def send(step, carry):
            to = block * 16 + lax.rem(f + step, 16)

            @pl.when(to != f)
            def _():
                remote(
                    a2send.at[which, to], a2recv.at[which, f],
                    a2_ssem.at[which], a2_rsem.at[which], to, m,
                ).start()

            return carry

        lax.fori_loop(0, 16, send, 0)

    def exchange_wait(which):
        some = pl.ds(0, FR - 1)
        return remote(
            a2send.at[which, some], a2recv.at[which, some],
            a2_ssem.at[which], a2_rsem.at[which], f, m,
        )

    def pack(which, block, parts):
        joined = jnp.concatenate(parts, axis=0)
        a2send[which, pl.ds(block * 16, 16)] = (
            dot(perm[...], joined).astype(BF16).reshape(16, 16, LW)
        )

    def unpack(which, target):
        for b in range(4):
            block = a2recv[which, 16 * b : 16 * b + 16].reshape(LW, LW)
            apart = dot_at(perm[...], block).astype(BF16)
            for t in range(4):
                target[t, 64 * b : 64 * b + 64] = apart[64 * t : 64 * t + 64]

    for at, k in enumerate((0, 1, 3, 2)):
        block = lax.rem(m + MP - k, MP)
        if k:
            ag_h[at - 1].wait_recv()
        rows = nhall[block]
        parts = [dot(rows, wt[j]).astype(BF16) for j in range(3)]
        pack(0, block, parts + [dat[block]])
        exchange_block(0, block)
    a2recv[0, f] = a2send[0, f]
    exchange_wait(0).wait_recv()
    unpack(0, tq)

    zero = jnp.zeros((LW, LW), F32)
    attn_t, d_q, d_k, d_v = zero, zero, zero, zero
    for h in range(HEADS_LOC):
        qm = tq[0] * masks[h]
        km = tq[1] * masks[h]
        vm = tq[2] * masks[h]
        om = tq[3] * masks[h]
        p = softmax(dot_bt(qm, tq[1]) * HD ** (-0.5) + bias[...])
        pb = p.astype(BF16)
        attn_t = attn_t + dot(pb, vm)
        d_v = d_v + dot_at(pb, om)
        ds = score_grads(p, dot_bt(om, tq[2]))
        d_q = d_q + dot(ds, km)
        d_k = d_k + dot_at(ds, qm)
    back = [t.astype(BF16) for t in (d_q, d_k, d_v, attn_t)]
    for b in range(4):
        pack(1, b, [t[64 * b : 64 * b + 64] for t in back])
    for b in range(4):
        exchange_block(1, lax.rem(f // 16 + b, 4))
    a2recv[1, f] = a2send[1, f]
    exchange_wait(1).wait_recv()
    unpack(1, dqkv)

    def project_back(which, grads, weights):
        for c in range(4):
            cols = pl.ds(c * 256, 256)
            part = dot_bt(grads[0], weights[0, cols])
            part = part + dot_bt(grads[1], weights[1, cols])
            part = part + dot_bt(grads[2], weights[2, cols])
            rsend[which, :, :, cols] = part.astype(BF16).reshape(MP, ROWS, 256)

    def own_back(grads_ref, weights):
        mine = pl.ds(pl.multiple_of(m * ROWS, ROWS), ROWS)
        part = dot_bt(grads_ref[0, mine], weights[0])
        part = part + dot_bt(grads_ref[1, mine], weights[1])
        return part + dot_bt(grads_ref[2, mine], weights[2])

    def weight_grad(which, j, left_ref, right):
        for c in range(4):
            left = left_ref[:, :, c * 256 : (c + 1) * 256].reshape(LW, 256)
            gbuf[which, j, 8 * c : 8 * c + 8] = (
                dot_at(left, right).astype(BF16).reshape(8, 2, 16, LW)
            )

    def core_send(which):
        copy = remote(
            gbuf.at[which, :, :, 1 - core], grecv1.at[which],
            c_send.at[which], c_recv.at[which], f + 1 - 2 * core, m,
        )
        copy.start()
        pending.append(copy)
        return copy

    def core_sum_x_send(which, copy):
        copy.wait_recv()
        for j in range(4):
            summed = gbuf[which, j, :, core].astype(F32) + grecv1[which, j].astype(F32)
            gsum1[which, j] = summed.astype(BF16).reshape(ZS, XS, 16, LW)
        copies = []
        for k in (1, 3, 2):
            to = lax.rem(xpos + k, XS)
            copy = remote(
                gsum1.at[which, :, :, to], grecv2.at[which, k - 1],
                x_send.at[which, k - 1], x_recv.at[which, k - 1],
                (zpos * XS + to) * 2 + core, m,
            )
            copy.start()
            copies.append(copy)
        pending.extend(copies)
        return copies

    def x_sum_z_send(which, copies):
        for copy in copies:
            copy.wait_recv()
        for j in range(4):
            summed = gsum1[which, j, :, xpos].astype(F32)
            for k in range(3):
                summed = summed + grecv2[which, k, j].astype(F32)
            gsum2[which, j] = summed.astype(BF16)
        copies = []
        for k in range(1, ZS):
            to = lax.rem(zpos + k, ZS)
            copy = remote(
                gsum2.at[which, :, to], grecv3.at[which, k - 1],
                z_send.at[which, k - 1], z_recv.at[which, k - 1],
                (to * XS + xpos) * 2 + core, m,
            )
            copy.start()
            copies.append(copy)
        pending.extend(copies)
        return copies

    def z_sum(which, copies, qkv_out, out_out):
        for copy in copies:
            copy.wait_recv()
        for j in range(4):
            summed = gsum2[which, j, zpos].astype(F32)
            for k in range(ZS - 1):
                summed = summed + grecv3[which, k, j].astype(F32)
            if j < 3:
                qkv_out[j] = summed
            else:
                out_out[...] = summed

    project_back(1, [dqkv[j] for j in range(3)], wt)
    rs2 = scatter_mp(4, 1)
    for j in range(3):
        weight_grad(0, j, nhall, dqkv[j])
    weight_grad(0, 3, gall, dqkv[3])
    core_t = core_send(0)
    d_nh = own_back(dqkv, wt)
    for copy in rs2:
        copy.wait_recv()
    for k in range(3):
        d_nh = d_nh + rrecv[1, k].astype(F32)
    hidden = hid[...]
    inv_h = lax.rsqrt(jnp.mean(hidden * hidden, -1, keepdims=True) + EPS)
    d_hidden = g_ref[...].astype(F32) + norm_back(hidden, inv_h, d_nh)
    dhid[...] = d_hidden
    dhall[m] = d_hidden.astype(BF16)
    ag_d = gather_mp(5, dhall.at[m], dhall)
    x_t = core_sum_x_send(0, core_t)
    for copy in ag_d:
        copy.wait_recv()

    das = dot_bt(dhall[...].reshape(LW, D), wos[...]).astype(BF16)
    d_q, d_k, d_v = zero, zero, zero
    for h in range(HEADS_LOC):
        om = das * masks[h]
        p = probs[h]
        d_v = d_v + dot_at(p.astype(BF16), om)
        ds = score_grads(p, dot_bt(om, qkvs[2]))
        d_q = d_q + dot(ds, qkvs[1] * masks[h])
        d_k = d_k + dot_at(ds, qkvs[0] * masks[h])
    grads_s = [t.astype(BF16) for t in (d_q, d_k, d_v)]
    for j in range(3):
        dqkv[4 + j] = grads_s[j]
        weight_grad(1, j, xall, grads_s[j])
    weight_grad(1, 3, dhall, attns[...].reshape(LW, LW))
    core_s = core_send(1)
    project_back(2, grads_s, ws)
    rs3 = scatter_mp(6, 2)
    z_t = x_sum_z_send(0, x_t)
    x_s = core_sum_x_send(1, core_s)
    d_nx = own_back(dqkv.at[4:7], ws)
    for copy in rs3:
        copy.wait_recv()
    for k in range(3):
        d_nx = d_nx + rrecv[2, k].astype(F32)
    x = x_ref[...].astype(F32)
    inv_x = lax.rsqrt(jnp.mean(x * x, -1, keepdims=True) + EPS)
    tok_ref[...] = (dhid[...] + norm_back(x, inv_x, d_nx)).astype(BF16)
    z_sum(0, z_t, gt_ref, gto_ref)
    z_s = x_sum_z_send(1, x_s)
    z_sum(1, z_s, gs_ref, gso_ref)
    for copy in pending:
        copy.wait_send()
    exchange_wait(0).wait_send()
    exchange_wait(1).wait_send()


def shards(x, g, ws, wos, wt, wot, clip_frames):
    clips = clip_frames.shape[0]
    vmem = pl.BlockSpec(memory_space=pltpu.VMEM)
    anywhere = pl.BlockSpec(memory_space=pl.ANY)
    dma = pltpu.SemaphoreType.DMA
    scratch = [
        pltpu.VMEM((3, D, LW), BF16),
        pltpu.VMEM((LW, D), BF16),
        pltpu.VMEM((3, D, LW), BF16),
        pltpu.VMEM((LW, D), BF16),
        pltpu.VMEM((MP, ROWS, D), BF16),
        pltpu.VMEM((MP, ROWS, D), BF16),
        pltpu.VMEM((MP, ROWS, D), BF16),
        pltpu.VMEM((MP, ROWS, D), BF16),
        pltpu.VMEM((LW, LW), BF16),
        pltpu.VMEM((LW, LW), F32),
        pltpu.VMEM((3, LW, LW), BF16),
        pltpu.VMEM((HEADS_LOC, LW, LW), F32),
        pltpu.VMEM((MP, ROWS, LW), BF16),
        pltpu.VMEM((MP, ROWS, LW), BF16),
        pltpu.VMEM((ROWS, D), F32),
        pltpu.VMEM((ROWS, D), F32),
        pltpu.VMEM((3, MP, ROWS, D), BF16),
        pltpu.VMEM((3, MP - 1, ROWS, D), BF16),
        pltpu.VMEM((2, FR, 16, LW), BF16),
        pltpu.VMEM((2, FR, 16, LW), BF16),
        pltpu.VMEM((4, LW, LW), BF16),
        pltpu.VMEM((7, LW, LW), BF16),
        pltpu.VMEM((2, 4, FR // 2, 2, 16, LW), BF16),
        pltpu.VMEM((2, 4, FR // 2, 16, LW), BF16),
        pltpu.VMEM((2, 4, ZS, XS, 16, LW), BF16),
        pltpu.VMEM((2, XS - 1, 4, ZS, 16, LW), BF16),
        pltpu.VMEM((2, 4, ZS, 16, LW), BF16),
        pltpu.VMEM((2, ZS - 1, 4, 16, LW), BF16),
        dma((4,)),
        dma((7, 3)),
        dma((7, 3)),
        dma((2,)),
        dma((2,)),
        dma((2,)),
        dma((2,)),
        dma((2, XS - 1)),
        dma((2, XS - 1)),
        dma((2, ZS - 1)),
        dma((2, ZS - 1)),
    ]
    tokens, gs, gso, gt, gto = pl.pallas_call(
        kernel,
        out_shape=(
            jax.ShapeDtypeStruct((ROWS, D), BF16),
            jax.ShapeDtypeStruct((3, 16, LW), F32),
            jax.ShapeDtypeStruct((16, LW), F32),
            jax.ShapeDtypeStruct((3, 16, LW), F32),
            jax.ShapeDtypeStruct((16, LW), F32),
        ),
        in_specs=[vmem] * 4 + [anywhere] * 4,
        out_specs=[vmem] * 5,
        scratch_shapes=scratch,
        compiler_params=pltpu.CompilerParams(
            collective_id=0, has_side_effects=True, vmem_limit_bytes=48 * 1024 * 1024
        ),
        cost_estimate=pl.CostEstimate(
            flops=3_500_000_000, bytes_accessed=6_000_000, transcendentals=1_000_000
        ),
    )(
        x.reshape(ROWS, D), g.reshape(ROWS, D),
        clip_frames.reshape(1, clips), clip_frames.reshape(clips, 1),
        ws, wos, wt, wot,
    )
    return tokens.reshape(1, ROWS, D), gs, gso.T, gt, gto.T


def solution(mesh):
    placed = (
        P("frames", "mp", None),
        P("frames", "mp", None),
        P(None, None, "mp"),
        P("mp", None),
        P(None, None, "mp"),
        P("mp", None),
        P(),
    )
    return jax.shard_map(
        shards,
        mesh=mesh,
        in_specs=placed,
        out_specs=(
            P("frames", "mp", None),
            P(None, "frames", "mp"),
            P("mp", "frames"),
            P(None, "frames", "mp"),
            P("mp", "frames"),
        ),
        check_vma=False,
    )
```

```python
import jax
import jax.numpy as jnp
from jax import lax
from jax.experimental import pallas as pl
from jax.experimental.pallas import tpu as pltpu
from jax.sharding import PartitionSpec as P

HD = 64
EPS = 1e-06
NEGATIVE = -1e30
FR = 64
MP = 4
XS = 4
ZS = 8
PL = 8
HALO = 3
D = 1024
LW = 256
ROWS = 64
HEADS_LOC = 4
MESH = pl.DeviceIdType.MESH
F32 = jnp.float32
BF16 = jnp.bfloat16


def dot(a, b):
    return lax.dot_general(a, b, (((1,), (0,)), ((), ())), preferred_element_type=F32)


def dot_bt(a, b):
    return lax.dot_general(a, b, (((1,), (1,)), ((), ())), preferred_element_type=F32)


def dot_at(a, b):
    return lax.dot_general(a, b, (((0,), (0,)), ((), ())), preferred_element_type=F32)


def head_mask(h):
    lane = lax.broadcasted_iota(jnp.int32, (1, LW), 1)
    return jnp.where(lane // HD == h, 1.0, 0.0).astype(BF16)


def softmax(scores):
    expo = jnp.exp(scores - jnp.max(scores, -1, keepdims=True))
    return expo / jnp.sum(expo, -1, keepdims=True)


def score_grads(probs, d_probs):
    delta = jnp.sum(probs * d_probs, -1, keepdims=True)
    return (probs * (d_probs - delta) * HD ** (-0.5)).astype(BF16)


def norm_back(values_in, inv_rms, upstream):
    mean = jnp.mean(upstream * values_in, -1, keepdims=True)
    return inv_rms * (upstream - values_in * (inv_rms * inv_rms) * mean)


def kernel(
    x_hbm, g_hbm, cf_hbm, ws_hbm, wos_hbm, wt_hbm, wot_hbm,
    tok_ref, gs_ref, gso_ref, gt_ref, gto_ref,
    x_ref, g_ref, cf_row, ws, wos, wt, wot, xall, gall, nhall, dhall,
    bias, qkvs, probs, attns, hid, dhid,
    rsend, rrecv, tsend, tbuf, tres, dqkv, dqs,
    gbuf, grecv1, gsum1, grecv2, gsum2, grecv3,
    w_sem, mp_send, mp_recv, t_send, t_recv, h_send, h_recv, b_send, b_recv,
    c_send, c_recv, x_send, x_recv, z_send, z_recv,
):
    f = lax.axis_index("frames")
    m = lax.axis_index("mp")
    core = lax.rem(f, 2)
    xpos = lax.rem(f // 2, XS)
    zpos = f // PL
    w = lax.rem(f, PL)

    def remote(src, dst, ssem, rsem, to_f, to_m):
        return pltpu.make_async_remote_copy(
            src_ref=src, dst_ref=dst, send_sem=ssem, recv_sem=rsem,
            device_id=(to_f, to_m), device_id_type=MESH,
        )

    pending = []

    loads = [
        pltpu.make_async_copy(hbm, vmem, w_sem.at[i])
        for i, (hbm, vmem) in enumerate(
            (
                (x_hbm, x_ref), (g_hbm, g_ref), (cf_hbm, cf_row),
                (ws_hbm, ws), (wos_hbm, wos), (wot_hbm, wot), (wt_hbm, wt),
            )
        )
    ]
    for load in loads:
        load.start()

    barrier = pltpu.get_barrier_semaphore()

    for k in range(1, MP):
        pl.semaphore_signal(
            barrier, inc=1, device_id=(f, lax.rem(m + k, MP)), device_id_type=MESH
        )
    for k in range(1, PL):
        pl.semaphore_signal(
            barrier, inc=1, device_id=(zpos * PL + lax.rem(w + k, PL), m), device_id_type=MESH
        )
    for k in range(1, ZS):
        pl.semaphore_signal(
            barrier, inc=1, device_id=(lax.rem(zpos + k, ZS) * PL + w, m), device_id_type=MESH
        )

    def gather_mp(phase, src, buf):
        copies = []
        for k in (1, 3, 2):
            copy = remote(
                src, buf.at[m], mp_send.at[phase, k - 1], mp_recv.at[phase, k - 1],
                f, lax.rem(m + k, MP),
            )
            copy.start()
            copies.append(copy)
        pending.extend(copies)
        return copies

    def scatter_mp(phase, which):
        copies = []
        for k in (1, 3, 2):
            to = lax.rem(m + k, MP)
            copy = remote(
                rsend.at[which, to], rrecv.at[which, k - 1],
                mp_send.at[phase, k - 1], mp_recv.at[phase, k - 1], f, to,
            )
            copy.start()
            copies.append(copy)
        pending.extend(copies)
        return copies

    loads[0].wait()
    x = x_ref[...].astype(F32)
    inv_x = lax.rsqrt(jnp.mean(x * x, -1, keepdims=True) + EPS)
    xall[m] = (x * inv_x).astype(BF16)
    pl.semaphore_wait(barrier, MP - 1 + PL - 1 + ZS - 1)

    ag_x = gather_mp(0, xall.at[m], xall)

    loads[1].wait()
    loads[2].wait()
    gall[m] = g_ref[...]
    row = lax.broadcasted_iota(jnp.int32, (LW, LW), 0)
    col = lax.broadcasted_iota(jnp.int32, (LW, LW), 1)
    clips = cf_row.shape[1]
    c_row = lax.broadcasted_iota(jnp.int32, (clips, clips), 0)
    c_col = lax.broadcasted_iota(jnp.int32, (clips, clips), 1)
    ends_col = jnp.sum(jnp.where(c_col <= c_row, cf_row[...], 0), axis=1, keepdims=True)
    ends_row = jnp.sum(jnp.where(c_row == c_col, ends_col, 0), axis=0, keepdims=True)

    def clip_of(slot, ends, axis):
        frame = lax.rem(zpos * PL + FR - HALO + slot, FR)
        count = jnp.sum(jnp.where(frame >= ends, 1, 0), axis=axis, keepdims=True)
        return count

    slot_lane = lax.broadcasted_iota(jnp.int32, (clips, LW), 1) // 16
    slot_sub = lax.broadcasted_iota(jnp.int32, (LW, clips), 0) // 16
    id_lane = clip_of(slot_lane, ends_col, 0)
    id_sub = clip_of(slot_sub, ends_row, 1)
    used = PL + 2 * HALO
    id_lane = jnp.where(col[:1] // 16 < used, id_lane, -1)
    id_sub = jnp.where(row[:, :1] // 16 < used, id_sub, -1)
    same = jnp.logical_and(id_lane == id_sub, row % 16 == col % 16)
    bias[...] = jnp.where(same, 0.0, NEGATIVE)
    for t in range(4):
        for g in range(2):
            tbuf[t, g, used:] = jnp.zeros((16 - used, 16, LW), BF16)

    masks = [head_mask(h) for h in range(HEADS_LOC)]

    loads[3].wait()
    for copy in ag_x:
        copy.wait_recv()
    ag_g = gather_mp(1, g_ref, gall)
    x_all = xall[...].reshape(LW, D)
    for j in range(3):
        qkvs[j] = dot(x_all, ws[j]).astype(BF16)

    total = jnp.zeros((LW, LW), F32)
    for h in range(HEADS_LOC):
        p = softmax(dot_bt(qkvs[0] * masks[h], qkvs[1]) * HD ** (-0.5))
        probs[h] = p
        total = total + dot(p.astype(BF16), qkvs[2] * masks[h])
    attn = total.astype(BF16)
    attns[...] = attn.reshape(MP, ROWS, LW)

    loads[4].wait()
    for c in range(4):
        cols = pl.ds(c * 256, 256)
        rsend[0, :, :, cols] = dot(attn, wos[:, cols]).astype(BF16).reshape(MP, ROWS, 256)
    rs1 = scatter_mp(2, 0)
    own = dot(attns[m], wos[...])

    loads[5].wait()
    for copy in ag_g:
        copy.wait_recv()
    tsend[3] = dot_bt(gall[...].reshape(LW, D), wot[...]).astype(BF16).reshape(2, PL, 16, LW)

    for copy in rs1:
        copy.wait_recv()
    hidden = x_ref[...].astype(F32) + own
    for k in range(3):
        hidden = hidden + rrecv[0, k].astype(F32)
    inv_h = lax.rsqrt(jnp.mean(hidden * hidden, -1, keepdims=True) + EPS)
    hid[...] = hidden
    nhall[m] = (hidden * inv_h).astype(BF16)
    ag_h = gather_mp(3, nhall.at[m], nhall)

    loads[6].wait()
    for copy in ag_h:
        copy.wait_recv()
    h_all = nhall[...].reshape(LW, D)
    for j in range(3):
        tsend[j] = dot(h_all, wt[j]).astype(BF16).reshape(2, PL, 16, LW)

    there = []
    for g in range(2):
        for k in range(1, PL):
            to = lax.rem(w + k, PL)
            copy = remote(
                tsend.at[:, g, to], tbuf.at[:, g, HALO + w],
                t_send.at[g, k - 1], t_recv.at[g, k - 1], zpos * PL + to, m,
            )
            copy.start()
            there.append(copy)
    pending.extend(there)
    for t in range(4):
        for g in range(2):
            tbuf[t, g, HALO + w] = tsend[t, g, w]

    def hand_on(g, frame):
        def to_plane(step, slot):
            return remote(
                tbuf.at[:, g, HALO + frame], tbuf.at[:, g, slot],
                h_send.at[g], h_recv.at[g], lax.rem(zpos + step, ZS) * PL + w, m,
            )

        @pl.when(frame < HALO)
        def _():
            to_plane(ZS - 1, HALO + PL + frame).start()

        @pl.when(frame >= PL - HALO)
        def _():
            to_plane(1, frame - (PL - HALO)).start()

    def hand_wait(g):
        some = pl.ds(0, 2 * HALO)
        return remote(
            tbuf.at[:, g, some], tbuf.at[:, g, some], h_send.at[g], h_recv.at[g], f, m
        )

    for g in range(2):
        hand_on(g, w)
        for k in range(1, PL):
            there[g * (PL - 1) + k - 1].wait_recv()
            hand_on(g, lax.rem(w + PL - k, PL))

    zero = jnp.zeros((LW, LW), F32)
    back = []
    for g in range(2):
        hand_wait(g).wait_recv()
        queries, keys, values, upstream = [tbuf[t, g].reshape(LW, LW) for t in range(4)]
        attn_t, d_q, d_k, d_v = zero, zero, zero, zero
        for h in range(HEADS_LOC):
            qm = queries * masks[h]
            om = upstream * masks[h]
            p = softmax(dot_bt(qm, keys) * HD ** (-0.5) + bias[...])
            pb = p.astype(BF16)
            attn_t = attn_t + dot(pb, values * masks[h])
            d_v = d_v + dot_at(pb, om)
            ds = score_grads(p, dot_bt(om, values))
            d_q = d_q + dot(ds, keys * masks[h])
            d_k = d_k + dot_at(ds, qm)
        for t, full in enumerate((d_q, d_k, d_v, attn_t)):
            mine = full[16 * HALO : 16 * (HALO + PL)]
            tres[t, g] = mine.astype(BF16).reshape(PL, 16, LW)
        for k in range(1, PL):
            to = lax.rem(w + k, PL)
            copy = remote(
                tres.at[:, g, to], dqkv.at[:, g, w],
                b_send.at[g, k - 1], b_recv.at[g, k - 1], zpos * PL + to, m,
            )
            copy.start()
            back.append(copy)
        for t in range(4):
            dqkv[t, g, w] = tres[t, g, w]
    pending.extend(back)
    for copy in back:
        copy.wait_recv()

    def project_back(which, grads, weights):
        for c in range(4):
            cols = pl.ds(c * 256, 256)
            part = dot_bt(grads[0], weights[0, cols])
            part = part + dot_bt(grads[1], weights[1, cols])
            part = part + dot_bt(grads[2], weights[2, cols])
            rsend[which, :, :, cols] = part.astype(BF16).reshape(MP, ROWS, 256)

    def own_back(grads, weights):
        part = dot_bt(grads[0], weights[0])
        part = part + dot_bt(grads[1], weights[1])
        return part + dot_bt(grads[2], weights[2])

    def weight_grad(which, j, left_ref, right):
        for c in range(4):
            left = left_ref[:, :, c * 256 : (c + 1) * 256].reshape(LW, 256)
            gbuf[which, j, 8 * c : 8 * c + 8] = (
                dot_at(left, right).astype(BF16).reshape(8, 2, 16, LW)
            )

    def core_send(which):
        copy = remote(
            gbuf.at[which, :, :, 1 - core], grecv1.at[which],
            c_send.at[which], c_recv.at[which], f + 1 - 2 * core, m,
        )
        copy.start()
        pending.append(copy)
        return copy

    def core_sum_x_send(which, copy):
        copy.wait_recv()
        for j in range(4):
            summed = gbuf[which, j, :, core].astype(F32) + grecv1[which, j].astype(F32)
            gsum1[which, j] = summed.astype(BF16).reshape(ZS, XS, 16, LW)
        copies = []
        for k in (1, 3, 2):
            to = lax.rem(xpos + k, XS)
            copy = remote(
                gsum1.at[which, :, :, to], grecv2.at[which, k - 1],
                x_send.at[which, k - 1], x_recv.at[which, k - 1],
                (zpos * XS + to) * 2 + core, m,
            )
            copy.start()
            copies.append(copy)
        pending.extend(copies)
        return copies

    def x_sum_z_send(which, copies):
        for copy in copies:
            copy.wait_recv()
        for j in range(4):
            summed = gsum1[which, j, :, xpos].astype(F32)
            for k in range(3):
                summed = summed + grecv2[which, k, j].astype(F32)
            gsum2[which, j] = summed.astype(BF16)
        copies = []
        for k in range(1, ZS):
            to = lax.rem(zpos + k, ZS)
            copy = remote(
                gsum2.at[which, :, to], grecv3.at[which, k - 1],
                z_send.at[which, k - 1], z_recv.at[which, k - 1],
                (to * XS + xpos) * 2 + core, m,
            )
            copy.start()
            copies.append(copy)
        pending.extend(copies)
        return copies

    def z_sum(which, copies, qkv_out, out_out):
        for copy in copies:
            copy.wait_recv()
        for j in range(4):
            summed = gsum2[which, j, zpos].astype(F32)
            for k in range(ZS - 1):
                summed = summed + grecv3[which, k, j].astype(F32)
            if j < 3:
                qkv_out[j] = summed
            else:
                out_out[...] = summed

    grads_t = [dqkv[j].reshape(LW, LW) for j in range(4)]
    project_back(1, grads_t[:3], wt)
    rs2 = scatter_mp(4, 1)
    for j in range(3):
        weight_grad(0, j, nhall, grads_t[j])
    weight_grad(0, 3, gall, grads_t[3])
    core_t = core_send(0)
    half = pl.ds(4 * lax.rem(m, 2), 4)
    d_nh = own_back([dqkv[j, m // 2, half].reshape(ROWS, LW) for j in range(3)], wt)
    for copy in rs2:
        copy.wait_recv()
    for k in range(3):
        d_nh = d_nh + rrecv[1, k].astype(F32)
    hidden = hid[...]
    inv_h = lax.rsqrt(jnp.mean(hidden * hidden, -1, keepdims=True) + EPS)
    d_hidden = g_ref[...].astype(F32) + norm_back(hidden, inv_h, d_nh)
    dhid[...] = d_hidden
    dhall[m] = d_hidden.astype(BF16)
    ag_d = gather_mp(5, dhall.at[m], dhall)
    x_t = core_sum_x_send(0, core_t)
    for copy in ag_d:
        copy.wait_recv()

    das = dot_bt(dhall[...].reshape(LW, D), wos[...]).astype(BF16)
    d_q, d_k, d_v = zero, zero, zero
    for h in range(HEADS_LOC):
        om = das * masks[h]
        p = probs[h]
        d_v = d_v + dot_at(p.astype(BF16), om)
        ds = score_grads(p, dot_bt(om, qkvs[2]))
        d_q = d_q + dot(ds, qkvs[1] * masks[h])
        d_k = d_k + dot_at(ds, qkvs[0] * masks[h])
    grads_s = [t.astype(BF16) for t in (d_q, d_k, d_v)]
    for j in range(3):
        dqs[j] = grads_s[j].reshape(MP, ROWS, LW)
        weight_grad(1, j, xall, grads_s[j])
    weight_grad(1, 3, dhall, attns[...].reshape(LW, LW))
    core_s = core_send(1)
    project_back(2, grads_s, ws)
    rs3 = scatter_mp(6, 2)
    z_t = x_sum_z_send(0, x_t)
    x_s = core_sum_x_send(1, core_s)
    d_nx = own_back([dqs[j, m] for j in range(3)], ws)
    for copy in rs3:
        copy.wait_recv()
    for k in range(3):
        d_nx = d_nx + rrecv[2, k].astype(F32)
    x = x_ref[...].astype(F32)
    inv_x = lax.rsqrt(jnp.mean(x * x, -1, keepdims=True) + EPS)
    tok_ref[...] = (dhid[...] + norm_back(x, inv_x, d_nx)).astype(BF16)
    z_sum(0, z_t, gt_ref, gto_ref)
    z_s = x_sum_z_send(1, x_s)
    z_sum(1, z_s, gs_ref, gso_ref)
    for copy in pending:
        copy.wait_send()
    for g in range(2):
        hand_wait(g).wait_send()


def shards(x, g, ws, wos, wt, wot, clip_frames):
    clips = clip_frames.shape[0]
    vmem = pl.BlockSpec(memory_space=pltpu.VMEM)
    dma = pltpu.SemaphoreType.DMA
    scratch = [
        pltpu.VMEM((ROWS, D), BF16),
        pltpu.VMEM((ROWS, D), BF16),
        pltpu.VMEM((1, clips), jnp.int32),
        pltpu.VMEM((3, D, LW), BF16),
        pltpu.VMEM((LW, D), BF16),
        pltpu.VMEM((3, D, LW), BF16),
        pltpu.VMEM((LW, D), BF16),
        pltpu.VMEM((MP, ROWS, D), BF16),
        pltpu.VMEM((MP, ROWS, D), BF16),
        pltpu.VMEM((MP, ROWS, D), BF16),
        pltpu.VMEM((MP, ROWS, D), BF16),
        pltpu.VMEM((LW, LW), F32),
        pltpu.VMEM((3, LW, LW), BF16),
        pltpu.VMEM((HEADS_LOC, LW, LW), F32),
        pltpu.VMEM((MP, ROWS, LW), BF16),
        pltpu.VMEM((ROWS, D), F32),
        pltpu.VMEM((ROWS, D), F32),
        pltpu.VMEM((3, MP, ROWS, D), BF16),
        pltpu.VMEM((3, MP - 1, ROWS, D), BF16),
        pltpu.VMEM((4, 2, PL, 16, LW), BF16),
        pltpu.VMEM((4, 2, 16, 16, LW), BF16),
        pltpu.VMEM((4, 2, PL, 16, LW), BF16),
        pltpu.VMEM((4, 2, PL, 16, LW), BF16),
        pltpu.VMEM((3, MP, ROWS, LW), BF16),
        pltpu.VMEM((2, 4, FR // 2, 2, 16, LW), BF16),
        pltpu.VMEM((2, 4, FR // 2, 16, LW), BF16),
        pltpu.VMEM((2, 4, ZS, XS, 16, LW), BF16),
        pltpu.VMEM((2, XS - 1, 4, ZS, 16, LW), BF16),
        pltpu.VMEM((2, 4, ZS, 16, LW), BF16),
        pltpu.VMEM((2, ZS - 1, 4, 16, LW), BF16),
        dma((7,)),
        dma((7, 3)),
        dma((7, 3)),
        dma((2, PL - 1)),
        dma((2, PL - 1)),
        dma((2,)),
        dma((2,)),
        dma((2, PL - 1)),
        dma((2, PL - 1)),
        dma((2,)),
        dma((2,)),
        dma((2, XS - 1)),
        dma((2, XS - 1)),
        dma((2, ZS - 1)),
        dma((2, ZS - 1)),
    ]
    tokens, gs, gso, gt, gto = pl.pallas_call(
        kernel,
        out_shape=(
            jax.ShapeDtypeStruct((ROWS, D), BF16),
            jax.ShapeDtypeStruct((3, 16, LW), F32),
            jax.ShapeDtypeStruct((16, LW), F32),
            jax.ShapeDtypeStruct((3, 16, LW), F32),
            jax.ShapeDtypeStruct((16, LW), F32),
        ),
        in_specs=[pl.BlockSpec(memory_space=pltpu.HBM)] * 7,
        out_specs=[vmem] * 5,
        scratch_shapes=scratch,
        compiler_params=pltpu.CompilerParams(
            collective_id=0, has_side_effects=True, vmem_limit_bytes=60 * 1024 * 1024
        ),
        cost_estimate=pl.CostEstimate(
            flops=3_500_000_000, bytes_accessed=6_000_000, transcendentals=1_000_000
        ),
    )(
        x.reshape(ROWS, D), g.reshape(ROWS, D), clip_frames.reshape(1, clips), ws, wos, wt, wot,
    )
    return tokens.reshape(1, ROWS, D), gs, gso.T, gt, gto.T


def solution(mesh):
    placed = (
        P("frames", "mp", None),
        P("frames", "mp", None),
        P(None, None, "mp"),
        P("mp", None),
        P(None, None, "mp"),
        P("mp", None),
        P(),
    )
    return jax.shard_map(
        shards,
        mesh=mesh,
        in_specs=placed,
        out_specs=(
            P("frames", "mp", None),
            P(None, "frames", "mp"),
            P("mp", "frames"),
            P(None, "frames", "mp"),
            P("mp", "frames"),
        ),
        check_vma=False,
    )
```

```python
import jax
import jax.numpy as jnp
from jax import lax
from jax.experimental import pallas as pl
from jax.experimental.pallas import tpu as pltpu
from jax.sharding import PartitionSpec as P

HD = 64
EPS = 1e-06
NEGATIVE = -1e30
FR = 64
MP = 4
XS = 4
ZS = 8
PL = 8
HALO = 3
D = 1024
LW = 256
ROWS = 64
HEADS_LOC = 4
MESH = pl.DeviceIdType.MESH
F32 = jnp.float32
BF16 = jnp.bfloat16


def dot(a, b):
    return lax.dot_general(a, b, (((1,), (0,)), ((), ())), preferred_element_type=F32)


def dot_bt(a, b):
    return lax.dot_general(a, b, (((1,), (1,)), ((), ())), preferred_element_type=F32)


def dot_at(a, b):
    return lax.dot_general(a, b, (((0,), (0,)), ((), ())), preferred_element_type=F32)


def head_mask(h):
    lane = lax.broadcasted_iota(jnp.int32, (1, LW), 1)
    return jnp.where(lane // HD == h, 1.0, 0.0).astype(BF16)


def softmax(scores):
    expo = jnp.exp(scores - jnp.max(scores, -1, keepdims=True))
    return expo / jnp.sum(expo, -1, keepdims=True)


def score_grads(probs, d_probs):
    delta = jnp.sum(probs * d_probs, -1, keepdims=True)
    return (probs * (d_probs - delta) * HD ** (-0.5)).astype(BF16)


def norm_back(values_in, inv_rms, upstream):
    mean = jnp.mean(upstream * values_in, -1, keepdims=True)
    return inv_rms * (upstream - values_in * (inv_rms * inv_rms) * mean)


def kernel(
    x_hbm, g_hbm, cf_hbm, ws_hbm, wos_hbm, wt_hbm, wot_hbm,
    tok_ref, gs_ref, gso_ref, gt_ref, gto_ref,
    x_ref, g_ref, cf_row, ws, wos, wt, wot, xall, gall, nhall, dhall,
    bias, qkvs, probs, attns, hid, dhid,
    rsend, rrecv, tsend, tbuf, tres, dqkv, dqs,
    gbuf, grecv1, gsum1, grecv2, gsum2, grecv3,
    w_sem, mp_send, mp_recv, t_send, t_recv, h_send, h_recv, b_send, b_recv,
    c_send, c_recv, x_send, x_recv, z_send, z_recv,
):
    f = lax.axis_index("frames")
    m = lax.axis_index("mp")
    core = lax.rem(f, 2)
    xpos = lax.rem(f // 2, XS)
    zpos = f // PL
    w = lax.rem(f, PL)

    def remote(src, dst, ssem, rsem, to_f, to_m):
        return pltpu.make_async_remote_copy(
            src_ref=src, dst_ref=dst, send_sem=ssem, recv_sem=rsem,
            device_id=(to_f, to_m), device_id_type=MESH,
        )

    pending = []

    loads = [
        pltpu.make_async_copy(hbm, vmem, w_sem.at[i])
        for i, (hbm, vmem) in enumerate(
            (
                (x_hbm, x_ref), (g_hbm, g_ref), (cf_hbm, cf_row),
                (ws_hbm, ws), (wos_hbm, wos), (wot_hbm, wot), (wt_hbm, wt),
            )
        )
    ]
    for load in loads:
        load.start()

    barrier = pltpu.get_barrier_semaphore()

    for k in range(1, MP):
        pl.semaphore_signal(
            barrier, inc=1, device_id=(f, lax.rem(m + k, MP)), device_id_type=MESH
        )
    for k in range(1, PL):
        pl.semaphore_signal(
            barrier, inc=1, device_id=(zpos * PL + lax.rem(w + k, PL), m), device_id_type=MESH
        )
    for k in range(1, ZS):
        pl.semaphore_signal(
            barrier, inc=1, device_id=(lax.rem(zpos + k, ZS) * PL + w, m), device_id_type=MESH
        )

    def gather_mp(phase, src, buf):
        copies = []
        for k in (1, 3, 2):
            copy = remote(
                src, buf.at[m], mp_send.at[phase, k - 1], mp_recv.at[phase, k - 1],
                f, lax.rem(m + k, MP),
            )
            copy.start()
            copies.append(copy)
        pending.extend(copies)
        return copies

    def scatter_mp(phase, which):
        copies = []
        for k in (1, 3, 2):
            to = lax.rem(m + k, MP)
            copy = remote(
                rsend.at[which, to], rrecv.at[which, k - 1],
                mp_send.at[phase, k - 1], mp_recv.at[phase, k - 1], f, to,
            )
            copy.start()
            copies.append(copy)
        pending.extend(copies)
        return copies

    loads[0].wait()
    x = x_ref[...].astype(F32)
    inv_x = lax.rsqrt(jnp.mean(x * x, -1, keepdims=True) + EPS)
    xall[m] = (x * inv_x).astype(BF16)
    pl.semaphore_wait(barrier, MP - 1 + PL - 1 + ZS - 1)

    ag_x = gather_mp(0, xall.at[m], xall)

    loads[1].wait()
    loads[2].wait()
    gall[m] = g_ref[...]
    row = lax.broadcasted_iota(jnp.int32, (LW, LW), 0)
    col = lax.broadcasted_iota(jnp.int32, (LW, LW), 1)
    clips = cf_row.shape[1]
    c_row = lax.broadcasted_iota(jnp.int32, (clips, clips), 0)
    c_col = lax.broadcasted_iota(jnp.int32, (clips, clips), 1)
    ends_col = jnp.sum(jnp.where(c_col <= c_row, cf_row[...], 0), axis=1, keepdims=True)
    ends_row = jnp.sum(jnp.where(c_row == c_col, ends_col, 0), axis=0, keepdims=True)

    def clip_of(slot, ends, axis):
        frame = lax.rem(zpos * PL + FR - HALO + slot, FR)
        count = jnp.sum(jnp.where(frame >= ends, 1, 0), axis=axis, keepdims=True)
        return count

    slot_lane = lax.broadcasted_iota(jnp.int32, (clips, LW), 1) // 16
    slot_sub = lax.broadcasted_iota(jnp.int32, (LW, clips), 0) // 16
    id_lane = clip_of(slot_lane, ends_col, 0)
    id_sub = clip_of(slot_sub, ends_row, 1)
    used = PL + 2 * HALO
    id_lane = jnp.where(col[:1] // 16 < used, id_lane, -1)
    id_sub = jnp.where(row[:, :1] // 16 < used, id_sub, -1)
    same = jnp.logical_and(id_lane == id_sub, row % 16 == col % 16)
    bias[...] = jnp.where(same, 0.0, NEGATIVE)
    for t in range(4):
        for g in range(2):
            tbuf[t, g, used:] = jnp.zeros((16 - used, 16, LW), BF16)

    masks = [head_mask(h) for h in range(HEADS_LOC)]

    loads[3].wait()
    for copy in ag_x:
        copy.wait_recv()
    ag_g = gather_mp(1, g_ref, gall)
    x_all = xall[...].reshape(LW, D)
    for j in range(3):
        qkvs[j] = dot(x_all, ws[j]).astype(BF16)

    total = jnp.zeros((LW, LW), F32)
    for h in range(HEADS_LOC):
        p = softmax(dot_bt(qkvs[0] * masks[h], qkvs[1]) * HD ** (-0.5))
        probs[h] = p
        total = total + dot(p.astype(BF16), qkvs[2] * masks[h])
    attn = total.astype(BF16)
    attns[...] = attn.reshape(MP, ROWS, LW)

    loads[4].wait()
    for c in range(4):
        cols = pl.ds(c * 256, 256)
        rsend[0, :, :, cols] = dot(attn, wos[:, cols]).astype(BF16).reshape(MP, ROWS, 256)
    rs1 = scatter_mp(2, 0)
    own = dot(attns[m], wos[...])

    loads[5].wait()
    for copy in ag_g:
        copy.wait_recv()
    tsend[3] = dot_bt(gall[...].reshape(LW, D), wot[...]).astype(BF16).reshape(2, PL, 16, LW)

    for copy in rs1:
        copy.wait_recv()
    hidden = x_ref[...].astype(F32) + own
    for k in range(3):
        hidden = hidden + rrecv[0, k].astype(F32)
    inv_h = lax.rsqrt(jnp.mean(hidden * hidden, -1, keepdims=True) + EPS)
    hid[...] = hidden
    nhall[m] = (hidden * inv_h).astype(BF16)
    ag_h = gather_mp(3, nhall.at[m], nhall)

    loads[6].wait()
    for copy in ag_h:
        copy.wait_recv()
    h_all = nhall[...].reshape(LW, D)
    for j in range(3):
        tsend[j] = dot(h_all, wt[j]).astype(BF16).reshape(2, PL, 16, LW)

    there = []
    for g in range(2):
        for k in range(1, PL):
            to = lax.rem(w + k, PL)
            copy = remote(
                tsend.at[:, g, to], tbuf.at[:, g, HALO + w],
                t_send.at[g, k - 1], t_recv.at[g, k - 1], zpos * PL + to, m,
            )
            copy.start()
            there.append(copy)
    pending.extend(there)
    for t in range(4):
        for g in range(2):
            tbuf[t, g, HALO + w] = tsend[t, g, w]

    def hand_on(g, frame):
        def to_plane(step, slot):
            return remote(
                tbuf.at[:, g, HALO + frame], tbuf.at[:, g, slot],
                h_send.at[g], h_recv.at[g], lax.rem(zpos + step, ZS) * PL + w, m,
            )

        @pl.when(frame < HALO)
        def _():
            to_plane(ZS - 1, HALO + PL + frame).start()

        @pl.when(frame >= PL - HALO)
        def _():
            to_plane(1, frame - (PL - HALO)).start()

    def hand_wait(g):
        some = pl.ds(0, 2 * HALO)
        return remote(
            tbuf.at[:, g, some], tbuf.at[:, g, some], h_send.at[g], h_recv.at[g], f, m
        )

    for g in range(2):
        hand_on(g, w)
        for k in range(1, PL):
            there[g * (PL - 1) + k - 1].wait_recv()
            hand_on(g, lax.rem(w + PL - k, PL))

    zero = jnp.zeros((LW, LW), F32)
    back = []
    for g in range(2):
        hand_wait(g).wait_recv()
        queries, keys, values, upstream = [tbuf[t, g].reshape(LW, LW) for t in range(4)]
        attn_t, d_q, d_k, d_v = zero, zero, zero, zero
        for h in range(HEADS_LOC):
            qm = queries * masks[h]
            om = upstream * masks[h]
            p = softmax(dot_bt(qm, keys) * HD ** (-0.5) + bias[...])
            pb = p.astype(BF16)
            attn_t = attn_t + dot(pb, values * masks[h])
            d_v = d_v + dot_at(pb, om)
            ds = score_grads(p, dot_bt(om, values))
            d_q = d_q + dot(ds, keys * masks[h])
            d_k = d_k + dot_at(ds, qm)
        for t, full in enumerate((d_q, d_k, d_v, attn_t)):
            mine = full[16 * HALO : 16 * (HALO + PL)]
            tres[t, g] = mine.astype(BF16).reshape(PL, 16, LW)
        for k in range(1, PL):
            to = lax.rem(w + k, PL)
            copy = remote(
                tres.at[:, g, to], dqkv.at[:, g, w],
                b_send.at[g, k - 1], b_recv.at[g, k - 1], zpos * PL + to, m,
            )
            copy.start()
            back.append(copy)
        for t in range(4):
            dqkv[t, g, w] = tres[t, g, w]
    pending.extend(back)
    for copy in back:
        copy.wait_recv()

    def project_back(which, grads, weights):
        for c in range(4):
            cols = pl.ds(c * 256, 256)
            part = dot_bt(grads[0], weights[0, cols])
            part = part + dot_bt(grads[1], weights[1, cols])
            part = part + dot_bt(grads[2], weights[2, cols])
            rsend[which, :, :, cols] = part.astype(BF16).reshape(MP, ROWS, 256)

    def own_back(grads, weights):
        part = dot_bt(grads[0], weights[0])
        part = part + dot_bt(grads[1], weights[1])
        return part + dot_bt(grads[2], weights[2])

    def weight_grad(j, left_ref, right):
        for c in range(4):
            left = left_ref[:, :, c * 256 : (c + 1) * 256].reshape(LW, 256)
            gbuf[j, 8 * c : 8 * c + 8] = dot_at(left, right).astype(BF16).reshape(8, 2, 16, LW)

    first = [0, 4, 5, 6, 7]
    count = [4, 1, 1, 1, 1]

    def core_send(b):
        some = slice(first[b], first[b] + count[b])
        copy = remote(
            gbuf.at[some, :, 1 - core], grecv1.at[some],
            c_send.at[b], c_recv.at[b], f + 1 - 2 * core, m,
        )
        copy.start()
        pending.append(copy)
        return copy

    def core_sum_x_send(b, copy):
        copy.wait_recv()
        some = slice(first[b], first[b] + count[b])
        for j in range(some.start, some.stop):
            summed = gbuf[j, :, core].astype(F32) + grecv1[j].astype(F32)
            gsum1[j] = summed.astype(BF16).reshape(ZS, XS, 16, LW)
        copies = []
        for k in (1, 3, 2):
            to = lax.rem(xpos + k, XS)
            copy = remote(
                gsum1.at[some, :, to], grecv2.at[k - 1, some],
                x_send.at[b, k - 1], x_recv.at[b, k - 1],
                (zpos * XS + to) * 2 + core, m,
            )
            copy.start()
            copies.append(copy)
        pending.extend(copies)
        return copies

    def x_sum_z_send(b, copies):
        for copy in copies:
            copy.wait_recv()
        some = slice(first[b], first[b] + count[b])
        for j in range(some.start, some.stop):
            summed = gsum1[j, :, xpos].astype(F32)
            for k in range(3):
                summed = summed + grecv2[k, j].astype(F32)
            gsum2[j] = summed.astype(BF16)
        copies = []
        for k in (4, 3, 5, 2, 6, 1, 7):
            to = lax.rem(zpos + k, ZS)
            copy = remote(
                gsum2.at[some, to], grecv3.at[k - 1, some],
                z_send.at[b, k - 1], z_recv.at[b, k - 1],
                (to * XS + xpos) * 2 + core, m,
            )
            copy.start()
            copies.append(copy)
        pending.extend(copies)
        return copies

    def z_sum(b, copies, outs):
        for copy in copies:
            copy.wait_recv()
        for at, out in enumerate(outs):
            j = first[b] + at
            summed = gsum2[j, zpos].astype(F32)
            for k in range(ZS - 1):
                summed = summed + grecv3[k, j].astype(F32)
            out[...] = summed

    grads_t = [dqkv[j].reshape(LW, LW) for j in range(4)]
    project_back(1, grads_t[:3], wt)
    rs2 = scatter_mp(4, 1)
    for j in range(3):
        weight_grad(j, nhall, grads_t[j])
    weight_grad(3, gall, grads_t[3])
    core_t = core_send(0)
    half = pl.ds(4 * lax.rem(m, 2), 4)
    d_nh = own_back([dqkv[j, m // 2, half].reshape(ROWS, LW) for j in range(3)], wt)
    for copy in rs2:
        copy.wait_recv()
    for k in range(3):
        d_nh = d_nh + rrecv[1, k].astype(F32)
    hidden = hid[...]
    inv_h = lax.rsqrt(jnp.mean(hidden * hidden, -1, keepdims=True) + EPS)
    d_hidden = g_ref[...].astype(F32) + norm_back(hidden, inv_h, d_nh)
    dhid[...] = d_hidden
    dhall[m] = d_hidden.astype(BF16)
    ag_d = gather_mp(5, dhall.at[m], dhall)
    x_t = core_sum_x_send(0, core_t)
    for copy in ag_d:
        copy.wait_recv()

    weight_grad(7, dhall, attns[...].reshape(LW, LW))
    core_o = core_send(4)
    das = dot_bt(dhall[...].reshape(LW, D), wos[...]).astype(BF16)

    def keep(j, grad):
        dqs[j] = grad.astype(BF16).reshape(MP, ROWS, LW)
        weight_grad(4 + j, xall, dqs[j].reshape(LW, LW))
        return core_send(1 + j)

    d_v = zero
    for h in range(HEADS_LOC):
        d_v = d_v + dot_at(probs[h].astype(BF16), das * masks[h])
    core_v = keep(2, d_v)
    x_o = core_sum_x_send(4, core_o)
    d_q, d_k = zero, zero
    for h in range(HEADS_LOC):
        ds = score_grads(probs[h], dot_bt(das * masks[h], qkvs[2]))
        d_q = d_q + dot(ds, qkvs[1] * masks[h])
        d_k = d_k + dot_at(ds, qkvs[0] * masks[h])
    core_q = keep(0, d_q)
    core_k = keep(1, d_k)
    x_v = core_sum_x_send(3, core_v)
    z_t = x_sum_z_send(0, x_t)
    x_q = core_sum_x_send(1, core_q)
    x_k = core_sum_x_send(2, core_k)
    project_back(2, [dqs[j].reshape(LW, LW) for j in range(3)], ws)
    rs3 = scatter_mp(6, 2)
    z_o = x_sum_z_send(4, x_o)
    z_v = x_sum_z_send(3, x_v)
    z_sum(0, z_t, [gt_ref.at[0], gt_ref.at[1], gt_ref.at[2], gto_ref])
    d_nx = own_back([dqs[j, m] for j in range(3)], ws)
    z_q = x_sum_z_send(1, x_q)
    for copy in rs3:
        copy.wait_recv()
    for k in range(3):
        d_nx = d_nx + rrecv[2, k].astype(F32)
    x = x_ref[...].astype(F32)
    inv_x = lax.rsqrt(jnp.mean(x * x, -1, keepdims=True) + EPS)
    tok_ref[...] = (dhid[...] + norm_back(x, inv_x, d_nx)).astype(BF16)
    z_k = x_sum_z_send(2, x_k)
    z_sum(4, z_o, [gso_ref])
    z_sum(3, z_v, [gs_ref.at[2]])
    z_sum(1, z_q, [gs_ref.at[0]])
    z_sum(2, z_k, [gs_ref.at[1]])
    for copy in pending:
        copy.wait_send()
    for g in range(2):
        hand_wait(g).wait_send()


def deliver(*refs):
    for source, target in zip(refs[:5], refs[5:]):
        target[...] = source[...]


def shards(x, g, ws, wos, wt, wot, clip_frames):
    clips = clip_frames.shape[0]
    vmem = pl.BlockSpec(memory_space=pltpu.VMEM)
    dma = pltpu.SemaphoreType.DMA
    scratch = [
        pltpu.VMEM((ROWS, D), BF16),
        pltpu.VMEM((ROWS, D), BF16),
        pltpu.VMEM((1, clips), jnp.int32),
        pltpu.VMEM((3, D, LW), BF16),
        pltpu.VMEM((LW, D), BF16),
        pltpu.VMEM((3, D, LW), BF16),
        pltpu.VMEM((LW, D), BF16),
        pltpu.VMEM((MP, ROWS, D), BF16),
        pltpu.VMEM((MP, ROWS, D), BF16),
        pltpu.VMEM((MP, ROWS, D), BF16),
        pltpu.VMEM((MP, ROWS, D), BF16),
        pltpu.VMEM((LW, LW), F32),
        pltpu.VMEM((3, LW, LW), BF16),
        pltpu.VMEM((HEADS_LOC, LW, LW), F32),
        pltpu.VMEM((MP, ROWS, LW), BF16),
        pltpu.VMEM((ROWS, D), F32),
        pltpu.VMEM((ROWS, D), F32),
        pltpu.VMEM((3, MP, ROWS, D), BF16),
        pltpu.VMEM((3, MP - 1, ROWS, D), BF16),
        pltpu.VMEM((4, 2, PL, 16, LW), BF16),
        pltpu.VMEM((4, 2, 16, 16, LW), BF16),
        pltpu.VMEM((4, 2, PL, 16, LW), BF16),
        pltpu.VMEM((4, 2, PL, 16, LW), BF16),
        pltpu.VMEM((3, MP, ROWS, LW), BF16),
        pltpu.VMEM((8, FR // 2, 2, 16, LW), BF16),
        pltpu.VMEM((8, FR // 2, 16, LW), BF16),
        pltpu.VMEM((8, ZS, XS, 16, LW), BF16),
        pltpu.VMEM((XS - 1, 8, ZS, 16, LW), BF16),
        pltpu.VMEM((8, ZS, 16, LW), BF16),
        pltpu.VMEM((ZS - 1, 8, 16, LW), BF16),
        dma((7,)),
        dma((7, 3)),
        dma((7, 3)),
        dma((2, PL - 1)),
        dma((2, PL - 1)),
        dma((2,)),
        dma((2,)),
        dma((2, PL - 1)),
        dma((2, PL - 1)),
        dma((5,)),
        dma((5,)),
        dma((5, XS - 1)),
        dma((5, XS - 1)),
        dma((5, ZS - 1)),
        dma((5, ZS - 1)),
    ]
    tokens, gs, gso, gt, gto = pl.pallas_call(
        kernel,
        out_shape=(
            jax.ShapeDtypeStruct((ROWS, D), BF16),
            jax.ShapeDtypeStruct((3, 16, LW), F32),
            jax.ShapeDtypeStruct((16, LW), F32),
            jax.ShapeDtypeStruct((3, 16, LW), F32),
            jax.ShapeDtypeStruct((16, LW), F32),
        ),
        in_specs=[pl.BlockSpec(memory_space=pltpu.HBM)] * 7,
        out_specs=[vmem] * 5,
        scratch_shapes=scratch,
        compiler_params=pltpu.CompilerParams(
            collective_id=0, has_side_effects=True, vmem_limit_bytes=60 * 1024 * 1024
        ),
        cost_estimate=pl.CostEstimate(
            flops=3_500_000_000, bytes_accessed=6_000_000, transcendentals=1_000_000
        ),
    )(
        x.reshape(ROWS, D), g.reshape(ROWS, D), clip_frames.reshape(1, clips), ws, wos, wt, wot,
    )
    results = (tokens, gs, gso, gt, gto)
    tokens, gs, gso, gt, gto = pl.pallas_call(
        deliver,
        out_shape=tuple(jax.ShapeDtypeStruct(r.shape, r.dtype) for r in results),
        in_specs=[vmem] * 5,
        out_specs=[vmem] * 5,
        compiler_params=pltpu.CompilerParams(vmem_limit_bytes=60 * 1024 * 1024),
    )(*results)
    return tokens.reshape(1, ROWS, D), gs, gso.T, gt, gto.T


def solution(mesh):
    placed = (
        P("frames", "mp", None),
        P("frames", "mp", None),
        P(None, None, "mp"),
        P("mp", None),
        P(None, None, "mp"),
        P("mp", None),
        P(),
    )
    return jax.shard_map(
        shards,
        mesh=mesh,
        in_specs=placed,
        out_specs=(
            P("frames", "mp", None),
            P(None, "frames", "mp"),
            P("mp", "frames"),
            P(None, "frames", "mp"),
            P("mp", "frames"),
        ),
        check_vma=False,
    )
```

```python
import jax
import jax.numpy as jnp
from jax import lax
from jax.experimental import pallas as pl
from jax.experimental.pallas import tpu as pltpu
from jax.sharding import PartitionSpec as P

HD = 64
EPS = 1e-06
NEGATIVE = -1e30
FR = 64
MP = 4
XS = 4
ZS = 8
PL = 8
HALO = 3
D = 1024
LW = 256
ROWS = 64
HEADS_LOC = 4
MESH = pl.DeviceIdType.MESH
F32 = jnp.float32
BF16 = jnp.bfloat16


def dot(a, b):
    return lax.dot_general(a, b, (((1,), (0,)), ((), ())), preferred_element_type=F32)


def dot_bt(a, b):
    return lax.dot_general(a, b, (((1,), (1,)), ((), ())), preferred_element_type=F32)


def dot_at(a, b):
    return lax.dot_general(a, b, (((0,), (0,)), ((), ())), preferred_element_type=F32)


def head_mask(h):
    lane = lax.broadcasted_iota(jnp.int32, (1, LW), 1)
    return jnp.where(lane // HD == h, 1.0, 0.0).astype(BF16)


def softmax(scores):
    expo = jnp.exp(scores - jnp.max(scores, -1, keepdims=True))
    return expo / jnp.sum(expo, -1, keepdims=True)


def score_grads(probs, d_probs):
    delta = jnp.sum(probs * d_probs, -1, keepdims=True)
    return (probs * (d_probs - delta) * HD ** (-0.5)).astype(BF16)


def norm_back(values_in, inv_rms, upstream):
    mean = jnp.mean(upstream * values_in, -1, keepdims=True)
    return inv_rms * (upstream - values_in * (inv_rms * inv_rms) * mean)


def kernel(
    x_hbm, g_hbm, cf_hbm, ws_hbm, wos_hbm, wt_hbm, wot_hbm,
    tok_ref, gs_ref, gso_ref, gt_ref, gto_ref,
    x_ref, g_ref, cf_row, ws, wos, wt, wot, xall, gall, nhall, dhall,
    bias, qkvs, probs, attns, hid, dhid,
    rsend, rrecv, tsend, tbuf, tres, dqkv, dqs,
    gbuf, grecv1, gsum1, grecv2, gsum2, grecv3,
    w_sem, mp_send, mp_recv, t_send, t_recv, h_send, h_recv, b_send, b_recv,
    c_send, c_recv, x_send, x_recv, z_send, z_recv,
):
    f = lax.axis_index("frames")
    m = lax.axis_index("mp")
    core = lax.rem(f, 2)
    xpos = lax.rem(f // 2, XS)
    zpos = f // PL
    w = lax.rem(f, PL)

    def remote(src, dst, ssem, rsem, to_f, to_m):
        return pltpu.make_async_remote_copy(
            src_ref=src, dst_ref=dst, send_sem=ssem, recv_sem=rsem,
            device_id=(to_f, to_m), device_id_type=MESH,
        )

    pending = []

    loads = [
        pltpu.make_async_copy(hbm, vmem, w_sem.at[i])
        for i, (hbm, vmem) in enumerate(
            (
                (x_hbm, x_ref), (g_hbm, g_ref), (cf_hbm, cf_row),
                (ws_hbm, ws), (wos_hbm, wos), (wot_hbm, wot), (wt_hbm, wt),
            )
        )
    ]
    for load in loads:
        load.start()

    barrier = pltpu.get_barrier_semaphore()

    for k in range(1, MP):
        pl.semaphore_signal(
            barrier, inc=1, device_id=(f, lax.rem(m + k, MP)), device_id_type=MESH
        )
    for k in range(1, PL):
        pl.semaphore_signal(
            barrier, inc=1, device_id=(zpos * PL + lax.rem(w + k, PL), m), device_id_type=MESH
        )
    for k in range(1, ZS):
        pl.semaphore_signal(
            barrier, inc=1, device_id=(lax.rem(zpos + k, ZS) * PL + w, m), device_id_type=MESH
        )

    def gather_mp(phase, src, buf, rows=slice(0, ROWS)):
        copies = []
        for k in (1, 3, 2):
            copy = remote(
                src.at[rows], buf.at[m, rows], mp_send.at[phase, k - 1], mp_recv.at[phase, k - 1],
                f, lax.rem(m + k, MP),
            )
            copy.start()
            copies.append(copy)
        pending.extend(copies)
        return copies

    def scatter_mp(phase, which):
        copies = []
        for k in (1, 3, 2):
            to = lax.rem(m + k, MP)
            copy = remote(
                rsend.at[which, to], rrecv.at[which, k - 1],
                mp_send.at[phase, k - 1], mp_recv.at[phase, k - 1], f, to,
            )
            copy.start()
            copies.append(copy)
        pending.extend(copies)
        return copies

    loads[0].wait()
    x = x_ref[...].astype(F32)
    inv_x = lax.rsqrt(jnp.mean(x * x, -1, keepdims=True) + EPS)
    xall[m] = (x * inv_x).astype(BF16)
    pl.semaphore_wait(barrier, MP - 1 + PL - 1 + ZS - 1)

    ag_x = gather_mp(0, xall.at[m], xall)

    loads[1].wait()
    loads[2].wait()
    gall[m] = g_ref[...]
    row = lax.broadcasted_iota(jnp.int32, (LW, LW), 0)
    col = lax.broadcasted_iota(jnp.int32, (LW, LW), 1)
    clips = cf_row.shape[1]
    c_row = lax.broadcasted_iota(jnp.int32, (clips, clips), 0)
    c_col = lax.broadcasted_iota(jnp.int32, (clips, clips), 1)
    ends_col = jnp.sum(jnp.where(c_col <= c_row, cf_row[...], 0), axis=1, keepdims=True)
    ends_row = jnp.sum(jnp.where(c_row == c_col, ends_col, 0), axis=0, keepdims=True)

    def clip_of(slot, ends, axis):
        frame = lax.rem(zpos * PL + FR - HALO + slot, FR)
        count = jnp.sum(jnp.where(frame >= ends, 1, 0), axis=axis, keepdims=True)
        return count

    slot_lane = lax.broadcasted_iota(jnp.int32, (clips, LW), 1) // 16
    slot_sub = lax.broadcasted_iota(jnp.int32, (LW, clips), 0) // 16
    id_lane = clip_of(slot_lane, ends_col, 0)
    id_sub = clip_of(slot_sub, ends_row, 1)
    used = PL + 2 * HALO
    id_lane = jnp.where(col[:1] // 16 < used, id_lane, -1)
    id_sub = jnp.where(row[:, :1] // 16 < used, id_sub, -1)
    same = jnp.logical_and(id_lane == id_sub, row % 16 == col % 16)
    bias[...] = jnp.where(same, 0.0, NEGATIVE)
    for t in range(4):
        for g in range(2):
            tbuf[t, g, used:] = jnp.zeros((16 - used, 16, LW), BF16)

    masks = [head_mask(h) for h in range(HEADS_LOC)]

    loads[3].wait()
    for copy in ag_x:
        copy.wait_recv()
    ag_g = gather_mp(1, g_ref, gall, slice(0, ROWS // 2))
    x_all = xall[...].reshape(LW, D)
    for j in range(3):
        qkvs[j] = dot(x_all, ws[j]).astype(BF16)

    total = jnp.zeros((LW, LW), F32)
    for h in range(HEADS_LOC):
        p = softmax(dot_bt(qkvs[0] * masks[h], qkvs[1]) * HD ** (-0.5))
        probs[h] = p
        total = total + dot(p.astype(BF16), qkvs[2] * masks[h])
    attn = total.astype(BF16)
    attns[...] = attn.reshape(MP, ROWS, LW)

    loads[4].wait()
    for c in range(4):
        cols = pl.ds(c * 256, 256)
        rsend[0, :, :, cols] = dot(attn, wos[:, cols]).astype(BF16).reshape(MP, ROWS, 256)
    rs1 = scatter_mp(2, 0)
    ag_g = ag_g + gather_mp(7, g_ref, gall, slice(ROWS // 2, ROWS))
    own = dot(attns[m], wos[...])

    for copy in rs1:
        copy.wait_recv()
    hidden = x_ref[...].astype(F32) + own
    for k in range(3):
        hidden = hidden + rrecv[0, k].astype(F32)
    inv_h = lax.rsqrt(jnp.mean(hidden * hidden, -1, keepdims=True) + EPS)
    hid[...] = hidden
    nhall[m] = (hidden * inv_h).astype(BF16)
    ag_h = gather_mp(3, nhall.at[m], nhall)

    def plane_send(part, source, target, ssems, rsems):
        copies = []
        for k in range(1, PL):
            to = lax.rem(w + k, PL)
            copy = remote(
                source(to), target, ssems.at[part, k - 1], rsems.at[part, k - 1],
                zpos * PL + to, m,
            )
            copy.start()
            copies.append(copy)
        pending.extend(copies)
        return copies

    def halo_view(part, slots):
        return tbuf.at[3, :, slots] if part == 2 else tbuf.at[:3, part, slots]

    def hand_on(part, frame):
        def to_plane(step, slot):
            return remote(
                halo_view(part, HALO + frame), halo_view(part, slot),
                h_send.at[part], h_recv.at[part], lax.rem(zpos + step, ZS) * PL + w, m,
            )

        @pl.when(frame < HALO)
        def _():
            to_plane(ZS - 1, HALO + PL + frame).start()

        @pl.when(frame >= PL - HALO)
        def _():
            to_plane(1, frame - (PL - HALO)).start()

    def hand_wait(part):
        some = halo_view(part, pl.ds(0, 2 * HALO))
        return remote(some, some, h_send.at[part], h_recv.at[part], f, m)

    def receive(part, copies):
        hand_on(part, w)
        for k in range(1, PL):
            copies[k - 1].wait_recv()
            hand_on(part, lax.rem(w + PL - k, PL))

    loads[5].wait()
    for copy in ag_g:
        copy.wait_recv()
    tsend[3] = dot_bt(gall[...].reshape(LW, D), wot[...]).astype(BF16).reshape(2, PL, 16, LW)
    there_up = plane_send(
        2, lambda to: tsend.at[3, :, to], halo_view(2, HALO + w), t_send, t_recv
    )
    for g in range(2):
        tbuf[3, g, HALO + w] = tsend[3, g, w]
    receive(2, there_up)
    loads[6].wait()
    for copy in ag_h:
        copy.wait_recv()
    h_all = nhall[...].reshape(LW, D)
    for j in range(3):
        tsend[j] = dot(h_all, wt[j]).astype(BF16).reshape(2, PL, 16, LW)

    there = [
        plane_send(g, lambda to, g=g: tsend.at[:3, g, to], halo_view(g, HALO + w), t_send, t_recv)
        for g in range(2)
    ]
    for t in range(3):
        for g in range(2):
            tbuf[t, g, HALO + w] = tsend[t, g, w]

    for g in range(2):
        receive(g, there[g])

    zero = jnp.zeros((LW, LW), F32)
    own_slots = slice(HALO, HALO + PL)
    back = []
    for g in range(2):
        hand_wait(g).wait_recv()
        if g == 0:
            hand_wait(2).wait_recv()
        queries, keys, values, upstream = [tbuf[t, g].reshape(LW, LW) for t in range(4)]
        attn_t, d_q, d_k, d_v = zero, zero, zero, zero
        for h in range(HEADS_LOC):
            qm = queries * masks[h]
            om = upstream * masks[h]
            p = softmax(dot_bt(qm, keys) * HD ** (-0.5) + bias[...])
            pb = p.astype(BF16)
            attn_t = attn_t + dot(pb, values * masks[h])
            d_v = d_v + dot_at(pb, om)
            ds = score_grads(p, dot_bt(om, values))
            d_q = d_q + dot(ds, keys * masks[h])
            d_k = d_k + dot_at(ds, qm)
        for t, full in enumerate((d_q, d_k, d_v, attn_t)):
            tres[t, g] = full.astype(BF16).reshape(16, 16, LW)[own_slots]
        back += plane_send(
            g, lambda to, g=g: tres.at[:3, g, to], dqkv.at[:3, g, w], b_send, b_recv
        )
        for t in range(4):
            dqkv[t, g, w] = tres[t, g, w]
    back_attn = plane_send(2, lambda to: tres.at[3, :, to], dqkv.at[3, :, w], b_send, b_recv)
    for copy in back:
        copy.wait_recv()

    def project_back(which, grads, weights):
        for c in range(4):
            cols = pl.ds(c * 256, 256)
            part = dot_bt(grads[0], weights[0, cols])
            part = part + dot_bt(grads[1], weights[1, cols])
            part = part + dot_bt(grads[2], weights[2, cols])
            rsend[which, :, :, cols] = part.astype(BF16).reshape(MP, ROWS, 256)

    def own_back(grads, weights):
        part = dot_bt(grads[0], weights[0])
        part = part + dot_bt(grads[1], weights[1])
        return part + dot_bt(grads[2], weights[2])

    def weight_grad(j, left_ref, right):
        for c in range(4):
            left = left_ref[:, :, c * 256 : (c + 1) * 256].reshape(LW, 256)
            gbuf[j, 8 * c : 8 * c + 8] = dot_at(left, right).astype(BF16).reshape(8, 2, 16, LW)

    first = [0, 4, 5, 6, 7]
    count = [4, 1, 1, 1, 1]

    def core_send(b):
        some = slice(first[b], first[b] + count[b])
        copy = remote(
            gbuf.at[some, :, 1 - core], grecv1.at[some],
            c_send.at[b], c_recv.at[b], f + 1 - 2 * core, m,
        )
        copy.start()
        pending.append(copy)
        return copy

    def core_sum_x_send(b, copy):
        copy.wait_recv()
        some = slice(first[b], first[b] + count[b])
        for j in range(some.start, some.stop):
            summed = gbuf[j, :, core].astype(F32) + grecv1[j].astype(F32)
            gsum1[j] = summed.astype(BF16).reshape(ZS, XS, 16, LW)
        copies = []
        for k in (1, 3, 2):
            to = lax.rem(xpos + k, XS)
            copy = remote(
                gsum1.at[some, :, to], grecv2.at[k - 1, some],
                x_send.at[b, k - 1], x_recv.at[b, k - 1],
                (zpos * XS + to) * 2 + core, m,
            )
            copy.start()
            copies.append(copy)
        pending.extend(copies)
        return copies

    def x_sum_z_send(b, copies):
        for copy in copies:
            copy.wait_recv()
        some = slice(first[b], first[b] + count[b])
        for j in range(some.start, some.stop):
            summed = gsum1[j, :, xpos].astype(F32)
            for k in range(3):
                summed = summed + grecv2[k, j].astype(F32)
            gsum2[j] = summed.astype(BF16)
        copies = []
        for k in (4, 3, 5, 2, 6, 1, 7):
            to = lax.rem(zpos + k, ZS)
            copy = remote(
                gsum2.at[some, to], grecv3.at[k - 1, some],
                z_send.at[b, k - 1], z_recv.at[b, k - 1],
                (to * XS + xpos) * 2 + core, m,
            )
            copy.start()
            copies.append(copy)
        pending.extend(copies)
        return copies

    def z_sum(b, copies, outs):
        for copy in copies:
            copy.wait_recv()
        for at, out in enumerate(outs):
            j = first[b] + at
            summed = gsum2[j, zpos].astype(F32)
            for k in range(ZS - 1):
                summed = summed + grecv3[k, j].astype(F32)
            out[...] = summed

    grads_t = [dqkv[j].reshape(LW, LW) for j in range(3)]
    project_back(1, grads_t, wt)
    rs2 = scatter_mp(4, 1)
    for j in range(3):
        weight_grad(j, nhall, grads_t[j])
    for copy in back_attn:
        copy.wait_recv()
    weight_grad(3, gall, dqkv[3].reshape(LW, LW))
    core_t = core_send(0)
    half = pl.ds(4 * lax.rem(m, 2), 4)
    d_nh = own_back([dqkv[j, m // 2, half].reshape(ROWS, LW) for j in range(3)], wt)
    x_t = core_sum_x_send(0, core_t)
    for copy in rs2:
        copy.wait_recv()
    for k in range(3):
        d_nh = d_nh + rrecv[1, k].astype(F32)
    hidden = hid[...]
    inv_h = lax.rsqrt(jnp.mean(hidden * hidden, -1, keepdims=True) + EPS)
    d_hidden = g_ref[...].astype(F32) + norm_back(hidden, inv_h, d_nh)
    dhid[...] = d_hidden
    dhall[m] = d_hidden.astype(BF16)
    ag_d = gather_mp(5, dhall.at[m], dhall)
    for copy in ag_d:
        copy.wait_recv()

    weight_grad(7, dhall, attns[...].reshape(LW, LW))
    core_o = core_send(4)
    das = dot_bt(dhall[...].reshape(LW, D), wos[...]).astype(BF16)

    def keep(j, grad):
        dqs[j] = grad.astype(BF16).reshape(MP, ROWS, LW)
        weight_grad(4 + j, xall, dqs[j].reshape(LW, LW))
        return core_send(1 + j)

    d_v = zero
    for h in range(HEADS_LOC):
        d_v = d_v + dot_at(probs[h].astype(BF16), das * masks[h])
    core_v = keep(2, d_v)
    x_o = core_sum_x_send(4, core_o)
    d_q, d_k = zero, zero
    for h in range(HEADS_LOC):
        ds = score_grads(probs[h], dot_bt(das * masks[h], qkvs[2]))
        d_q = d_q + dot(ds, qkvs[1] * masks[h])
        d_k = d_k + dot_at(ds, qkvs[0] * masks[h])
    core_q = keep(0, d_q)
    core_k = keep(1, d_k)
    x_v = core_sum_x_send(3, core_v)
    z_t = x_sum_z_send(0, x_t)
    x_q = core_sum_x_send(1, core_q)
    x_k = core_sum_x_send(2, core_k)
    project_back(2, [dqs[j].reshape(LW, LW) for j in range(3)], ws)
    rs3 = scatter_mp(6, 2)
    z_o = x_sum_z_send(4, x_o)
    z_v = x_sum_z_send(3, x_v)
    z_sum(0, z_t, [gt_ref.at[0], gt_ref.at[1], gt_ref.at[2], gto_ref])
    d_nx = own_back([dqs[j, m] for j in range(3)], ws)
    z_q = x_sum_z_send(1, x_q)
    for copy in rs3:
        copy.wait_recv()
    for k in range(3):
        d_nx = d_nx + rrecv[2, k].astype(F32)
    x = x_ref[...].astype(F32)
    inv_x = lax.rsqrt(jnp.mean(x * x, -1, keepdims=True) + EPS)
    tok_ref[...] = (dhid[...] + norm_back(x, inv_x, d_nx)).astype(BF16)
    z_k = x_sum_z_send(2, x_k)
    z_sum(4, z_o, [gso_ref])
    z_sum(3, z_v, [gs_ref.at[2]])
    z_sum(1, z_q, [gs_ref.at[0]])
    z_sum(2, z_k, [gs_ref.at[1]])
    for copy in pending:
        copy.wait_send()
    for part in range(3):
        hand_wait(part).wait_send()


def deliver(*refs):
    for source, target in zip(refs[:5], refs[5:]):
        target[...] = source[...]


def shards(x, g, ws, wos, wt, wot, clip_frames):
    clips = clip_frames.shape[0]
    vmem = pl.BlockSpec(memory_space=pltpu.VMEM)
    dma = pltpu.SemaphoreType.DMA
    scratch = [
        pltpu.VMEM((ROWS, D), BF16),
        pltpu.VMEM((ROWS, D), BF16),
        pltpu.VMEM((1, clips), jnp.int32),
        pltpu.VMEM((3, D, LW), BF16),
        pltpu.VMEM((LW, D), BF16),
        pltpu.VMEM((3, D, LW), BF16),
        pltpu.VMEM((LW, D), BF16),
        pltpu.VMEM((MP, ROWS, D), BF16),
        pltpu.VMEM((MP, ROWS, D), BF16),
        pltpu.VMEM((MP, ROWS, D), BF16),
        pltpu.VMEM((MP, ROWS, D), BF16),
        pltpu.VMEM((LW, LW), F32),
        pltpu.VMEM((3, LW, LW), BF16),
        pltpu.VMEM((HEADS_LOC, LW, LW), F32),
        pltpu.VMEM((MP, ROWS, LW), BF16),
        pltpu.VMEM((ROWS, D), F32),
        pltpu.VMEM((ROWS, D), F32),
        pltpu.VMEM((3, MP, ROWS, D), BF16),
        pltpu.VMEM((3, MP - 1, ROWS, D), BF16),
        pltpu.VMEM((4, 2, PL, 16, LW), BF16),
        pltpu.VMEM((4, 2, 16, 16, LW), BF16),
        pltpu.VMEM((4, 2, PL, 16, LW), BF16),
        pltpu.VMEM((4, 2, PL, 16, LW), BF16),
        pltpu.VMEM((3, MP, ROWS, LW), BF16),
        pltpu.VMEM((8, FR // 2, 2, 16, LW), BF16),
        pltpu.VMEM((8, FR // 2, 16, LW), BF16),
        pltpu.VMEM((8, ZS, XS, 16, LW), BF16),
        pltpu.VMEM((XS - 1, 8, ZS, 16, LW), BF16),
        pltpu.VMEM((8, ZS, 16, LW), BF16),
        pltpu.VMEM((ZS - 1, 8, 16, LW), BF16),
        dma((7,)),
        dma((8, 3)),
        dma((8, 3)),
        dma((3, PL - 1)),
        dma((3, PL - 1)),
        dma((3,)),
        dma((3,)),
        dma((3, PL - 1)),
        dma((3, PL - 1)),
        dma((5,)),
        dma((5,)),
        dma((5, XS - 1)),
        dma((5, XS - 1)),
        dma((5, ZS - 1)),
        dma((5, ZS - 1)),
    ]
    tokens, gs, gso, gt, gto = pl.pallas_call(
        kernel,
        out_shape=(
            jax.ShapeDtypeStruct((ROWS, D), BF16),
            jax.ShapeDtypeStruct((3, 16, LW), F32),
            jax.ShapeDtypeStruct((16, LW), F32),
            jax.ShapeDtypeStruct((3, 16, LW), F32),
            jax.ShapeDtypeStruct((16, LW), F32),
        ),
        in_specs=[pl.BlockSpec(memory_space=pltpu.HBM)] * 7,
        out_specs=[vmem] * 5,
        scratch_shapes=scratch,
        compiler_params=pltpu.CompilerParams(
            collective_id=0, has_side_effects=True, vmem_limit_bytes=60 * 1024 * 1024
        ),
        cost_estimate=pl.CostEstimate(
            flops=3_500_000_000, bytes_accessed=6_000_000, transcendentals=1_000_000
        ),
    )(
        x.reshape(ROWS, D), g.reshape(ROWS, D), clip_frames.reshape(1, clips), ws, wos, wt, wot,
    )
    results = (tokens, gs, gso, gt, gto)
    tokens, gs, gso, gt, gto = pl.pallas_call(
        deliver,
        out_shape=tuple(jax.ShapeDtypeStruct(r.shape, r.dtype) for r in results),
        in_specs=[vmem] * 5,
        out_specs=[vmem] * 5,
        compiler_params=pltpu.CompilerParams(vmem_limit_bytes=60 * 1024 * 1024),
    )(*results)
    return tokens.reshape(1, ROWS, D), gs, gso.T, gt, gto.T


def solution(mesh):
    placed = (
        P("frames", "mp", None),
        P("frames", "mp", None),
        P(None, None, "mp"),
        P("mp", None),
        P(None, None, "mp"),
        P("mp", None),
        P(),
    )
    return jax.shard_map(
        shards,
        mesh=mesh,
        in_specs=placed,
        out_specs=(
            P("frames", "mp", None),
            P(None, "frames", "mp"),
            P("mp", "frames"),
            P(None, "frames", "mp"),
            P("mp", "frames"),
        ),
        check_vma=False,
    )
```

```python
import jax
import jax.numpy as jnp
from jax import lax
from jax.experimental import pallas as pl
from jax.experimental.pallas import tpu as pltpu
from jax.sharding import PartitionSpec as P

HD = 64
EPS = 1e-06
NEGATIVE = -1e30
FR = 64
MP = 4
XS = 4
ZS = 8
PL = 8
HALO = 3
D = 1024
LW = 256
ROWS = 64
HEADS_LOC = 4
MESH = pl.DeviceIdType.MESH
F32 = jnp.float32
BF16 = jnp.bfloat16


def dot(a, b):
    return lax.dot_general(a, b, (((1,), (0,)), ((), ())), preferred_element_type=F32)


def dot_bt(a, b):
    return lax.dot_general(a, b, (((1,), (1,)), ((), ())), preferred_element_type=F32)


def dot_at(a, b):
    return lax.dot_general(a, b, (((0,), (0,)), ((), ())), preferred_element_type=F32)


def head_mask(h):
    lane = lax.broadcasted_iota(jnp.int32, (1, LW), 1)
    return jnp.where(lane // HD == h, 1.0, 0.0).astype(BF16)


def softmax(scores):
    expo = jnp.exp(scores - jnp.max(scores, -1, keepdims=True))
    return expo / jnp.sum(expo, -1, keepdims=True)


def score_grads(probs, d_probs):
    delta = jnp.sum(probs * d_probs, -1, keepdims=True)
    return (probs * (d_probs - delta) * HD ** (-0.5)).astype(BF16)


def norm_back(values_in, inv_rms, upstream):
    mean = jnp.mean(upstream * values_in, -1, keepdims=True)
    return inv_rms * (upstream - values_in * (inv_rms * inv_rms) * mean)


def kernel(
    x_hbm, g_hbm, cf_hbm, ws_hbm, wos_hbm, wt_hbm, wot_hbm,
    tok_ref, gs_ref, gso_ref, gt_ref, gto_ref,
    x_ref, g_ref, cf_row, ws, wos, wt, wot, xall, gall, nhall, dhall,
    bias, qkvs, probs, attns, hid, dhid,
    rsend, rrecv, tsend, tbuf, tres, dqkv, dqs,
    gbuf, grecv1, gsum1, grecv2, gsum2, grecv3, hrecv2, hsum2, hrecv3,
    w_sem, mp_send, mp_recv, t_send, t_recv, h_send, h_recv, b_send, b_recv,
    c_send, c_recv, x_send, x_recv, z_send, z_recv,
):
    f = lax.axis_index("frames")
    m = lax.axis_index("mp")
    core = lax.rem(f, 2)
    xpos = lax.rem(f // 2, XS)
    zpos = f // PL
    w = lax.rem(f, PL)

    def remote(src, dst, ssem, rsem, to_f, to_m):
        return pltpu.make_async_remote_copy(
            src_ref=src, dst_ref=dst, send_sem=ssem, recv_sem=rsem,
            device_id=(to_f, to_m), device_id_type=MESH,
        )

    pending = []

    loads = [
        pltpu.make_async_copy(hbm, vmem, w_sem.at[i])
        for i, (hbm, vmem) in enumerate(
            (
                (x_hbm, x_ref), (g_hbm, g_ref), (cf_hbm, cf_row),
                (ws_hbm, ws), (wos_hbm, wos), (wot_hbm, wot), (wt_hbm, wt),
            )
        )
    ]
    for load in loads:
        load.start()

    barrier = pltpu.get_barrier_semaphore()

    for k in range(1, MP):
        pl.semaphore_signal(
            barrier, inc=1, device_id=(f, lax.rem(m + k, MP)), device_id_type=MESH
        )
    for k in range(1, PL):
        pl.semaphore_signal(
            barrier, inc=1, device_id=(zpos * PL + lax.rem(w + k, PL), m), device_id_type=MESH
        )
    for k in range(1, ZS):
        pl.semaphore_signal(
            barrier, inc=1, device_id=(lax.rem(zpos + k, ZS) * PL + w, m), device_id_type=MESH
        )

    def gather_mp(phase, src, buf, rows=slice(0, ROWS)):
        copies = []
        for k in (1, 3, 2):
            copy = remote(
                src.at[rows], buf.at[m, rows], mp_send.at[phase, k - 1], mp_recv.at[phase, k - 1],
                f, lax.rem(m + k, MP),
            )
            copy.start()
            copies.append(copy)
        pending.extend(copies)
        return copies

    def scatter_mp(phase, which, rows=slice(0, ROWS)):
        copies = []
        for k in (1, 3, 2):
            to = lax.rem(m + k, MP)
            copy = remote(
                rsend.at[which, to, rows], rrecv.at[which, k - 1, rows],
                mp_send.at[phase, k - 1], mp_recv.at[phase, k - 1], f, to,
            )
            copy.start()
            copies.append(copy)
        pending.extend(copies)
        return copies

    loads[0].wait()
    x = x_ref[...].astype(F32)
    inv_x = lax.rsqrt(jnp.mean(x * x, -1, keepdims=True) + EPS)
    xall[m] = (x * inv_x).astype(BF16)
    pl.semaphore_wait(barrier, MP - 1 + PL - 1 + ZS - 1)

    ag_x = gather_mp(0, xall.at[m], xall)

    loads[1].wait()
    loads[2].wait()
    gall[m] = g_ref[...]
    row = lax.broadcasted_iota(jnp.int32, (LW, LW), 0)
    col = lax.broadcasted_iota(jnp.int32, (LW, LW), 1)
    clips = cf_row.shape[1]
    c_row = lax.broadcasted_iota(jnp.int32, (clips, clips), 0)
    c_col = lax.broadcasted_iota(jnp.int32, (clips, clips), 1)
    ends_col = jnp.sum(jnp.where(c_col <= c_row, cf_row[...], 0), axis=1, keepdims=True)
    ends_row = jnp.sum(jnp.where(c_row == c_col, ends_col, 0), axis=0, keepdims=True)

    def clip_of(slot, ends, axis):
        frame = lax.rem(zpos * PL + FR - HALO + slot, FR)
        count = jnp.sum(jnp.where(frame >= ends, 1, 0), axis=axis, keepdims=True)
        return count

    slot_lane = lax.broadcasted_iota(jnp.int32, (clips, LW), 1) // 16
    slot_sub = lax.broadcasted_iota(jnp.int32, (LW, clips), 0) // 16
    id_lane = clip_of(slot_lane, ends_col, 0)
    id_sub = clip_of(slot_sub, ends_row, 1)
    used = PL + 2 * HALO
    id_lane = jnp.where(col[:1] // 16 < used, id_lane, -1)
    id_sub = jnp.where(row[:, :1] // 16 < used, id_sub, -1)
    same = jnp.logical_and(id_lane == id_sub, row % 16 == col % 16)
    bias[...] = jnp.where(same, 0.0, NEGATIVE)
    for t in range(4):
        for g in range(2):
            tbuf[t, g, used:] = jnp.zeros((16 - used, 16, LW), BF16)

    halves = [slice(0, ROWS // 2), slice(ROWS // 2, ROWS)]
    masks = [head_mask(h) for h in range(HEADS_LOC)]

    loads[3].wait()
    for copy in ag_x:
        copy.wait_recv()
    ag_g = gather_mp(1, g_ref, gall, slice(0, ROWS // 2))
    x_all = xall[...].reshape(LW, D)
    for j in range(3):
        qkvs[j] = dot(x_all, ws[j]).astype(BF16)

    total = jnp.zeros((LW, LW), F32)
    for h in range(HEADS_LOC):
        p = softmax(dot_bt(qkvs[0] * masks[h], qkvs[1]) * HD ** (-0.5))
        probs[h] = p
        total = total + dot(p.astype(BF16), qkvs[2] * masks[h])
    attn = total.astype(BF16)
    attns[...] = attn.reshape(MP, ROWS, LW)

    loads[4].wait()
    for c in range(4):
        cols = pl.ds(c * 256, 256)
        rsend[0, :, :, cols] = dot(attn, wos[:, cols]).astype(BF16).reshape(MP, ROWS, 256)
    rs1 = [scatter_mp(p, 0, rows) for p, rows in zip((2, 8), halves)]
    ag_g = ag_g + gather_mp(7, g_ref, gall, slice(ROWS // 2, ROWS))
    own = dot(attns[m], wos[...])

    ag_h = []
    for at, rows in enumerate(halves):
        for copy in rs1[at]:
            copy.wait_recv()
        hidden = x_ref[rows].astype(F32) + own[rows]
        for k in range(3):
            hidden = hidden + rrecv[0, k, rows].astype(F32)
        inv_h = lax.rsqrt(jnp.mean(hidden * hidden, -1, keepdims=True) + EPS)
        hid[rows] = hidden
        nhall[m, rows] = (hidden * inv_h).astype(BF16)
        ag_h += gather_mp((3, 9)[at], nhall.at[m], nhall, rows)

    def plane_send(part, source, target, ssems, rsems):
        copies = []
        for k in range(1, PL):
            to = lax.rem(w + k, PL)
            copy = remote(
                source(to), target, ssems.at[part, k - 1], rsems.at[part, k - 1],
                zpos * PL + to, m,
            )
            copy.start()
            copies.append(copy)
        pending.extend(copies)
        return copies

    def halo_view(part, slots):
        return tbuf.at[3, :, slots] if part == 2 else tbuf.at[:3, part, slots]

    def hand_on(part, frame):
        def to_plane(step, slot):
            return remote(
                halo_view(part, HALO + frame), halo_view(part, slot),
                h_send.at[part], h_recv.at[part], lax.rem(zpos + step, ZS) * PL + w, m,
            )

        @pl.when(frame < HALO)
        def _():
            to_plane(ZS - 1, HALO + PL + frame).start()

        @pl.when(frame >= PL - HALO)
        def _():
            to_plane(1, frame - (PL - HALO)).start()

    def hand_wait(part):
        some = halo_view(part, pl.ds(0, 2 * HALO))
        return remote(some, some, h_send.at[part], h_recv.at[part], f, m)

    def receive(part, copies):
        hand_on(part, w)
        for k in range(1, PL):
            copies[k - 1].wait_recv()
            hand_on(part, lax.rem(w + PL - k, PL))

    loads[5].wait()
    for copy in ag_g:
        copy.wait_recv()
    tsend[3] = dot_bt(gall[...].reshape(LW, D), wot[...]).astype(BF16).reshape(2, PL, 16, LW)
    there_up = plane_send(
        2, lambda to: tsend.at[3, :, to], halo_view(2, HALO + w), t_send, t_recv
    )
    for g in range(2):
        tbuf[3, g, HALO + w] = tsend[3, g, w]
    receive(2, there_up)
    loads[6].wait()
    for copy in ag_h:
        copy.wait_recv()
    h_all = nhall[...].reshape(LW, D)
    for j in range(3):
        tsend[j] = dot(h_all, wt[j]).astype(BF16).reshape(2, PL, 16, LW)

    there = [
        plane_send(g, lambda to, g=g: tsend.at[:3, g, to], halo_view(g, HALO + w), t_send, t_recv)
        for g in range(2)
    ]
    for t in range(3):
        for g in range(2):
            tbuf[t, g, HALO + w] = tsend[t, g, w]

    for g in range(2):
        receive(g, there[g])

    zero = jnp.zeros((LW, LW), F32)
    own_slots = slice(HALO, HALO + PL)
    back = []
    for g in range(2):
        hand_wait(g).wait_recv()
        if g == 0:
            hand_wait(2).wait_recv()
        queries, keys, values, upstream = [tbuf[t, g].reshape(LW, LW) for t in range(4)]
        attn_t, d_q, d_k, d_v = zero, zero, zero, zero
        for h in range(HEADS_LOC):
            qm = queries * masks[h]
            om = upstream * masks[h]
            p = softmax(dot_bt(qm, keys) * HD ** (-0.5) + bias[...])
            pb = p.astype(BF16)
            attn_t = attn_t + dot(pb, values * masks[h])
            d_v = d_v + dot_at(pb, om)
            ds = score_grads(p, dot_bt(om, values))
            d_q = d_q + dot(ds, keys * masks[h])
            d_k = d_k + dot_at(ds, qm)
        for t, full in enumerate((d_q, d_k, d_v, attn_t)):
            tres[t, g] = full.astype(BF16).reshape(16, 16, LW)[own_slots]
        back += plane_send(
            g, lambda to, g=g: tres.at[:3, g, to], dqkv.at[:3, g, w], b_send, b_recv
        )
        for t in range(4):
            dqkv[t, g, w] = tres[t, g, w]
    back_attn = plane_send(2, lambda to: tres.at[3, :, to], dqkv.at[3, :, w], b_send, b_recv)
    for copy in back:
        copy.wait_recv()

    def project_back(which, grads, weights):
        for c in range(4):
            cols = pl.ds(c * 256, 256)
            part = dot_bt(grads[0], weights[0, cols])
            part = part + dot_bt(grads[1], weights[1, cols])
            part = part + dot_bt(grads[2], weights[2, cols])
            rsend[which, :, :, cols] = part.astype(BF16).reshape(MP, ROWS, 256)

    def own_back(grads, weights):
        part = dot_bt(grads[0], weights[0])
        part = part + dot_bt(grads[1], weights[1])
        return part + dot_bt(grads[2], weights[2])

    def weight_grad(j, left_ref, right):
        for c in range(4):
            left = left_ref[:, :, c * 256 : (c + 1) * 256].reshape(LW, 256)
            gbuf[j, 8 * c : 8 * c + 8] = dot_at(left, right).astype(BF16).reshape(8, 2, 16, LW)

    first = [0, 2, 4, 5, 6, 7]
    count = [2, 2, 1, 1, 1, 1]

    def core_send(b):
        some = slice(first[b], first[b] + count[b])
        copy = remote(
            gbuf.at[some, :, 1 - core], grecv1.at[some],
            c_send.at[b], c_recv.at[b], f + 1 - 2 * core, m,
        )
        copy.start()
        pending.append(copy)
        return copy

    def send_x(b, source, target):
        copies = []
        for k in (1, 3, 2):
            to = lax.rem(xpos + k, XS)
            copy = remote(
                source(to), target(k - 1), x_send.at[b, k - 1], x_recv.at[b, k - 1],
                (zpos * XS + to) * 2 + core, m,
            )
            copy.start()
            copies.append(copy)
        pending.extend(copies)
        return copies

    def send_z(b, source, target):
        copies = []
        for k in (4, 3, 5, 2, 6, 1, 7):
            to = lax.rem(zpos + k, ZS)
            copy = remote(
                source(to), target(k - 1), z_send.at[b, k - 1], z_recv.at[b, k - 1],
                (to * XS + xpos) * 2 + core, m,
            )
            copy.start()
            copies.append(copy)
        pending.extend(copies)
        return copies

    def mats(b):
        return slice(first[b], first[b] + count[b])

    def wait_all(copies):
        for copy in copies:
            copy.wait_recv()

    def core_sum(b, copy):
        copy.wait_recv()
        for j in range(first[b], first[b] + count[b]):
            summed = gbuf[j, :, core].astype(F32) + grecv1[j].astype(F32)
            gsum1[j] = summed.astype(BF16).reshape(ZS, XS, 16, LW)

    def core_sum_x_send(b, copy):
        core_sum(b, copy)
        return send_x(b, lambda to: gsum1.at[mats(b), :, to], lambda k: grecv2.at[k, mats(b)])

    def core_sum_z_send(b, copy):
        core_sum(b, copy)
        return send_z(b, lambda to: gsum1.at[mats(b), to], lambda k: hrecv2.at[k, mats(b)])

    def x_sum_z_send(b, copies):
        wait_all(copies)
        for j in range(first[b], first[b] + count[b]):
            summed = gsum1[j, :, xpos].astype(F32)
            for k in range(XS - 1):
                summed = summed + grecv2[k, j].astype(F32)
            gsum2[j] = summed.astype(BF16)
        return send_z(b, lambda to: gsum2.at[mats(b), to], lambda k: grecv3.at[k, mats(b)])

    def z_sum_x_send(b, copies):
        wait_all(copies)
        for j in range(first[b], first[b] + count[b]):
            summed = gsum1[j, zpos].astype(F32)
            for k in range(ZS - 1):
                summed = summed + hrecv2[k, j].astype(F32)
            hsum2[j] = summed.astype(BF16)
        return send_x(b, lambda to: hsum2.at[mats(b), to], lambda k: hrecv3.at[k, mats(b)])

    def z_sum(b, copies, outs):
        wait_all(copies)
        for at, out in enumerate(outs):
            j = first[b] + at
            summed = gsum2[j, zpos].astype(F32)
            for k in range(ZS - 1):
                summed = summed + grecv3[k, j].astype(F32)
            out[...] = summed

    def x_sum(b, copies, outs):
        wait_all(copies)
        for at, out in enumerate(outs):
            j = first[b] + at
            summed = hsum2[j, xpos].astype(F32)
            for k in range(XS - 1):
                summed = summed + hrecv3[k, j].astype(F32)
            out[...] = summed

    grads_t = [dqkv[j].reshape(LW, LW) for j in range(3)]
    project_back(1, grads_t, wt)
    rs2 = [scatter_mp(p, 1, rows) for p, rows in zip((4, 10), halves)]
    for j in range(2):
        weight_grad(j, nhall, grads_t[j])
    core_t1 = core_send(0)
    weight_grad(2, nhall, grads_t[2])
    wait_all(back_attn)
    weight_grad(3, gall, dqkv[3].reshape(LW, LW))
    core_t2 = core_send(1)
    quarter = pl.ds(4 * lax.rem(m, 2), 4)
    own = own_back([dqkv[j, m // 2, quarter].reshape(ROWS, LW) for j in range(3)], wt)
    x_t1 = core_sum_x_send(0, core_t1)
    z_t2 = core_sum_z_send(1, core_t2)
    ag_d = []
    for at, rows in enumerate(halves):
        wait_all(rs2[at])
        d_nh = own[rows]
        for k in range(3):
            d_nh = d_nh + rrecv[1, k, rows].astype(F32)
        hidden = hid[rows]
        inv_h = lax.rsqrt(jnp.mean(hidden * hidden, -1, keepdims=True) + EPS)
        d_hidden = g_ref[rows].astype(F32) + norm_back(hidden, inv_h, d_nh)
        dhid[rows] = d_hidden
        dhall[m, rows] = d_hidden.astype(BF16)
        ag_d += gather_mp((5, 11)[at], dhall.at[m], dhall, rows)
    z_t1 = x_sum_z_send(0, x_t1)
    wait_all(ag_d)

    weight_grad(7, dhall, attns[...].reshape(LW, LW))
    core_o = core_send(5)
    das = dot_bt(dhall[...].reshape(LW, D), wos[...]).astype(BF16)

    def keep(j, grad):
        dqs[j] = grad.astype(BF16).reshape(MP, ROWS, LW)
        weight_grad(4 + j, xall, dqs[j].reshape(LW, LW))
        return core_send(2 + j)

    d_v = zero
    for h in range(HEADS_LOC):
        d_v = d_v + dot_at(probs[h].astype(BF16), das * masks[h])
    core_v = keep(2, d_v)
    x_o = core_sum_x_send(5, core_o)
    d_q, d_k = zero, zero
    for h in range(HEADS_LOC):
        ds = score_grads(probs[h], dot_bt(das * masks[h], qkvs[2]))
        d_q = d_q + dot(ds, qkvs[1] * masks[h])
        d_k = d_k + dot_at(ds, qkvs[0] * masks[h])
    core_q = keep(0, d_q)
    core_k = keep(1, d_k)
    z_v = core_sum_z_send(4, core_v)
    x_q = core_sum_x_send(2, core_q)
    x_k = core_sum_x_send(3, core_k)
    project_back(2, [dqs[j].reshape(LW, LW) for j in range(3)], ws)
    rs3 = scatter_mp(6, 2)
    x_t2 = z_sum_x_send(1, z_t2)
    z_o = x_sum_z_send(5, x_o)
    z_sum(0, z_t1, [gt_ref.at[0], gt_ref.at[1]])
    d_nx = own_back([dqs[j, m] for j in range(3)], ws)
    z_q = x_sum_z_send(2, x_q)
    x_sum(1, x_t2, [gt_ref.at[2], gto_ref])
    z_k = x_sum_z_send(3, x_k)
    x_v = z_sum_x_send(4, z_v)
    wait_all(rs3)
    for k in range(3):
        d_nx = d_nx + rrecv[2, k].astype(F32)
    x = x_ref[...].astype(F32)
    inv_x = lax.rsqrt(jnp.mean(x * x, -1, keepdims=True) + EPS)
    tok_ref[...] = (dhid[...] + norm_back(x, inv_x, d_nx)).astype(BF16)
    z_sum(5, z_o, [gso_ref])
    x_sum(4, x_v, [gs_ref.at[2]])
    z_sum(2, z_q, [gs_ref.at[0]])
    z_sum(3, z_k, [gs_ref.at[1]])
    for copy in pending:
        copy.wait_send()
    for part in range(3):
        hand_wait(part).wait_send()


def deliver(*refs):
    for source, target in zip(refs[:5], refs[5:]):
        target[...] = source[...]


def shards(x, g, ws, wos, wt, wot, clip_frames):
    clips = clip_frames.shape[0]
    vmem = pl.BlockSpec(memory_space=pltpu.VMEM)
    dma = pltpu.SemaphoreType.DMA
    scratch = [
        pltpu.VMEM((ROWS, D), BF16),
        pltpu.VMEM((ROWS, D), BF16),
        pltpu.VMEM((1, clips), jnp.int32),
        pltpu.VMEM((3, D, LW), BF16),
        pltpu.VMEM((LW, D), BF16),
        pltpu.VMEM((3, D, LW), BF16),
        pltpu.VMEM((LW, D), BF16),
        pltpu.VMEM((MP, ROWS, D), BF16),
        pltpu.VMEM((MP, ROWS, D), BF16),
        pltpu.VMEM((MP, ROWS, D), BF16),
        pltpu.VMEM((MP, ROWS, D), BF16),
        pltpu.VMEM((LW, LW), F32),
        pltpu.VMEM((3, LW, LW), BF16),
        pltpu.VMEM((HEADS_LOC, LW, LW), F32),
        pltpu.VMEM((MP, ROWS, LW), BF16),
        pltpu.VMEM((ROWS, D), F32),
        pltpu.VMEM((ROWS, D), F32),
        pltpu.VMEM((3, MP, ROWS, D), BF16),
        pltpu.VMEM((3, MP - 1, ROWS, D), BF16),
        pltpu.VMEM((4, 2, PL, 16, LW), BF16),
        pltpu.VMEM((4, 2, 16, 16, LW), BF16),
        pltpu.VMEM((4, 2, PL, 16, LW), BF16),
        pltpu.VMEM((4, 2, PL, 16, LW), BF16),
        pltpu.VMEM((3, MP, ROWS, LW), BF16),
        pltpu.VMEM((8, FR // 2, 2, 16, LW), BF16),
        pltpu.VMEM((8, FR // 2, 16, LW), BF16),
        pltpu.VMEM((8, ZS, XS, 16, LW), BF16),
        pltpu.VMEM((XS - 1, 8, ZS, 16, LW), BF16),
        pltpu.VMEM((8, ZS, 16, LW), BF16),
        pltpu.VMEM((ZS - 1, 8, 16, LW), BF16),
        pltpu.VMEM((ZS - 1, 8, XS, 16, LW), BF16),
        pltpu.VMEM((8, XS, 16, LW), BF16),
        pltpu.VMEM((XS - 1, 8, 16, LW), BF16),
        dma((7,)),
        dma((12, 3)),
        dma((12, 3)),
        dma((3, PL - 1)),
        dma((3, PL - 1)),
        dma((3,)),
        dma((3,)),
        dma((3, PL - 1)),
        dma((3, PL - 1)),
        dma((6,)),
        dma((6,)),
        dma((6, XS - 1)),
        dma((6, XS - 1)),
        dma((6, ZS - 1)),
        dma((6, ZS - 1)),
    ]
    tokens, gs, gso, gt, gto = pl.pallas_call(
        kernel,
        out_shape=(
            jax.ShapeDtypeStruct((ROWS, D), BF16),
            jax.ShapeDtypeStruct((3, 16, LW), F32),
            jax.ShapeDtypeStruct((16, LW), F32),
            jax.ShapeDtypeStruct((3, 16, LW), F32),
            jax.ShapeDtypeStruct((16, LW), F32),
        ),
        in_specs=[pl.BlockSpec(memory_space=pltpu.HBM)] * 7,
        out_specs=[vmem] * 5,
        scratch_shapes=scratch,
        compiler_params=pltpu.CompilerParams(
            collective_id=0, has_side_effects=True, vmem_limit_bytes=60 * 1024 * 1024
        ),
        cost_estimate=pl.CostEstimate(
            flops=3_500_000_000, bytes_accessed=6_000_000, transcendentals=1_000_000
        ),
    )(
        x.reshape(ROWS, D), g.reshape(ROWS, D), clip_frames.reshape(1, clips), ws, wos, wt, wot,
    )
    results = (tokens, gs, gso, gt, gto)
    tokens, gs, gso, gt, gto = pl.pallas_call(
        deliver,
        out_shape=tuple(jax.ShapeDtypeStruct(r.shape, r.dtype) for r in results),
        in_specs=[vmem] * 5,
        out_specs=[vmem] * 5,
        compiler_params=pltpu.CompilerParams(vmem_limit_bytes=60 * 1024 * 1024),
    )(*results)
    return tokens.reshape(1, ROWS, D), gs, gso.T, gt, gto.T


def solution(mesh):
    placed = (
        P("frames", "mp", None),
        P("frames", "mp", None),
        P(None, None, "mp"),
        P("mp", None),
        P(None, None, "mp"),
        P("mp", None),
        P(),
    )
    return jax.shard_map(
        shards,
        mesh=mesh,
        in_specs=placed,
        out_specs=(
            P("frames", "mp", None),
            P(None, "frames", "mp"),
            P("mp", "frames"),
            P(None, "frames", "mp"),
            P("mp", "frames"),
        ),
        check_vma=False,
    )
```

```python
import jax
import jax.numpy as jnp
from jax import lax
from jax.experimental import pallas as pl
from jax.experimental.pallas import tpu as pltpu
from jax.sharding import PartitionSpec as P

HD = 64
EPS = 1e-06
NEGATIVE = -1e30
FR = 64
MP = 4
XS = 4
ZS = 8
PL = 8
HALO = 3
D = 1024
LW = 256
ROWS = 64
HEADS_LOC = 4
MESH = pl.DeviceIdType.MESH
F32 = jnp.float32
BF16 = jnp.bfloat16


def dot(a, b):
    return lax.dot_general(a, b, (((1,), (0,)), ((), ())), preferred_element_type=F32)


def dot_bt(a, b):
    return lax.dot_general(a, b, (((1,), (1,)), ((), ())), preferred_element_type=F32)


def dot_at(a, b):
    return lax.dot_general(a, b, (((0,), (0,)), ((), ())), preferred_element_type=F32)


def head_mask(h):
    lane = lax.broadcasted_iota(jnp.int32, (1, LW), 1)
    return jnp.where(lane // HD == h, 1.0, 0.0).astype(BF16)


def softmax(scores):
    expo = jnp.exp(scores - jnp.max(scores, -1, keepdims=True))
    return expo / jnp.sum(expo, -1, keepdims=True)


def score_grads(probs, d_probs):
    delta = jnp.sum(probs * d_probs, -1, keepdims=True)
    return (probs * (d_probs - delta) * HD ** (-0.5)).astype(BF16)


def norm_back(values_in, inv_rms, upstream):
    mean = jnp.mean(upstream * values_in, -1, keepdims=True)
    return inv_rms * (upstream - values_in * (inv_rms * inv_rms) * mean)


def kernel(
    x_hbm, g_hbm, cf_hbm, ws_hbm, wos_hbm, wt_hbm, wot_hbm,
    tok_ref, gs_ref, gso_ref, gt_ref, gto_ref,
    x_ref, g_ref, cf_row, ws, wos, wt, wot, xall, gall, nhall, dhall,
    bias, qkvs, probs, attns, hid, dhid,
    rsend, rrecv, tsend, tbuf, tres, dqkv, dqs,
    gbuf, grecv1, gsum1, grecv2, gsum2, grecv3, hrecv2, hsum2, hrecv3,
    w_sem, mp_send, mp_recv, t_send, t_recv, h_send, h_recv, b_send, b_recv,
    c_send, c_recv, x_send, x_recv, z_send, z_recv,
):
    f = lax.axis_index("frames")
    m = lax.axis_index("mp")
    core = lax.rem(f, 2)
    xpos = lax.rem(f // 2, XS)
    zpos = f // PL
    w = lax.rem(f, PL)

    def remote(src, dst, ssem, rsem, to_f, to_m):
        return pltpu.make_async_remote_copy(
            src_ref=src, dst_ref=dst, send_sem=ssem, recv_sem=rsem,
            device_id=(to_f, to_m), device_id_type=MESH,
        )

    pending = []

    loads = [
        pltpu.make_async_copy(hbm, vmem, w_sem.at[i])
        for i, (hbm, vmem) in enumerate(
            (
                (x_hbm, x_ref), (g_hbm, g_ref), (cf_hbm, cf_row),
                (ws_hbm, ws), (wos_hbm, wos), (wot_hbm, wot), (wt_hbm, wt),
            )
        )
    ]
    for load in loads:
        load.start()

    barrier = pltpu.get_barrier_semaphore()

    for k in range(1, MP):
        pl.semaphore_signal(
            barrier, inc=1, device_id=(f, lax.rem(m + k, MP)), device_id_type=MESH
        )
    for k in range(1, PL):
        pl.semaphore_signal(
            barrier, inc=1, device_id=(zpos * PL + lax.rem(w + k, PL), m), device_id_type=MESH
        )
    for k in range(1, ZS):
        pl.semaphore_signal(
            barrier, inc=1, device_id=(lax.rem(zpos + k, ZS) * PL + w, m), device_id_type=MESH
        )

    def gather_mp(phase, src, buf, rows=slice(0, ROWS)):
        copies = []
        for k in (1, 3, 2):
            copy = remote(
                src.at[rows], buf.at[m, rows], mp_send.at[phase, k - 1], mp_recv.at[phase, k - 1],
                f, lax.rem(m + k, MP),
            )
            copy.start()
            copies.append(copy)
        pending.extend(copies)
        return copies

    def scatter_mp(phase, which, rows=slice(0, ROWS)):
        copies = []
        for k in (1, 3, 2):
            to = lax.rem(m + k, MP)
            copy = remote(
                rsend.at[which, to, rows], rrecv.at[which, k - 1, rows],
                mp_send.at[phase, k - 1], mp_recv.at[phase, k - 1], f, to,
            )
            copy.start()
            copies.append(copy)
        pending.extend(copies)
        return copies

    loads[0].wait()
    x = x_ref[...].astype(F32)
    inv_x = lax.rsqrt(jnp.mean(x * x, -1, keepdims=True) + EPS)
    xall[m] = (x * inv_x).astype(BF16)
    pl.semaphore_wait(barrier, MP - 1 + PL - 1 + ZS - 1)

    ag_x = gather_mp(0, xall.at[m], xall)

    loads[1].wait()
    loads[2].wait()
    gall[m] = g_ref[...]
    row = lax.broadcasted_iota(jnp.int32, (LW, LW), 0)
    col = lax.broadcasted_iota(jnp.int32, (LW, LW), 1)
    clips = cf_row.shape[1]
    c_row = lax.broadcasted_iota(jnp.int32, (clips, clips), 0)
    c_col = lax.broadcasted_iota(jnp.int32, (clips, clips), 1)
    ends_col = jnp.sum(jnp.where(c_col <= c_row, cf_row[...], 0), axis=1, keepdims=True)
    ends_row = jnp.sum(jnp.where(c_row == c_col, ends_col, 0), axis=0, keepdims=True)

    def clip_of(slot, ends, axis):
        frame = lax.rem(zpos * PL + FR - HALO + slot, FR)
        count = jnp.sum(jnp.where(frame >= ends, 1, 0), axis=axis, keepdims=True)
        return count

    slot_lane = lax.broadcasted_iota(jnp.int32, (clips, LW), 1) // 16
    slot_sub = lax.broadcasted_iota(jnp.int32, (LW, clips), 0) // 16
    id_lane = clip_of(slot_lane, ends_col, 0)
    id_sub = clip_of(slot_sub, ends_row, 1)
    used = PL + 2 * HALO
    id_lane = jnp.where(col[:1] // 16 < used, id_lane, -1)
    id_sub = jnp.where(row[:, :1] // 16 < used, id_sub, -1)
    same = jnp.logical_and(id_lane == id_sub, row % 16 == col % 16)
    bias[...] = jnp.where(same, 0.0, NEGATIVE)
    for t in range(4):
        for g in range(2):
            tbuf[t, g, used:] = jnp.zeros((16 - used, 16, LW), BF16)

    halves = [slice(0, ROWS // 2), slice(ROWS // 2, ROWS)]
    masks = [head_mask(h) for h in range(HEADS_LOC)]

    loads[3].wait()
    for copy in ag_x:
        copy.wait_recv()
    near_g = {}
    for k in (1, 3):
        near_g[k] = remote(
            g_ref, gall.at[m], mp_send.at[1, k - 1], mp_recv.at[1, k - 1], f, lax.rem(m + k, MP)
        )
        near_g[k].start()
        pending.append(near_g[k])
    x_all = xall[...].reshape(LW, D)
    for j in range(3):
        qkvs[j] = dot(x_all, ws[j]).astype(BF16)

    total = jnp.zeros((LW, LW), F32)
    for h in range(HEADS_LOC):
        p = softmax(dot_bt(qkvs[0] * masks[h], qkvs[1]) * HD ** (-0.5))
        probs[h] = p
        total = total + dot(p.astype(BF16), qkvs[2] * masks[h])
    attn = total.astype(BF16)
    attns[...] = attn.reshape(MP, ROWS, LW)

    loads[4].wait()
    for c in range(4):
        cols = pl.ds(c * 256, 256)
        rsend[0, :, :, cols] = dot(attn, wos[:, cols]).astype(BF16).reshape(MP, ROWS, 256)
    rs1 = [scatter_mp(p, 0, rows) for p, rows in zip((2, 8), halves)]
    own = dot(attns[m], wos[...])
    far_g = []
    for k, rows in zip((1, 3), halves):
        near_g[k].wait_recv()
        chunk = gall.at[lax.rem(m + MP - k, MP), rows]
        copy = remote(
            chunk, chunk, mp_send.at[7, k - 1], mp_recv.at[7, k - 1], f, lax.rem(m + k, MP)
        )
        copy.start()
        far_g.append(copy)
    pending.extend(far_g)

    ag_h = []
    for at, rows in enumerate(halves):
        for copy in rs1[at]:
            copy.wait_recv()
        hidden = x_ref[rows].astype(F32) + own[rows]
        for k in range(3):
            hidden = hidden + rrecv[0, k, rows].astype(F32)
        inv_h = lax.rsqrt(jnp.mean(hidden * hidden, -1, keepdims=True) + EPS)
        hid[rows] = hidden
        nhall[m, rows] = (hidden * inv_h).astype(BF16)
        ag_h += gather_mp((3, 9)[at], nhall.at[m], nhall, rows)

    def plane_send(part, source, target, ssems, rsems):
        copies = []
        for k in range(1, PL):
            to = lax.rem(w + k, PL)
            copy = remote(
                source(to), target, ssems.at[part, k - 1], rsems.at[part, k - 1],
                zpos * PL + to, m,
            )
            copy.start()
            copies.append(copy)
        pending.extend(copies)
        return copies

    def halo_view(part, slots):
        return tbuf.at[3, :, slots] if part == 2 else tbuf.at[:3, part, slots]

    def hand_on(part, frame):
        def to_plane(step, slot):
            return remote(
                halo_view(part, HALO + frame), halo_view(part, slot),
                h_send.at[part], h_recv.at[part], lax.rem(zpos + step, ZS) * PL + w, m,
            )

        @pl.when(frame < HALO)
        def _():
            to_plane(ZS - 1, HALO + PL + frame).start()

        @pl.when(frame >= PL - HALO)
        def _():
            to_plane(1, frame - (PL - HALO)).start()

    def hand_wait(part):
        some = halo_view(part, pl.ds(0, 2 * HALO))
        return remote(some, some, h_send.at[part], h_recv.at[part], f, m)

    def receive(part, copies):
        hand_on(part, w)
        for k in range(1, PL):
            copies[k - 1].wait_recv()
            hand_on(part, lax.rem(w + PL - k, PL))

    loads[5].wait()
    for copy in far_g:
        copy.wait_recv()
    tsend[3] = dot_bt(gall[...].reshape(LW, D), wot[...]).astype(BF16).reshape(2, PL, 16, LW)
    there_up = plane_send(
        2, lambda to: tsend.at[3, :, to], halo_view(2, HALO + w), t_send, t_recv
    )
    for g in range(2):
        tbuf[3, g, HALO + w] = tsend[3, g, w]
    receive(2, there_up)
    loads[6].wait()
    for copy in ag_h:
        copy.wait_recv()
    h_all = nhall[...].reshape(LW, D)
    for j in range(3):
        tsend[j] = dot(h_all, wt[j]).astype(BF16).reshape(2, PL, 16, LW)

    there = [
        plane_send(g, lambda to, g=g: tsend.at[:3, g, to], halo_view(g, HALO + w), t_send, t_recv)
        for g in range(2)
    ]
    for t in range(3):
        for g in range(2):
            tbuf[t, g, HALO + w] = tsend[t, g, w]

    for g in range(2):
        receive(g, there[g])

    zero = jnp.zeros((LW, LW), F32)
    own_slots = slice(HALO, HALO + PL)
    back = []
    for g in range(2):
        hand_wait(g).wait_recv()
        if g == 0:
            hand_wait(2).wait_recv()
        queries, keys, values, upstream = [tbuf[t, g].reshape(LW, LW) for t in range(4)]
        attn_t, d_q, d_k, d_v = zero, zero, zero, zero
        for h in range(HEADS_LOC):
            qm = queries * masks[h]
            om = upstream * masks[h]
            p = softmax(dot_bt(qm, keys) * HD ** (-0.5) + bias[...])
            pb = p.astype(BF16)
            attn_t = attn_t + dot(pb, values * masks[h])
            d_v = d_v + dot_at(pb, om)
            ds = score_grads(p, dot_bt(om, values))
            d_q = d_q + dot(ds, keys * masks[h])
            d_k = d_k + dot_at(ds, qm)
        for t, full in enumerate((d_q, d_k, d_v, attn_t)):
            tres[t, g] = full.astype(BF16).reshape(16, 16, LW)[own_slots]
        back += plane_send(
            g, lambda to, g=g: tres.at[:3, g, to], dqkv.at[:3, g, w], b_send, b_recv
        )
        for t in range(4):
            dqkv[t, g, w] = tres[t, g, w]
    back_attn = plane_send(2, lambda to: tres.at[3, :, to], dqkv.at[3, :, w], b_send, b_recv)
    for copy in back:
        copy.wait_recv()

    def project_back(which, grads, weights):
        for c in range(4):
            cols = pl.ds(c * 256, 256)
            part = dot_bt(grads[0], weights[0, cols])
            part = part + dot_bt(grads[1], weights[1, cols])
            part = part + dot_bt(grads[2], weights[2, cols])
            rsend[which, :, :, cols] = part.astype(BF16).reshape(MP, ROWS, 256)

    def own_back(grads, weights):
        part = dot_bt(grads[0], weights[0])
        part = part + dot_bt(grads[1], weights[1])
        return part + dot_bt(grads[2], weights[2])

    def weight_grad(j, left_ref, right):
        for c in range(4):
            left = left_ref[:, :, c * 256 : (c + 1) * 256].reshape(LW, 256)
            gbuf[j, 8 * c : 8 * c + 8] = dot_at(left, right).astype(BF16).reshape(8, 2, 16, LW)

    first = [0, 2, 4, 5, 6, 7]
    count = [2, 2, 1, 1, 1, 1]

    def core_send(b):
        some = slice(first[b], first[b] + count[b])
        copy = remote(
            gbuf.at[some, :, 1 - core], grecv1.at[some],
            c_send.at[b], c_recv.at[b], f + 1 - 2 * core, m,
        )
        copy.start()
        pending.append(copy)
        return copy

    def send_x(b, source, target):
        copies = []
        for k in (1, 3, 2):
            to = lax.rem(xpos + k, XS)
            copy = remote(
                source(to), target(k - 1), x_send.at[b, k - 1], x_recv.at[b, k - 1],
                (zpos * XS + to) * 2 + core, m,
            )
            copy.start()
            copies.append(copy)
        pending.extend(copies)
        return copies

    def send_z(b, source, target):
        copies = []
        for k in (4, 3, 5, 2, 6, 1, 7):
            to = lax.rem(zpos + k, ZS)
            copy = remote(
                source(to), target(k - 1), z_send.at[b, k - 1], z_recv.at[b, k - 1],
                (to * XS + xpos) * 2 + core, m,
            )
            copy.start()
            copies.append(copy)
        pending.extend(copies)
        return copies

    def mats(b):
        return slice(first[b], first[b] + count[b])

    def wait_all(copies):
        for copy in copies:
            copy.wait_recv()

    def core_sum(b, copy):
        copy.wait_recv()
        for j in range(first[b], first[b] + count[b]):
            summed = gbuf[j, :, core].astype(F32) + grecv1[j].astype(F32)
            gsum1[j] = summed.astype(BF16).reshape(ZS, XS, 16, LW)

    def core_sum_x_send(b, copy):
        core_sum(b, copy)
        return send_x(b, lambda to: gsum1.at[mats(b), :, to], lambda k: grecv2.at[k, mats(b)])

    def core_sum_z_send(b, copy):
        core_sum(b, copy)
        return send_z(b, lambda to: gsum1.at[mats(b), to], lambda k: hrecv2.at[k, mats(b)])

    def x_sum_z_send(b, copies):
        wait_all(copies)
        for j in range(first[b], first[b] + count[b]):
            summed = gsum1[j, :, xpos].astype(F32)
            for k in range(XS - 1):
                summed = summed + grecv2[k, j].astype(F32)
            gsum2[j] = summed.astype(BF16)
        return send_z(b, lambda to: gsum2.at[mats(b), to], lambda k: grecv3.at[k, mats(b)])

    def z_sum_x_send(b, copies):
        wait_all(copies)
        for j in range(first[b], first[b] + count[b]):
            summed = gsum1[j, zpos].astype(F32)
            for k in range(ZS - 1):
                summed = summed + hrecv2[k, j].astype(F32)
            hsum2[j] = summed.astype(BF16)
        return send_x(b, lambda to: hsum2.at[mats(b), to], lambda k: hrecv3.at[k, mats(b)])

    def z_sum(b, copies, outs):
        wait_all(copies)
        for at, out in enumerate(outs):
            j = first[b] + at
            summed = gsum2[j, zpos].astype(F32)
            for k in range(ZS - 1):
                summed = summed + grecv3[k, j].astype(F32)
            out[...] = summed

    def x_sum(b, copies, outs):
        wait_all(copies)
        for at, out in enumerate(outs):
            j = first[b] + at
            summed = hsum2[j, xpos].astype(F32)
            for k in range(XS - 1):
                summed = summed + hrecv3[k, j].astype(F32)
            out[...] = summed

    grads_t = [dqkv[j].reshape(LW, LW) for j in range(3)]
    project_back(1, grads_t, wt)
    rs2 = [scatter_mp(p, 1, rows) for p, rows in zip((4, 10), halves)]
    for j in range(2):
        weight_grad(j, nhall, grads_t[j])
    core_t1 = core_send(0)
    weight_grad(2, nhall, grads_t[2])
    wait_all(back_attn)
    weight_grad(3, gall, dqkv[3].reshape(LW, LW))
    core_t2 = core_send(1)
    quarter = pl.ds(4 * lax.rem(m, 2), 4)
    own = own_back([dqkv[j, m // 2, quarter].reshape(ROWS, LW) for j in range(3)], wt)
    x_t1 = core_sum_x_send(0, core_t1)
    z_t2 = core_sum_z_send(1, core_t2)
    ag_d = []
    for at, rows in enumerate(halves):
        wait_all(rs2[at])
        d_nh = own[rows]
        for k in range(3):
            d_nh = d_nh + rrecv[1, k, rows].astype(F32)
        hidden = hid[rows]
        inv_h = lax.rsqrt(jnp.mean(hidden * hidden, -1, keepdims=True) + EPS)
        d_hidden = g_ref[rows].astype(F32) + norm_back(hidden, inv_h, d_nh)
        dhid[rows] = d_hidden
        dhall[m, rows] = d_hidden.astype(BF16)
        ag_d += gather_mp((5, 11)[at], dhall.at[m], dhall, rows)
    z_t1 = x_sum_z_send(0, x_t1)
    wait_all(ag_d)

    weight_grad(7, dhall, attns[...].reshape(LW, LW))
    core_o = core_send(5)
    das = dot_bt(dhall[...].reshape(LW, D), wos[...]).astype(BF16)

    def keep(j, grad):
        dqs[j] = grad.astype(BF16).reshape(MP, ROWS, LW)
        weight_grad(4 + j, xall, dqs[j].reshape(LW, LW))
        return core_send(2 + j)

    d_v = zero
    for h in range(HEADS_LOC):
        d_v = d_v + dot_at(probs[h].astype(BF16), das * masks[h])
    core_v = keep(2, d_v)
    x_o = core_sum_x_send(5, core_o)
    d_q, d_k = zero, zero
    for h in range(HEADS_LOC):
        ds = score_grads(probs[h], dot_bt(das * masks[h], qkvs[2]))
        d_q = d_q + dot(ds, qkvs[1] * masks[h])
        d_k = d_k + dot_at(ds, qkvs[0] * masks[h])
    core_q = keep(0, d_q)
    core_k = keep(1, d_k)
    z_v = core_sum_z_send(4, core_v)
    x_q = core_sum_x_send(2, core_q)
    x_k = core_sum_x_send(3, core_k)
    project_back(2, [dqs[j].reshape(LW, LW) for j in range(3)], ws)
    rs3 = scatter_mp(6, 2)
    x_t2 = z_sum_x_send(1, z_t2)
    z_o = x_sum_z_send(5, x_o)
    z_sum(0, z_t1, [gt_ref.at[0], gt_ref.at[1]])
    d_nx = own_back([dqs[j, m] for j in range(3)], ws)
    z_q = x_sum_z_send(2, x_q)
    x_sum(1, x_t2, [gt_ref.at[2], gto_ref])
    z_k = x_sum_z_send(3, x_k)
    x_v = z_sum_x_send(4, z_v)
    wait_all(rs3)
    for k in range(3):
        d_nx = d_nx + rrecv[2, k].astype(F32)
    x = x_ref[...].astype(F32)
    inv_x = lax.rsqrt(jnp.mean(x * x, -1, keepdims=True) + EPS)
    tok_ref[...] = (dhid[...] + norm_back(x, inv_x, d_nx)).astype(BF16)
    z_sum(5, z_o, [gso_ref])
    x_sum(4, x_v, [gs_ref.at[2]])
    z_sum(2, z_q, [gs_ref.at[0]])
    z_sum(3, z_k, [gs_ref.at[1]])
    for copy in pending:
        copy.wait_send()
    for part in range(3):
        hand_wait(part).wait_send()


def deliver(*refs):
    for source, target in zip(refs[:5], refs[5:]):
        target[...] = source[...]


def shards(x, g, ws, wos, wt, wot, clip_frames):
    clips = clip_frames.shape[0]
    vmem = pl.BlockSpec(memory_space=pltpu.VMEM)
    dma = pltpu.SemaphoreType.DMA
    scratch = [
        pltpu.VMEM((ROWS, D), BF16),
        pltpu.VMEM((ROWS, D), BF16),
        pltpu.VMEM((1, clips), jnp.int32),
        pltpu.VMEM((3, D, LW), BF16),
        pltpu.VMEM((LW, D), BF16),
        pltpu.VMEM((3, D, LW), BF16),
        pltpu.VMEM((LW, D), BF16),
        pltpu.VMEM((MP, ROWS, D), BF16),
        pltpu.VMEM((MP, ROWS, D), BF16),
        pltpu.VMEM((MP, ROWS, D), BF16),
        pltpu.VMEM((MP, ROWS, D), BF16),
        pltpu.VMEM((LW, LW), F32),
        pltpu.VMEM((3, LW, LW), BF16),
        pltpu.VMEM((HEADS_LOC, LW, LW), F32),
        pltpu.VMEM((MP, ROWS, LW), BF16),
        pltpu.VMEM((ROWS, D), F32),
        pltpu.VMEM((ROWS, D), F32),
        pltpu.VMEM((3, MP, ROWS, D), BF16),
        pltpu.VMEM((3, MP - 1, ROWS, D), BF16),
        pltpu.VMEM((4, 2, PL, 16, LW), BF16),
        pltpu.VMEM((4, 2, 16, 16, LW), BF16),
        pltpu.VMEM((4, 2, PL, 16, LW), BF16),
        pltpu.VMEM((4, 2, PL, 16, LW), BF16),
        pltpu.VMEM((3, MP, ROWS, LW), BF16),
        pltpu.VMEM((8, FR // 2, 2, 16, LW), BF16),
        pltpu.VMEM((8, FR // 2, 16, LW), BF16),
        pltpu.VMEM((8, ZS, XS, 16, LW), BF16),
        pltpu.VMEM((XS - 1, 8, ZS, 16, LW), BF16),
        pltpu.VMEM((8, ZS, 16, LW), BF16),
        pltpu.VMEM((ZS - 1, 8, 16, LW), BF16),
        pltpu.VMEM((ZS - 1, 8, XS, 16, LW), BF16),
        pltpu.VMEM((8, XS, 16, LW), BF16),
        pltpu.VMEM((XS - 1, 8, 16, LW), BF16),
        dma((7,)),
        dma((12, 3)),
        dma((12, 3)),
        dma((3, PL - 1)),
        dma((3, PL - 1)),
        dma((3,)),
        dma((3,)),
        dma((3, PL - 1)),
        dma((3, PL - 1)),
        dma((6,)),
        dma((6,)),
        dma((6, XS - 1)),
        dma((6, XS - 1)),
        dma((6, ZS - 1)),
        dma((6, ZS - 1)),
    ]
    tokens, gs, gso, gt, gto = pl.pallas_call(
        kernel,
        out_shape=(
            jax.ShapeDtypeStruct((ROWS, D), BF16),
            jax.ShapeDtypeStruct((3, 16, LW), F32),
            jax.ShapeDtypeStruct((16, LW), F32),
            jax.ShapeDtypeStruct((3, 16, LW), F32),
            jax.ShapeDtypeStruct((16, LW), F32),
        ),
        in_specs=[pl.BlockSpec(memory_space=pltpu.HBM)] * 7,
        out_specs=[vmem] * 5,
        scratch_shapes=scratch,
        compiler_params=pltpu.CompilerParams(
            collective_id=0, has_side_effects=True, vmem_limit_bytes=60 * 1024 * 1024
        ),
        cost_estimate=pl.CostEstimate(
            flops=3_500_000_000, bytes_accessed=6_000_000, transcendentals=1_000_000
        ),
    )(
        x.reshape(ROWS, D), g.reshape(ROWS, D), clip_frames.reshape(1, clips), ws, wos, wt, wot,
    )
    results = (tokens, gs, gso, gt, gto)
    tokens, gs, gso, gt, gto = pl.pallas_call(
        deliver,
        out_shape=tuple(jax.ShapeDtypeStruct(r.shape, r.dtype) for r in results),
        in_specs=[vmem] * 5,
        out_specs=[vmem] * 5,
        compiler_params=pltpu.CompilerParams(vmem_limit_bytes=60 * 1024 * 1024),
    )(*results)
    return tokens.reshape(1, ROWS, D), gs, gso.T, gt, gto.T


def solution(mesh):
    placed = (
        P("frames", "mp", None),
        P("frames", "mp", None),
        P(None, None, "mp"),
        P("mp", None),
        P(None, None, "mp"),
        P("mp", None),
        P(),
    )
    return jax.shard_map(
        shards,
        mesh=mesh,
        in_specs=placed,
        out_specs=(
            P("frames", "mp", None),
            P(None, "frames", "mp"),
            P("mp", "frames"),
            P(None, "frames", "mp"),
            P("mp", "frames"),
        ),
        check_vma=False,
    )
```

```python
import jax
import jax.numpy as jnp
from jax import lax
from jax.experimental import pallas as pl
from jax.experimental.pallas import tpu as pltpu
from jax.sharding import PartitionSpec as P

HD = 64
EPS = 1e-06
NEGATIVE = -1e30
FR = 64
MP = 4
XS = 4
ZS = 8
PL = 8
HALO = 3
D = 1024
LW = 256
ROWS = 64
HEADS_LOC = 4
MESH = pl.DeviceIdType.MESH
F32 = jnp.float32
BF16 = jnp.bfloat16


def dot(a, b):
    return lax.dot_general(a, b, (((1,), (0,)), ((), ())), preferred_element_type=F32)


def dot_bt(a, b):
    return lax.dot_general(a, b, (((1,), (1,)), ((), ())), preferred_element_type=F32)


def dot_at(a, b):
    return lax.dot_general(a, b, (((0,), (0,)), ((), ())), preferred_element_type=F32)


def head_mask(h):
    lane = lax.broadcasted_iota(jnp.int32, (1, LW), 1)
    return jnp.where(lane // HD == h, 1.0, 0.0).astype(BF16)


def softmax(scores):
    expo = jnp.exp(scores - jnp.max(scores, -1, keepdims=True))
    return expo / jnp.sum(expo, -1, keepdims=True)


def score_grads(probs, d_probs):
    delta = jnp.sum(probs * d_probs, -1, keepdims=True)
    return (probs * (d_probs - delta) * HD ** (-0.5)).astype(BF16)


def norm_back(values_in, inv_rms, upstream):
    mean = jnp.mean(upstream * values_in, -1, keepdims=True)
    return inv_rms * (upstream - values_in * (inv_rms * inv_rms) * mean)


def kernel(
    x_hbm, g_hbm, cf_hbm, ws_hbm, wos_hbm, wt_hbm, wot_hbm,
    tok_ref, gs_ref, gso_ref, gt_ref, gto_ref,
    x_ref, g_ref, cf_row, ws, wos, wt, wot, xall, gall, nhall, dhall,
    bias, qkvs, probs, x_turned, p_turned, attns, hid, dhid,
    rsend, rrecv, tsend, tbuf, tres, dqkv, dqs,
    gbuf, grecv1, gsum1, grecv2, gsum2, grecv3, hrecv2, hsum2, hrecv3,
    w_sem, mp_send, mp_recv, t_send, t_recv, h_send, h_recv, b_send, b_recv,
    c_send, c_recv, x_send, x_recv, z_send, z_recv,
):
    f = lax.axis_index("frames")
    m = lax.axis_index("mp")
    core = lax.rem(f, 2)
    xpos = lax.rem(f // 2, XS)
    zpos = f // PL
    w = lax.rem(f, PL)

    def remote(src, dst, ssem, rsem, to_f, to_m):
        return pltpu.make_async_remote_copy(
            src_ref=src, dst_ref=dst, send_sem=ssem, recv_sem=rsem,
            device_id=(to_f, to_m), device_id_type=MESH,
        )

    pending = []

    loads = [
        pltpu.make_async_copy(hbm, vmem, w_sem.at[i])
        for i, (hbm, vmem) in enumerate(
            (
                (x_hbm, x_ref), (g_hbm, g_ref), (cf_hbm, cf_row),
                (ws_hbm, ws), (wos_hbm, wos), (wot_hbm, wot), (wt_hbm, wt),
            )
        )
    ]
    for load in loads:
        load.start()

    barrier = pltpu.get_barrier_semaphore()

    for k in range(1, MP):
        pl.semaphore_signal(
            barrier, inc=1, device_id=(f, lax.rem(m + k, MP)), device_id_type=MESH
        )
    for k in range(1, PL):
        pl.semaphore_signal(
            barrier, inc=1, device_id=(zpos * PL + lax.rem(w + k, PL), m), device_id_type=MESH
        )
    for k in range(1, ZS):
        pl.semaphore_signal(
            barrier, inc=1, device_id=(lax.rem(zpos + k, ZS) * PL + w, m), device_id_type=MESH
        )

    def gather_mp(phase, src, buf, rows=slice(0, ROWS)):
        copies = []
        for k in (1, 3, 2):
            copy = remote(
                src.at[rows], buf.at[m, rows], mp_send.at[phase, k - 1], mp_recv.at[phase, k - 1],
                f, lax.rem(m + k, MP),
            )
            copy.start()
            copies.append(copy)
        pending.extend(copies)
        return copies

    def scatter_mp(phase, which, rows=slice(0, ROWS)):
        copies = []
        for k in (1, 3, 2):
            to = lax.rem(m + k, MP)
            copy = remote(
                rsend.at[which, to, rows], rrecv.at[which, k - 1, rows],
                mp_send.at[phase, k - 1], mp_recv.at[phase, k - 1], f, to,
            )
            copy.start()
            copies.append(copy)
        pending.extend(copies)
        return copies

    loads[0].wait()
    x = x_ref[...].astype(F32)
    inv_x = lax.rsqrt(jnp.mean(x * x, -1, keepdims=True) + EPS)
    xall[m] = (x * inv_x).astype(BF16)
    pl.semaphore_wait(barrier, MP - 1 + PL - 1 + ZS - 1)

    ag_x = gather_mp(0, xall.at[m], xall)

    loads[1].wait()
    loads[2].wait()
    gall[m] = g_ref[...]
    row = lax.broadcasted_iota(jnp.int32, (LW, LW), 0)
    col = lax.broadcasted_iota(jnp.int32, (LW, LW), 1)
    clips = cf_row.shape[1]
    c_row = lax.broadcasted_iota(jnp.int32, (clips, clips), 0)
    c_col = lax.broadcasted_iota(jnp.int32, (clips, clips), 1)
    ends_col = jnp.sum(jnp.where(c_col <= c_row, cf_row[...], 0), axis=1, keepdims=True)
    ends_row = jnp.sum(jnp.where(c_row == c_col, ends_col, 0), axis=0, keepdims=True)

    def clip_of(slot, ends, axis):
        frame = lax.rem(zpos * PL + FR - HALO + slot, FR)
        count = jnp.sum(jnp.where(frame >= ends, 1, 0), axis=axis, keepdims=True)
        return count

    slot_lane = lax.broadcasted_iota(jnp.int32, (clips, LW), 1) // 16
    slot_sub = lax.broadcasted_iota(jnp.int32, (LW, clips), 0) // 16
    id_lane = clip_of(slot_lane, ends_col, 0)
    id_sub = clip_of(slot_sub, ends_row, 1)
    used = PL + 2 * HALO
    id_lane = jnp.where(col[:1] // 16 < used, id_lane, -1)
    id_sub = jnp.where(row[:, :1] // 16 < used, id_sub, -1)
    same = jnp.logical_and(id_lane == id_sub, row % 16 == col % 16)
    bias[...] = jnp.where(same, 0.0, NEGATIVE)
    for t in range(4):
        for g in range(2):
            tbuf[t, g, used:] = jnp.zeros((16 - used, 16, LW), BF16)

    halves = [slice(0, ROWS // 2), slice(ROWS // 2, ROWS)]
    masks = [head_mask(h) for h in range(HEADS_LOC)]

    loads[3].wait()
    for copy in ag_x:
        copy.wait_recv()
    near_g = {}
    for k in (1, 3):
        near_g[k] = remote(
            g_ref, gall.at[m], mp_send.at[1, k - 1], mp_recv.at[1, k - 1], f, lax.rem(m + k, MP)
        )
        near_g[k].start()
        pending.append(near_g[k])
    x_all = xall[...].reshape(LW, D)
    for j in range(3):
        qkvs[j] = dot(x_all, ws[j]).astype(BF16)

    total = jnp.zeros((LW, LW), F32)
    for h in range(HEADS_LOC):
        p = softmax(dot_bt(qkvs[0] * masks[h], qkvs[1]) * HD ** (-0.5))
        probs[h] = p
        total = total + dot(p.astype(BF16), qkvs[2] * masks[h])
    attn = total.astype(BF16)
    attns[...] = attn.reshape(MP, ROWS, LW)

    loads[4].wait()
    for c in range(4):
        cols = pl.ds(c * 256, 256)
        rsend[0, :, :, cols] = dot(attn, wos[:, cols]).astype(BF16).reshape(MP, ROWS, 256)
    rs1 = [scatter_mp(p, 0, rows) for p, rows in zip((2, 8), halves)]
    own = dot(attns[m], wos[...])
    for c in range(4):
        x_turned[c] = xall[:, :, c * 256 : (c + 1) * 256].reshape(LW, 256).T
    for h in range(HEADS_LOC):
        p_turned[h] = probs[h].astype(BF16).T
    far_g = []
    for k, rows in zip((1, 3), halves):
        near_g[k].wait_recv()
        chunk = gall.at[lax.rem(m + MP - k, MP), rows]
        copy = remote(
            chunk, chunk, mp_send.at[7, k - 1], mp_recv.at[7, k - 1], f, lax.rem(m + k, MP)
        )
        copy.start()
        far_g.append(copy)
    pending.extend(far_g)

    ag_h = []
    for at, rows in enumerate(halves):
        for copy in rs1[at]:
            copy.wait_recv()
        hidden = x_ref[rows].astype(F32) + own[rows]
        for k in range(3):
            hidden = hidden + rrecv[0, k, rows].astype(F32)
        inv_h = lax.rsqrt(jnp.mean(hidden * hidden, -1, keepdims=True) + EPS)
        hid[rows] = hidden
        nhall[m, rows] = (hidden * inv_h).astype(BF16)
        ag_h += gather_mp((3, 9)[at], nhall.at[m], nhall, rows)

    def plane_send(part, source, target, ssems, rsems):
        copies = []
        for k in range(1, PL):
            to = lax.rem(w + k, PL)
            copy = remote(
                source(to), target, ssems.at[part, k - 1], rsems.at[part, k - 1],
                zpos * PL + to, m,
            )
            copy.start()
            copies.append(copy)
        pending.extend(copies)
        return copies

    def halo_view(part, slots):
        return tbuf.at[3, :, slots] if part == 2 else tbuf.at[:3, part, slots]

    def hand_on(part, frame):
        def to_plane(step, slot):
            return remote(
                halo_view(part, HALO + frame), halo_view(part, slot),
                h_send.at[part], h_recv.at[part], lax.rem(zpos + step, ZS) * PL + w, m,
            )

        @pl.when(frame < HALO)
        def _():
            to_plane(ZS - 1, HALO + PL + frame).start()

        @pl.when(frame >= PL - HALO)
        def _():
            to_plane(1, frame - (PL - HALO)).start()

    def hand_wait(part):
        some = halo_view(part, pl.ds(0, 2 * HALO))
        return remote(some, some, h_send.at[part], h_recv.at[part], f, m)

    def receive(part, copies):
        hand_on(part, w)
        for k in range(1, PL):
            copies[k - 1].wait_recv()
            hand_on(part, lax.rem(w + PL - k, PL))

    loads[5].wait()
    for copy in far_g:
        copy.wait_recv()
    tsend[3] = dot_bt(gall[...].reshape(LW, D), wot[...]).astype(BF16).reshape(2, PL, 16, LW)
    there_up = plane_send(
        2, lambda to: tsend.at[3, :, to], halo_view(2, HALO + w), t_send, t_recv
    )
    for g in range(2):
        tbuf[3, g, HALO + w] = tsend[3, g, w]
    receive(2, there_up)
    loads[6].wait()
    for copy in ag_h:
        copy.wait_recv()
    h_all = nhall[...].reshape(LW, D)
    for j in range(3):
        tsend[j] = dot(h_all, wt[j]).astype(BF16).reshape(2, PL, 16, LW)

    there = [
        plane_send(g, lambda to, g=g: tsend.at[:3, g, to], halo_view(g, HALO + w), t_send, t_recv)
        for g in range(2)
    ]
    for t in range(3):
        for g in range(2):
            tbuf[t, g, HALO + w] = tsend[t, g, w]

    for g in range(2):
        receive(g, there[g])

    zero = jnp.zeros((LW, LW), F32)
    own_slots = slice(HALO, HALO + PL)
    back = []
    for g in range(2):
        hand_wait(g).wait_recv()
        if g == 0:
            hand_wait(2).wait_recv()
        queries, keys, values, upstream = [tbuf[t, g].reshape(LW, LW) for t in range(4)]
        attn_t, d_q, d_k, d_v = zero, zero, zero, zero
        for h in range(HEADS_LOC):
            qm = queries * masks[h]
            om = upstream * masks[h]
            p = softmax(dot_bt(qm, keys) * HD ** (-0.5) + bias[...])
            pb = p.astype(BF16)
            attn_t = attn_t + dot(pb, values * masks[h])
            d_v = d_v + dot_at(pb, om)
            ds = score_grads(p, dot_bt(om, values))
            d_q = d_q + dot(ds, keys * masks[h])
            d_k = d_k + dot_at(ds, qm)
        for t, full in enumerate((d_q, d_k, d_v, attn_t)):
            tres[t, g] = full.astype(BF16).reshape(16, 16, LW)[own_slots]
        back += plane_send(
            g, lambda to, g=g: tres.at[:3, g, to], dqkv.at[:3, g, w], b_send, b_recv
        )
        for t in range(4):
            dqkv[t, g, w] = tres[t, g, w]
    back_attn = plane_send(2, lambda to: tres.at[3, :, to], dqkv.at[3, :, w], b_send, b_recv)
    for copy in back:
        copy.wait_recv()

    def project_back(which, grads, weights):
        for c in range(4):
            cols = pl.ds(c * 256, 256)
            part = dot_bt(grads[0], weights[0, cols])
            part = part + dot_bt(grads[1], weights[1, cols])
            part = part + dot_bt(grads[2], weights[2, cols])
            rsend[which, :, :, cols] = part.astype(BF16).reshape(MP, ROWS, 256)

    def own_back(grads, weights):
        part = dot_bt(grads[0], weights[0])
        part = part + dot_bt(grads[1], weights[1])
        return part + dot_bt(grads[2], weights[2])

    def weight_grad(j, left_ref, right):
        for c in range(4):
            left = left_ref[:, :, c * 256 : (c + 1) * 256].reshape(LW, 256)
            gbuf[j, 8 * c : 8 * c + 8] = dot_at(left, right).astype(BF16).reshape(8, 2, 16, LW)

    def weight_grad_x(j, right):
        for c in range(4):
            part = dot(x_turned[c], right)
            gbuf[j, 8 * c : 8 * c + 8] = part.astype(BF16).reshape(8, 2, 16, LW)

    first = [0, 2, 4, 5, 6, 7]
    count = [2, 2, 1, 1, 1, 1]

    def core_send(b):
        some = slice(first[b], first[b] + count[b])
        copy = remote(
            gbuf.at[some, :, 1 - core], grecv1.at[some],
            c_send.at[b], c_recv.at[b], f + 1 - 2 * core, m,
        )
        copy.start()
        pending.append(copy)
        return copy

    def send_x(b, source, target):
        copies = []
        for k in (1, 3, 2):
            to = lax.rem(xpos + k, XS)
            copy = remote(
                source(to), target(k - 1), x_send.at[b, k - 1], x_recv.at[b, k - 1],
                (zpos * XS + to) * 2 + core, m,
            )
            copy.start()
            copies.append(copy)
        pending.extend(copies)
        return copies

    def send_z(b, source, target):
        copies = []
        for k in (4, 3, 5, 2, 6, 1, 7):
            to = lax.rem(zpos + k, ZS)
            copy = remote(
                source(to), target(k - 1), z_send.at[b, k - 1], z_recv.at[b, k - 1],
                (to * XS + xpos) * 2 + core, m,
            )
            copy.start()
            copies.append(copy)
        pending.extend(copies)
        return copies

    def mats(b):
        return slice(first[b], first[b] + count[b])

    def wait_all(copies):
        for copy in copies:
            copy.wait_recv()

    def core_sum(b, copy):
        copy.wait_recv()
        for j in range(first[b], first[b] + count[b]):
            summed = gbuf[j, :, core].astype(F32) + grecv1[j].astype(F32)
            gsum1[j] = summed.astype(BF16).reshape(ZS, XS, 16, LW)

    def core_sum_x_send(b, copy):
        core_sum(b, copy)
        return send_x(b, lambda to: gsum1.at[mats(b), :, to], lambda k: grecv2.at[k, mats(b)])

    def core_sum_z_send(b, copy):
        core_sum(b, copy)
        return send_z(b, lambda to: gsum1.at[mats(b), to], lambda k: hrecv2.at[k, mats(b)])

    def x_sum_z_send(b, copies):
        wait_all(copies)
        for j in range(first[b], first[b] + count[b]):
            summed = gsum1[j, :, xpos].astype(F32)
            for k in range(XS - 1):
                summed = summed + grecv2[k, j].astype(F32)
            gsum2[j] = summed.astype(BF16)
        return send_z(b, lambda to: gsum2.at[mats(b), to], lambda k: grecv3.at[k, mats(b)])

    def z_sum_x_send(b, copies):
        wait_all(copies)
        for j in range(first[b], first[b] + count[b]):
            summed = gsum1[j, zpos].astype(F32)
            for k in range(ZS - 1):
                summed = summed + hrecv2[k, j].astype(F32)
            hsum2[j] = summed.astype(BF16)
        return send_x(b, lambda to: hsum2.at[mats(b), to], lambda k: hrecv3.at[k, mats(b)])

    def z_sum(b, copies, outs):
        wait_all(copies)
        for at, out in enumerate(outs):
            j = first[b] + at
            summed = gsum2[j, zpos].astype(F32)
            for k in range(ZS - 1):
                summed = summed + grecv3[k, j].astype(F32)
            out[...] = summed

    def x_sum(b, copies, outs):
        wait_all(copies)
        for at, out in enumerate(outs):
            j = first[b] + at
            summed = hsum2[j, xpos].astype(F32)
            for k in range(XS - 1):
                summed = summed + hrecv3[k, j].astype(F32)
            out[...] = summed

    grads_t = [dqkv[j].reshape(LW, LW) for j in range(3)]
    project_back(1, grads_t, wt)
    rs2 = [scatter_mp(p, 1, rows) for p, rows in zip((4, 10), halves)]
    for j in range(2):
        weight_grad(j, nhall, grads_t[j])
    core_t1 = core_send(0)
    weight_grad(2, nhall, grads_t[2])
    wait_all(back_attn)
    weight_grad(3, gall, dqkv[3].reshape(LW, LW))
    core_t2 = core_send(1)
    quarter = pl.ds(4 * lax.rem(m, 2), 4)
    own = own_back([dqkv[j, m // 2, quarter].reshape(ROWS, LW) for j in range(3)], wt)
    x_t1 = core_sum_x_send(0, core_t1)
    z_t2 = core_sum_z_send(1, core_t2)
    ag_d = []
    for at, rows in enumerate(halves):
        wait_all(rs2[at])
        d_nh = own[rows]
        for k in range(3):
            d_nh = d_nh + rrecv[1, k, rows].astype(F32)
        hidden = hid[rows]
        inv_h = lax.rsqrt(jnp.mean(hidden * hidden, -1, keepdims=True) + EPS)
        d_hidden = g_ref[rows].astype(F32) + norm_back(hidden, inv_h, d_nh)
        dhid[rows] = d_hidden
        dhall[m, rows] = d_hidden.astype(BF16)
        ag_d += gather_mp((5, 11)[at], dhall.at[m], dhall, rows)
    z_t1 = x_sum_z_send(0, x_t1)
    wait_all(ag_d)

    weight_grad(7, dhall, attns[...].reshape(LW, LW))
    core_o = core_send(5)
    das = dot_bt(dhall[...].reshape(LW, D), wos[...]).astype(BF16)

    def keep(j, grad):
        dqs[j] = grad.astype(BF16).reshape(MP, ROWS, LW)
        weight_grad_x(4 + j, dqs[j].reshape(LW, LW))
        return core_send(2 + j)

    d_v = zero
    for h in range(HEADS_LOC):
        d_v = d_v + dot(p_turned[h], das * masks[h])
    core_v = keep(2, d_v)
    x_o = core_sum_x_send(5, core_o)
    d_q, d_k = zero, zero
    for h in range(HEADS_LOC):
        ds = score_grads(probs[h], dot_bt(das * masks[h], qkvs[2]))
        d_q = d_q + dot(ds, qkvs[1] * masks[h])
        d_k = d_k + dot_at(ds, qkvs[0] * masks[h])
    z_v = core_sum_z_send(4, core_v)
    core_q = keep(0, d_q)
    core_k = keep(1, d_k)
    x_q = core_sum_x_send(2, core_q)
    x_k = core_sum_x_send(3, core_k)
    project_back(2, [dqs[j].reshape(LW, LW) for j in range(3)], ws)
    rs3 = scatter_mp(6, 2)
    x_t2 = z_sum_x_send(1, z_t2)
    z_o = x_sum_z_send(5, x_o)
    z_sum(0, z_t1, [gt_ref.at[0], gt_ref.at[1]])
    d_nx = own_back([dqs[j, m] for j in range(3)], ws)
    z_q = x_sum_z_send(2, x_q)
    x_sum(1, x_t2, [gt_ref.at[2], gto_ref])
    z_k = x_sum_z_send(3, x_k)
    x_v = z_sum_x_send(4, z_v)
    wait_all(rs3)
    for k in range(3):
        d_nx = d_nx + rrecv[2, k].astype(F32)
    x = x_ref[...].astype(F32)
    inv_x = lax.rsqrt(jnp.mean(x * x, -1, keepdims=True) + EPS)
    tok_ref[...] = (dhid[...] + norm_back(x, inv_x, d_nx)).astype(BF16)
    z_sum(5, z_o, [gso_ref])
    x_sum(4, x_v, [gs_ref.at[2]])
    z_sum(2, z_q, [gs_ref.at[0]])
    z_sum(3, z_k, [gs_ref.at[1]])
    for copy in pending:
        copy.wait_send()
    for part in range(3):
        hand_wait(part).wait_send()


def deliver(*refs):
    for source, target in zip(refs[:5], refs[5:]):
        target[...] = source[...]


def shards(x, g, ws, wos, wt, wot, clip_frames):
    clips = clip_frames.shape[0]
    vmem = pl.BlockSpec(memory_space=pltpu.VMEM)
    dma = pltpu.SemaphoreType.DMA
    scratch = [
        pltpu.VMEM((ROWS, D), BF16),
        pltpu.VMEM((ROWS, D), BF16),
        pltpu.VMEM((1, clips), jnp.int32),
        pltpu.VMEM((3, D, LW), BF16),
        pltpu.VMEM((LW, D), BF16),
        pltpu.VMEM((3, D, LW), BF16),
        pltpu.VMEM((LW, D), BF16),
        pltpu.VMEM((MP, ROWS, D), BF16),
        pltpu.VMEM((MP, ROWS, D), BF16),
        pltpu.VMEM((MP, ROWS, D), BF16),
        pltpu.VMEM((MP, ROWS, D), BF16),
        pltpu.VMEM((LW, LW), F32),
        pltpu.VMEM((3, LW, LW), BF16),
        pltpu.VMEM((HEADS_LOC, LW, LW), F32),
        pltpu.VMEM((4, LW, LW), BF16),
        pltpu.VMEM((HEADS_LOC, LW, LW), BF16),
        pltpu.VMEM((MP, ROWS, LW), BF16),
        pltpu.VMEM((ROWS, D), F32),
        pltpu.VMEM((ROWS, D), F32),
        pltpu.VMEM((3, MP, ROWS, D), BF16),
        pltpu.VMEM((3, MP - 1, ROWS, D), BF16),
        pltpu.VMEM((4, 2, PL, 16, LW), BF16),
        pltpu.VMEM((4, 2, 16, 16, LW), BF16),
        pltpu.VMEM((4, 2, PL, 16, LW), BF16),
        pltpu.VMEM((4, 2, PL, 16, LW), BF16),
        pltpu.VMEM((3, MP, ROWS, LW), BF16),
        pltpu.VMEM((8, FR // 2, 2, 16, LW), BF16),
        pltpu.VMEM((8, FR // 2, 16, LW), BF16),
        pltpu.VMEM((8, ZS, XS, 16, LW), BF16),
        pltpu.VMEM((XS - 1, 8, ZS, 16, LW), BF16),
        pltpu.VMEM((8, ZS, 16, LW), BF16),
        pltpu.VMEM((ZS - 1, 8, 16, LW), BF16),
        pltpu.VMEM((ZS - 1, 8, XS, 16, LW), BF16),
        pltpu.VMEM((8, XS, 16, LW), BF16),
        pltpu.VMEM((XS - 1, 8, 16, LW), BF16),
        dma((7,)),
        dma((12, 3)),
        dma((12, 3)),
        dma((3, PL - 1)),
        dma((3, PL - 1)),
        dma((3,)),
        dma((3,)),
        dma((3, PL - 1)),
        dma((3, PL - 1)),
        dma((6,)),
        dma((6,)),
        dma((6, XS - 1)),
        dma((6, XS - 1)),
        dma((6, ZS - 1)),
        dma((6, ZS - 1)),
    ]
    tokens, gs, gso, gt, gto = pl.pallas_call(
        kernel,
        out_shape=(
            jax.ShapeDtypeStruct((ROWS, D), BF16),
            jax.ShapeDtypeStruct((3, 16, LW), F32),
            jax.ShapeDtypeStruct((16, LW), F32),
            jax.ShapeDtypeStruct((3, 16, LW), F32),
            jax.ShapeDtypeStruct((16, LW), F32),
        ),
        in_specs=[pl.BlockSpec(memory_space=pltpu.HBM)] * 7,
        out_specs=[vmem] * 5,
        scratch_shapes=scratch,
        compiler_params=pltpu.CompilerParams(
            collective_id=0, has_side_effects=True, vmem_limit_bytes=60 * 1024 * 1024
        ),
        cost_estimate=pl.CostEstimate(
            flops=3_500_000_000, bytes_accessed=6_000_000, transcendentals=1_000_000
        ),
    )(
        x.reshape(ROWS, D), g.reshape(ROWS, D), clip_frames.reshape(1, clips), ws, wos, wt, wot,
    )
    results = (tokens, gs, gso, gt, gto)
    tokens, gs, gso, gt, gto = pl.pallas_call(
        deliver,
        out_shape=tuple(jax.ShapeDtypeStruct(r.shape, r.dtype) for r in results),
        in_specs=[vmem] * 5,
        out_specs=[vmem] * 5,
        compiler_params=pltpu.CompilerParams(vmem_limit_bytes=60 * 1024 * 1024),
    )(*results)
    return tokens.reshape(1, ROWS, D), gs, gso.T, gt, gto.T


def solution(mesh):
    placed = (
        P("frames", "mp", None),
        P("frames", "mp", None),
        P(None, None, "mp"),
        P("mp", None),
        P(None, None, "mp"),
        P("mp", None),
        P(),
    )
    return jax.shard_map(
        shards,
        mesh=mesh,
        in_specs=placed,
        out_specs=(
            P("frames", "mp", None),
            P(None, "frames", "mp"),
            P("mp", "frames"),
            P(None, "frames", "mp"),
            P("mp", "frames"),
        ),
        check_vma=False,
    )
```

```python
import jax
import jax.numpy as jnp
from jax import lax
from jax.experimental import pallas as pl
from jax.experimental.pallas import tpu as pltpu
from jax.sharding import PartitionSpec as P

HD = 64
EPS = 1e-06
NEGATIVE = -1e30
FR = 64
MP = 4
XS = 4
ZS = 8
PL = 8
HALO = 3
D = 1024
LW = 256
ROWS = 64
HEADS_LOC = 4
MESH = pl.DeviceIdType.MESH
F32 = jnp.float32
BF16 = jnp.bfloat16


def dot(a, b):
    return lax.dot_general(a, b, (((1,), (0,)), ((), ())), preferred_element_type=F32)


def dot_bt(a, b):
    return lax.dot_general(a, b, (((1,), (1,)), ((), ())), preferred_element_type=F32)


def dot_at(a, b):
    return lax.dot_general(a, b, (((0,), (0,)), ((), ())), preferred_element_type=F32)


def head_mask(h):
    lane = lax.broadcasted_iota(jnp.int32, (1, LW), 1)
    return jnp.where(lane // HD == h, 1.0, 0.0).astype(BF16)


def softmax(scores):
    expo = jnp.exp(scores - jnp.max(scores, -1, keepdims=True))
    return expo / jnp.sum(expo, -1, keepdims=True)


def score_grads(probs, d_probs):
    delta = jnp.sum(probs * d_probs, -1, keepdims=True)
    return (probs * (d_probs - delta) * HD ** (-0.5)).astype(BF16)


def norm_back(values_in, inv_rms, upstream):
    mean = jnp.mean(upstream * values_in, -1, keepdims=True)
    return inv_rms * (upstream - values_in * (inv_rms * inv_rms) * mean)


def kernel(
    x_hbm, g_hbm, cf_hbm, ws_hbm, wos_hbm, wt_hbm, wot_hbm,
    tok_out, gs_out, gso_out, gt_out, gto_out,
    tok_ref, gs_ref, gso_ref, gt_ref, gto_ref, out_sem,
    x_ref, g_ref, cf_row, ws, wos, wt, wot, xall, gall, nhall, dhall,
    bias, qkvs, probs, x_turned, p_turned, attns, hid, dhid,
    rsend, rrecv, tsend, tbuf, tres, dqkv, dqs,
    gbuf, grecv1, gsum1, grecv2, gsum2, grecv3, hrecv2, hsum2, hrecv3,
    w_sem, mp_send, mp_recv, t_send, t_recv, h_send, h_recv, b_send, b_recv,
    c_send, c_recv, x_send, x_recv, z_send, z_recv,
):
    f = lax.axis_index("frames")
    m = lax.axis_index("mp")
    core = lax.rem(f, 2)
    xpos = lax.rem(f // 2, XS)
    zpos = f // PL
    w = lax.rem(f, PL)

    def remote(src, dst, ssem, rsem, to_f, to_m):
        return pltpu.make_async_remote_copy(
            src_ref=src, dst_ref=dst, send_sem=ssem, recv_sem=rsem,
            device_id=(to_f, to_m), device_id_type=MESH,
        )

    pending = []

    loads = [
        pltpu.make_async_copy(hbm, vmem, w_sem.at[i])
        for i, (hbm, vmem) in enumerate(
            (
                (x_hbm, x_ref), (g_hbm, g_ref), (cf_hbm, cf_row),
                (ws_hbm, ws), (wos_hbm, wos), (wot_hbm, wot), (wt_hbm, wt),
            )
        )
    ]
    for load in loads:
        load.start()

    barrier = pltpu.get_barrier_semaphore()

    for k in range(1, MP):
        pl.semaphore_signal(
            barrier, inc=1, device_id=(f, lax.rem(m + k, MP)), device_id_type=MESH
        )
    for k in range(1, PL):
        pl.semaphore_signal(
            barrier, inc=1, device_id=(zpos * PL + lax.rem(w + k, PL), m), device_id_type=MESH
        )
    for k in range(1, ZS):
        pl.semaphore_signal(
            barrier, inc=1, device_id=(lax.rem(zpos + k, ZS) * PL + w, m), device_id_type=MESH
        )

    def gather_mp(phase, src, buf, rows=slice(0, ROWS)):
        copies = []
        for k in (1, 3, 2):
            copy = remote(
                src.at[rows], buf.at[m, rows], mp_send.at[phase, k - 1], mp_recv.at[phase, k - 1],
                f, lax.rem(m + k, MP),
            )
            copy.start()
            copies.append(copy)
        pending.extend(copies)
        return copies

    def scatter_mp(phase, which, rows=slice(0, ROWS)):
        copies = []
        for k in (1, 3, 2):
            to = lax.rem(m + k, MP)
            copy = remote(
                rsend.at[which, to, rows], rrecv.at[which, k - 1, rows],
                mp_send.at[phase, k - 1], mp_recv.at[phase, k - 1], f, to,
            )
            copy.start()
            copies.append(copy)
        pending.extend(copies)
        return copies

    loads[0].wait()
    x = x_ref[...].astype(F32)
    inv_x = lax.rsqrt(jnp.mean(x * x, -1, keepdims=True) + EPS)
    xall[m] = (x * inv_x).astype(BF16)
    pl.semaphore_wait(barrier, MP - 1 + PL - 1 + ZS - 1)

    ag_x = gather_mp(0, xall.at[m], xall)

    loads[1].wait()
    loads[2].wait()
    gall[m] = g_ref[...]
    row = lax.broadcasted_iota(jnp.int32, (LW, LW), 0)
    col = lax.broadcasted_iota(jnp.int32, (LW, LW), 1)
    clips = cf_row.shape[1]
    c_row = lax.broadcasted_iota(jnp.int32, (clips, clips), 0)
    c_col = lax.broadcasted_iota(jnp.int32, (clips, clips), 1)
    ends_col = jnp.sum(jnp.where(c_col <= c_row, cf_row[...], 0), axis=1, keepdims=True)
    ends_row = jnp.sum(jnp.where(c_row == c_col, ends_col, 0), axis=0, keepdims=True)

    def clip_of(slot, ends, axis):
        frame = lax.rem(zpos * PL + FR - HALO + slot, FR)
        count = jnp.sum(jnp.where(frame >= ends, 1, 0), axis=axis, keepdims=True)
        return count

    slot_lane = lax.broadcasted_iota(jnp.int32, (clips, LW), 1) // 16
    slot_sub = lax.broadcasted_iota(jnp.int32, (LW, clips), 0) // 16
    id_lane = clip_of(slot_lane, ends_col, 0)
    id_sub = clip_of(slot_sub, ends_row, 1)
    used = PL + 2 * HALO
    id_lane = jnp.where(col[:1] // 16 < used, id_lane, -1)
    id_sub = jnp.where(row[:, :1] // 16 < used, id_sub, -1)
    same = jnp.logical_and(id_lane == id_sub, row % 16 == col % 16)
    bias[...] = jnp.where(same, 0.0, NEGATIVE)
    for t in range(4):
        for g in range(2):
            tbuf[t, g, used:] = jnp.zeros((16 - used, 16, LW), BF16)

    halves = [slice(0, ROWS // 2), slice(ROWS // 2, ROWS)]
    masks = [head_mask(h) for h in range(HEADS_LOC)]

    loads[3].wait()
    for copy in ag_x:
        copy.wait_recv()
    near_g = {}
    for k in (1, 3):
        near_g[k] = remote(
            g_ref, gall.at[m], mp_send.at[1, k - 1], mp_recv.at[1, k - 1], f, lax.rem(m + k, MP)
        )
        near_g[k].start()
        pending.append(near_g[k])
    x_all = xall[...].reshape(LW, D)
    for j in range(3):
        qkvs[j] = dot(x_all, ws[j]).astype(BF16)

    total = jnp.zeros((LW, LW), F32)
    for h in range(HEADS_LOC):
        p = softmax(dot_bt(qkvs[0] * masks[h], qkvs[1]) * HD ** (-0.5))
        probs[h] = p
        total = total + dot(p.astype(BF16), qkvs[2] * masks[h])
    attn = total.astype(BF16)
    attns[...] = attn.reshape(MP, ROWS, LW)

    loads[4].wait()
    for c in range(4):
        cols = pl.ds(c * 256, 256)
        rsend[0, :, :, cols] = dot(attn, wos[:, cols]).astype(BF16).reshape(MP, ROWS, 256)
    rs1 = [scatter_mp(p, 0, rows) for p, rows in zip((2, 8), halves)]
    own = dot(attns[m], wos[...])
    for c in range(4):
        x_turned[c] = xall[:, :, c * 256 : (c + 1) * 256].reshape(LW, 256).T
    for h in range(HEADS_LOC):
        p_turned[h] = probs[h].astype(BF16).T
    far_g = []
    for k, rows in zip((1, 3), halves):
        near_g[k].wait_recv()
        chunk = gall.at[lax.rem(m + MP - k, MP), rows]
        copy = remote(
            chunk, chunk, mp_send.at[7, k - 1], mp_recv.at[7, k - 1], f, lax.rem(m + k, MP)
        )
        copy.start()
        far_g.append(copy)
    pending.extend(far_g)

    ag_h = []
    for at, rows in enumerate(halves):
        for copy in rs1[at]:
            copy.wait_recv()
        hidden = x_ref[rows].astype(F32) + own[rows]
        for k in range(3):
            hidden = hidden + rrecv[0, k, rows].astype(F32)
        inv_h = lax.rsqrt(jnp.mean(hidden * hidden, -1, keepdims=True) + EPS)
        hid[rows] = hidden
        nhall[m, rows] = (hidden * inv_h).astype(BF16)
        ag_h += gather_mp((3, 9)[at], nhall.at[m], nhall, rows)

    def plane_send(part, source, target, ssems, rsems):
        copies = []
        for k in range(1, PL):
            to = lax.rem(w + k, PL)
            copy = remote(
                source(to), target, ssems.at[part, k - 1], rsems.at[part, k - 1],
                zpos * PL + to, m,
            )
            copy.start()
            copies.append(copy)
        pending.extend(copies)
        return copies

    def halo_view(part, slots):
        return tbuf.at[3, :, slots] if part == 2 else tbuf.at[:3, part, slots]

    def hand_on(part, frame):
        def to_plane(step, slot):
            return remote(
                halo_view(part, HALO + frame), halo_view(part, slot),
                h_send.at[part], h_recv.at[part], lax.rem(zpos + step, ZS) * PL + w, m,
            )

        @pl.when(frame < HALO)
        def _():
            to_plane(ZS - 1, HALO + PL + frame).start()

        @pl.when(frame >= PL - HALO)
        def _():
            to_plane(1, frame - (PL - HALO)).start()

    def hand_wait(part):
        some = halo_view(part, pl.ds(0, 2 * HALO))
        return remote(some, some, h_send.at[part], h_recv.at[part], f, m)

    def receive(part, copies):
        hand_on(part, w)
        for k in range(1, PL):
            copies[k - 1].wait_recv()
            hand_on(part, lax.rem(w + PL - k, PL))

    loads[5].wait()
    for copy in far_g:
        copy.wait_recv()
    tsend[3] = dot_bt(gall[...].reshape(LW, D), wot[...]).astype(BF16).reshape(2, PL, 16, LW)
    there_up = plane_send(
        2, lambda to: tsend.at[3, :, to], halo_view(2, HALO + w), t_send, t_recv
    )
    for g in range(2):
        tbuf[3, g, HALO + w] = tsend[3, g, w]
    receive(2, there_up)
    loads[6].wait()
    for copy in ag_h:
        copy.wait_recv()
    h_all = nhall[...].reshape(LW, D)
    for j in range(3):
        tsend[j] = dot(h_all, wt[j]).astype(BF16).reshape(2, PL, 16, LW)

    there = [
        plane_send(g, lambda to, g=g: tsend.at[:3, g, to], halo_view(g, HALO + w), t_send, t_recv)
        for g in range(2)
    ]
    for t in range(3):
        for g in range(2):
            tbuf[t, g, HALO + w] = tsend[t, g, w]

    for g in range(2):
        receive(g, there[g])

    zero = jnp.zeros((LW, LW), F32)
    own_slots = slice(HALO, HALO + PL)
    back = []
    for g in range(2):
        hand_wait(g).wait_recv()
        if g == 0:
            hand_wait(2).wait_recv()
        queries, keys, values, upstream = [tbuf[t, g].reshape(LW, LW) for t in range(4)]
        attn_t, d_q, d_k, d_v = zero, zero, zero, zero
        for h in range(HEADS_LOC):
            qm = queries * masks[h]
            om = upstream * masks[h]
            p = softmax(dot_bt(qm, keys) * HD ** (-0.5) + bias[...])
            pb = p.astype(BF16)
            attn_t = attn_t + dot(pb, values * masks[h])
            d_v = d_v + dot_at(pb, om)
            ds = score_grads(p, dot_bt(om, values))
            d_q = d_q + dot(ds, keys * masks[h])
            d_k = d_k + dot_at(ds, qm)
        for t, full in enumerate((d_q, d_k, d_v, attn_t)):
            tres[t, g] = full.astype(BF16).reshape(16, 16, LW)[own_slots]
        back += plane_send(
            g, lambda to, g=g: tres.at[:3, g, to], dqkv.at[:3, g, w], b_send, b_recv
        )
        for t in range(4):
            dqkv[t, g, w] = tres[t, g, w]
    back_attn = plane_send(2, lambda to: tres.at[3, :, to], dqkv.at[3, :, w], b_send, b_recv)

    def project_back(which, grads, weights):
        for c in range(4):
            cols = pl.ds(c * 256, 256)
            part = dot_bt(grads[0], weights[0, cols])
            part = part + dot_bt(grads[1], weights[1, cols])
            part = part + dot_bt(grads[2], weights[2, cols])
            rsend[which, :, :, cols] = part.astype(BF16).reshape(MP, ROWS, 256)

    def own_back(grads, weights):
        part = dot_bt(grads[0], weights[0])
        part = part + dot_bt(grads[1], weights[1])
        return part + dot_bt(grads[2], weights[2])

    def weight_grad(j, left_ref, right):
        for c in range(4):
            left = left_ref[:, :, c * 256 : (c + 1) * 256].reshape(LW, 256)
            gbuf[j, 8 * c : 8 * c + 8] = dot_at(left, right).astype(BF16).reshape(8, 2, 16, LW)

    def weight_grad_x(j, right):
        for c in range(4):
            part = dot(x_turned[c], right)
            gbuf[j, 8 * c : 8 * c + 8] = part.astype(BF16).reshape(8, 2, 16, LW)

    first = [0, 2, 4, 5, 6, 7]
    count = [2, 2, 1, 1, 1, 1]

    def core_send(b):
        some = slice(first[b], first[b] + count[b])
        copy = remote(
            gbuf.at[some, :, 1 - core], grecv1.at[some],
            c_send.at[b], c_recv.at[b], f + 1 - 2 * core, m,
        )
        copy.start()
        pending.append(copy)
        return copy

    def send_x(b, source, target):
        copies = []
        for k in (1, 3, 2):
            to = lax.rem(xpos + k, XS)
            copy = remote(
                source(to), target(k - 1), x_send.at[b, k - 1], x_recv.at[b, k - 1],
                (zpos * XS + to) * 2 + core, m,
            )
            copy.start()
            copies.append(copy)
        pending.extend(copies)
        return copies

    def send_z(b, source, target):
        copies = []
        for k in (4, 3, 5, 2, 6, 1, 7):
            to = lax.rem(zpos + k, ZS)
            copy = remote(
                source(to), target(k - 1), z_send.at[b, k - 1], z_recv.at[b, k - 1],
                (to * XS + xpos) * 2 + core, m,
            )
            copy.start()
            copies.append(copy)
        pending.extend(copies)
        return copies

    def mats(b):
        return slice(first[b], first[b] + count[b])

    def wait_all(copies):
        for copy in copies:
            copy.wait_recv()

    def core_sum(b, copy):
        copy.wait_recv()
        for j in range(first[b], first[b] + count[b]):
            summed = gbuf[j, :, core].astype(F32) + grecv1[j].astype(F32)
            gsum1[j] = summed.astype(BF16).reshape(ZS, XS, 16, LW)

    def core_sum_x_send(b, copy):
        core_sum(b, copy)
        return send_x(b, lambda to: gsum1.at[mats(b), :, to], lambda k: grecv2.at[k, mats(b)])

    def core_sum_z_send(b, copy):
        core_sum(b, copy)
        return send_z(b, lambda to: gsum1.at[mats(b), to], lambda k: hrecv2.at[k, mats(b)])

    def x_sum_z_send(b, copies):
        wait_all(copies)
        for j in range(first[b], first[b] + count[b]):
            summed = gsum1[j, :, xpos].astype(F32)
            for k in range(XS - 1):
                summed = summed + grecv2[k, j].astype(F32)
            gsum2[j] = summed.astype(BF16)
        return send_z(b, lambda to: gsum2.at[mats(b), to], lambda k: grecv3.at[k, mats(b)])

    def z_sum_x_send(b, copies):
        wait_all(copies)
        for j in range(first[b], first[b] + count[b]):
            summed = gsum1[j, zpos].astype(F32)
            for k in range(ZS - 1):
                summed = summed + hrecv2[k, j].astype(F32)
            hsum2[j] = summed.astype(BF16)
        return send_x(b, lambda to: hsum2.at[mats(b), to], lambda k: hrecv3.at[k, mats(b)])

    def z_sum(b, copies, outs):
        wait_all(copies)
        for at, out in enumerate(outs):
            j = first[b] + at
            summed = gsum2[j, zpos].astype(F32)
            for k in range(ZS - 1):
                summed = summed + grecv3[k, j].astype(F32)
            out[...] = summed

    def x_sum(b, copies, outs):
        wait_all(copies)
        for at, out in enumerate(outs):
            j = first[b] + at
            summed = hsum2[j, xpos].astype(F32)
            for k in range(XS - 1):
                summed = summed + hrecv3[k, j].astype(F32)
            out[...] = summed

    rs2 = []
    for phase, rows in zip((4, 10), halves):
        copies = []
        for k in (1, 3, 2):
            to = lax.rem(m + k, MP)
            copies.append(remote(
                rsend.at[1, to, rows], rrecv.at[1, k - 1, rows],
                mp_send.at[phase, k - 1], mp_recv.at[phase, k - 1], f, to,
            ))
        rs2.append(copies)
        pending.extend(copies)
    for g in range(2):
        wait_all(back[g * (PL - 1) : (g + 1) * (PL - 1)])
        grads = [dqkv[j, g].reshape(LW // 2, LW) for j in range(3)]
        for c in range(4):
            cols = pl.ds(c * 256, 256)
            part = dot_bt(grads[0], wt[0, cols])
            part = part + dot_bt(grads[1], wt[1, cols])
            part = part + dot_bt(grads[2], wt[2, cols])
            rsend[1, 2 * g : 2 * g + 2, :, cols] = part.astype(BF16).reshape(2, ROWS, 256)
        for copies in rs2:
            for k, copy in zip((1, 3, 2), copies):

                @pl.when(lax.rem(m + k, MP) // 2 == g)
                def _():
                    copy.start()

    grads_t = [dqkv[j].reshape(LW, LW) for j in range(3)]
    for j in range(2):
        weight_grad(j, nhall, grads_t[j])
    core_t1 = core_send(0)
    weight_grad(2, nhall, grads_t[2])
    wait_all(back_attn)
    weight_grad(3, gall, dqkv[3].reshape(LW, LW))
    core_t2 = core_send(1)
    quarter = pl.ds(4 * lax.rem(m, 2), 4)
    own = own_back([dqkv[j, m // 2, quarter].reshape(ROWS, LW) for j in range(3)], wt)
    x_t1 = core_sum_x_send(0, core_t1)
    z_t2 = core_sum_z_send(1, core_t2)
    ag_d = []
    for at, rows in enumerate(halves):
        wait_all(rs2[at])
        d_nh = own[rows]
        for k in range(3):
            d_nh = d_nh + rrecv[1, k, rows].astype(F32)
        hidden = hid[rows]
        inv_h = lax.rsqrt(jnp.mean(hidden * hidden, -1, keepdims=True) + EPS)
        d_hidden = g_ref[rows].astype(F32) + norm_back(hidden, inv_h, d_nh)
        dhid[rows] = d_hidden
        dhall[m, rows] = d_hidden.astype(BF16)
        ag_d += gather_mp((5, 11)[at], dhall.at[m], dhall, rows)
    z_t1 = x_sum_z_send(0, x_t1)
    wait_all(ag_d)

    weight_grad(7, dhall, attns[...].reshape(LW, LW))
    core_o = core_send(5)
    das = dot_bt(dhall[...].reshape(LW, D), wos[...]).astype(BF16)

    def keep(j, grad):
        dqs[j] = grad.astype(BF16).reshape(MP, ROWS, LW)
        weight_grad_x(4 + j, dqs[j].reshape(LW, LW))
        return core_send(2 + j)

    d_v = zero
    for h in range(HEADS_LOC):
        d_v = d_v + dot(p_turned[h], das * masks[h])
    core_v = keep(2, d_v)
    x_o = core_sum_x_send(5, core_o)
    d_q, d_k = zero, zero
    for h in range(HEADS_LOC):
        ds = score_grads(probs[h], dot_bt(das * masks[h], qkvs[2]))
        d_q = d_q + dot(ds, qkvs[1] * masks[h])
        d_k = d_k + dot_at(ds, qkvs[0] * masks[h])
    z_v = core_sum_z_send(4, core_v)
    core_q = keep(0, d_q)
    core_k = keep(1, d_k)
    x_q = core_sum_x_send(2, core_q)
    x_k = core_sum_x_send(3, core_k)
    project_back(2, [dqs[j].reshape(LW, LW) for j in range(3)], ws)
    rs3 = scatter_mp(6, 2)
    stores = []

    def store(source, target):
        copy = pltpu.make_async_copy(source, target, out_sem.at[len(stores)])
        copy.start()
        stores.append(copy)

    x_t2 = z_sum_x_send(1, z_t2)
    z_o = x_sum_z_send(5, x_o)
    z_sum(0, z_t1, [gt_ref.at[0], gt_ref.at[1]])
    d_nx = own_back([dqs[j, m] for j in range(3)], ws)
    z_q = x_sum_z_send(2, x_q)
    x_sum(1, x_t2, [gt_ref.at[2], gto_ref])
    z_k = x_sum_z_send(3, x_k)
    store(gt_ref, gt_out)
    store(gto_ref, gto_out)
    x_v = z_sum_x_send(4, z_v)
    wait_all(rs3)
    for k in range(3):
        d_nx = d_nx + rrecv[2, k].astype(F32)
    x = x_ref[...].astype(F32)
    inv_x = lax.rsqrt(jnp.mean(x * x, -1, keepdims=True) + EPS)
    tok_ref[...] = (dhid[...] + norm_back(x, inv_x, d_nx)).astype(BF16)
    store(tok_ref, tok_out)
    z_sum(5, z_o, [gso_ref])
    store(gso_ref, gso_out)
    x_sum(4, x_v, [gs_ref.at[2]])
    store(gs_ref.at[2], gs_out.at[2])
    z_sum(2, z_q, [gs_ref.at[0]])
    store(gs_ref.at[0], gs_out.at[0])
    z_sum(3, z_k, [gs_ref.at[1]])
    store(gs_ref.at[1], gs_out.at[1])
    for copy in pending:
        copy.wait_send()
    for part in range(3):
        hand_wait(part).wait_send()
    for copy in stores:
        copy.wait()


def deliver(*refs):
    for source, target in zip(refs[:5], refs[5:]):
        target[...] = source[...]


def shards(x, g, ws, wos, wt, wot, clip_frames):
    clips = clip_frames.shape[0]
    vmem = pl.BlockSpec(memory_space=pltpu.VMEM)
    dma = pltpu.SemaphoreType.DMA
    scratch = [
        pltpu.VMEM((ROWS, D), BF16),
        pltpu.VMEM((3, 16, LW), F32),
        pltpu.VMEM((16, LW), F32),
        pltpu.VMEM((3, 16, LW), F32),
        pltpu.VMEM((16, LW), F32),
        dma((7,)),
        pltpu.VMEM((ROWS, D), BF16),
        pltpu.VMEM((ROWS, D), BF16),
        pltpu.VMEM((1, clips), jnp.int32),
        pltpu.VMEM((3, D, LW), BF16),
        pltpu.VMEM((LW, D), BF16),
        pltpu.VMEM((3, D, LW), BF16),
        pltpu.VMEM((LW, D), BF16),
        pltpu.VMEM((MP, ROWS, D), BF16),
        pltpu.VMEM((MP, ROWS, D), BF16),
        pltpu.VMEM((MP, ROWS, D), BF16),
        pltpu.VMEM((MP, ROWS, D), BF16),
        pltpu.VMEM((LW, LW), F32),
        pltpu.VMEM((3, LW, LW), BF16),
        pltpu.VMEM((HEADS_LOC, LW, LW), F32),
        pltpu.VMEM((4, LW, LW), BF16),
        pltpu.VMEM((HEADS_LOC, LW, LW), BF16),
        pltpu.VMEM((MP, ROWS, LW), BF16),
        pltpu.VMEM((ROWS, D), F32),
        pltpu.VMEM((ROWS, D), F32),
        pltpu.VMEM((3, MP, ROWS, D), BF16),
        pltpu.VMEM((3, MP - 1, ROWS, D), BF16),
        pltpu.VMEM((4, 2, PL, 16, LW), BF16),
        pltpu.VMEM((4, 2, 16, 16, LW), BF16),
        pltpu.VMEM((4, 2, PL, 16, LW), BF16),
        pltpu.VMEM((4, 2, PL, 16, LW), BF16),
        pltpu.VMEM((3, MP, ROWS, LW), BF16),
        pltpu.VMEM((8, FR // 2, 2, 16, LW), BF16),
        pltpu.VMEM((8, FR // 2, 16, LW), BF16),
        pltpu.VMEM((8, ZS, XS, 16, LW), BF16),
        pltpu.VMEM((XS - 1, 8, ZS, 16, LW), BF16),
        pltpu.VMEM((8, ZS, 16, LW), BF16),
        pltpu.VMEM((ZS - 1, 8, 16, LW), BF16),
        pltpu.VMEM((ZS - 1, 8, XS, 16, LW), BF16),
        pltpu.VMEM((8, XS, 16, LW), BF16),
        pltpu.VMEM((XS - 1, 8, 16, LW), BF16),
        dma((7,)),
        dma((12, 3)),
        dma((12, 3)),
        dma((3, PL - 1)),
        dma((3, PL - 1)),
        dma((3,)),
        dma((3,)),
        dma((3, PL - 1)),
        dma((3, PL - 1)),
        dma((6,)),
        dma((6,)),
        dma((6, XS - 1)),
        dma((6, XS - 1)),
        dma((6, ZS - 1)),
        dma((6, ZS - 1)),
    ]
    tokens, gs, gso, gt, gto = pl.pallas_call(
        kernel,
        out_shape=(
            jax.ShapeDtypeStruct((ROWS, D), BF16),
            jax.ShapeDtypeStruct((3, 16, LW), F32),
            jax.ShapeDtypeStruct((16, LW), F32),
            jax.ShapeDtypeStruct((3, 16, LW), F32),
            jax.ShapeDtypeStruct((16, LW), F32),
        ),
        in_specs=[pl.BlockSpec(memory_space=pltpu.HBM)] * 7,
        out_specs=[pl.BlockSpec(memory_space=pl.ANY)] * 5,
        scratch_shapes=scratch,
        compiler_params=pltpu.CompilerParams(
            collective_id=0, has_side_effects=True, vmem_limit_bytes=60 * 1024 * 1024
        ),
        cost_estimate=pl.CostEstimate(
            flops=3_500_000_000, bytes_accessed=6_000_000, transcendentals=1_000_000
        ),
    )(
        x.reshape(ROWS, D), g.reshape(ROWS, D), clip_frames.reshape(1, clips), ws, wos, wt, wot,
    )
    results = (tokens, gs, gso, gt, gto)
    tokens, gs, gso, gt, gto = pl.pallas_call(
        deliver,
        out_shape=tuple(jax.ShapeDtypeStruct(r.shape, r.dtype) for r in results),
        in_specs=[vmem] * 5,
        out_specs=[vmem] * 5,
        compiler_params=pltpu.CompilerParams(vmem_limit_bytes=60 * 1024 * 1024),
    )(*results)
    return tokens.reshape(1, ROWS, D), gs, gso.T, gt, gto.T


def solution(mesh):
    placed = (
        P("frames", "mp", None),
        P("frames", "mp", None),
        P(None, None, "mp"),
        P("mp", None),
        P(None, None, "mp"),
        P("mp", None),
        P(),
    )
    return jax.shard_map(
        shards,
        mesh=mesh,
        in_specs=placed,
        out_specs=(
            P("frames", "mp", None),
            P(None, "frames", "mp"),
            P("mp", "frames"),
            P(None, "frames", "mp"),
            P("mp", "frames"),
        ),
        check_vma=False,
    )
```

```python
import jax
import jax.numpy as jnp
from jax import lax
from jax.experimental import pallas as pl
from jax.experimental.pallas import tpu as pltpu
from jax.sharding import PartitionSpec as P

HD = 64
EPS = 1e-06
NEGATIVE = -1e30
FR = 64
MP = 4
XS = 4
ZS = 8
PL = 8
HALO = 3
D = 1024
LW = 256
ROWS = 64
HEADS_LOC = 4
MESH = pl.DeviceIdType.MESH
F32 = jnp.float32
BF16 = jnp.bfloat16


def dot(a, b):
    return lax.dot_general(a, b, (((1,), (0,)), ((), ())), preferred_element_type=F32)


def dot_bt(a, b):
    return lax.dot_general(a, b, (((1,), (1,)), ((), ())), preferred_element_type=F32)


def dot_at(a, b):
    return lax.dot_general(a, b, (((0,), (0,)), ((), ())), preferred_element_type=F32)


def head_mask(h):
    lane = lax.broadcasted_iota(jnp.int32, (1, LW), 1)
    return jnp.where(lane // HD == h, 1.0, 0.0).astype(BF16)


def softmax(scores):
    expo = jnp.exp(scores - jnp.max(scores, -1, keepdims=True))
    return expo / jnp.sum(expo, -1, keepdims=True)


def score_grads(probs, d_probs):
    delta = jnp.sum(probs * d_probs, -1, keepdims=True)
    return (probs * (d_probs - delta) * HD ** (-0.5)).astype(BF16)


def norm_back(values_in, inv_rms, upstream):
    mean = jnp.mean(upstream * values_in, -1, keepdims=True)
    return inv_rms * (upstream - values_in * (inv_rms * inv_rms) * mean)


def kernel(
    x_hbm, g_hbm, cf_hbm, ws_hbm, wos_hbm, wt_hbm, wot_hbm,
    tok_out, gs_out, gso_out, gt_out, gto_out,
    tok_ref, gs_ref, gso_ref, gt_ref, gto_ref, out_sem,
    x_ref, g_ref, cf_row, ws, wos, wt, wot, xall, gall, nhall, dhall,
    bias, qkvs, probs, x_turned, p_turned, attns, hid, dhid,
    rsend, rrecv, tsend, tbuf, tres, dqkv, dqs,
    gbuf, grecv1, gsum1, grecv2, gsum2, grecv3, hrecv2, hsum2, hrecv3,
    w_sem, mp_send, mp_recv, t_send, t_recv, h_send, h_recv, b_send, b_recv,
    c_send, c_recv, x_send, x_recv, z_send, z_recv,
):
    f = lax.axis_index("frames")
    m = lax.axis_index("mp")
    core = lax.rem(f, 2)
    xpos = lax.rem(f // 2, XS)
    zpos = f // PL
    w = lax.rem(f, PL)

    def remote(src, dst, ssem, rsem, to_f, to_m):
        return pltpu.make_async_remote_copy(
            src_ref=src, dst_ref=dst, send_sem=ssem, recv_sem=rsem,
            device_id=(to_f, to_m), device_id_type=MESH,
        )

    pending = []

    loads = [
        pltpu.make_async_copy(hbm, vmem, w_sem.at[i])
        for i, (hbm, vmem) in enumerate(
            (
                (x_hbm, x_ref), (g_hbm, g_ref), (cf_hbm, cf_row),
                (ws_hbm, ws), (wos_hbm, wos), (wot_hbm, wot), (wt_hbm, wt),
            )
        )
    ]
    for load in loads:
        load.start()

    barrier = pltpu.get_barrier_semaphore()

    for k in range(1, MP):
        pl.semaphore_signal(
            barrier, inc=1, device_id=(f, lax.rem(m + k, MP)), device_id_type=MESH
        )
    for k in range(1, PL):
        pl.semaphore_signal(
            barrier, inc=1, device_id=(zpos * PL + lax.rem(w + k, PL), m), device_id_type=MESH
        )
    for k in range(1, ZS):
        pl.semaphore_signal(
            barrier, inc=1, device_id=(lax.rem(zpos + k, ZS) * PL + w, m), device_id_type=MESH
        )

    def gather_mp(phase, src, buf, rows=slice(0, ROWS)):
        copies = []
        for k in (1, 3, 2):
            copy = remote(
                src.at[rows], buf.at[m, rows], mp_send.at[phase, k - 1], mp_recv.at[phase, k - 1],
                f, lax.rem(m + k, MP),
            )
            copy.start()
            copies.append(copy)
        pending.extend(copies)
        return copies

    def scatter_mp(phase, which, rows=slice(0, ROWS)):
        copies = []
        for k in (1, 3, 2):
            to = lax.rem(m + k, MP)
            copy = remote(
                rsend.at[which, to, rows], rrecv.at[which, k - 1, rows],
                mp_send.at[phase, k - 1], mp_recv.at[phase, k - 1], f, to,
            )
            copy.start()
            copies.append(copy)
        pending.extend(copies)
        return copies

    loads[0].wait()
    x = x_ref[...].astype(F32)
    inv_x = lax.rsqrt(jnp.mean(x * x, -1, keepdims=True) + EPS)
    xall[m] = (x * inv_x).astype(BF16)
    pl.semaphore_wait(barrier, MP - 1 + PL - 1 + ZS - 1)

    ag_x = gather_mp(0, xall.at[m], xall)

    loads[1].wait()
    loads[2].wait()
    gall[m] = g_ref[...]
    row = lax.broadcasted_iota(jnp.int32, (LW, LW), 0)
    col = lax.broadcasted_iota(jnp.int32, (LW, LW), 1)
    clips = cf_row.shape[1]
    c_row = lax.broadcasted_iota(jnp.int32, (clips, clips), 0)
    c_col = lax.broadcasted_iota(jnp.int32, (clips, clips), 1)
    ends_col = jnp.sum(jnp.where(c_col <= c_row, cf_row[...], 0), axis=1, keepdims=True)
    ends_row = jnp.sum(jnp.where(c_row == c_col, ends_col, 0), axis=0, keepdims=True)

    def clip_of(slot, ends, axis):
        frame = lax.rem(zpos * PL + FR - HALO + slot, FR)
        count = jnp.sum(jnp.where(frame >= ends, 1, 0), axis=axis, keepdims=True)
        return count

    slot_lane = lax.broadcasted_iota(jnp.int32, (clips, LW), 1) // 16
    slot_sub = lax.broadcasted_iota(jnp.int32, (LW, clips), 0) // 16
    id_lane = clip_of(slot_lane, ends_col, 0)
    id_sub = clip_of(slot_sub, ends_row, 1)
    used = PL + 2 * HALO
    id_lane = jnp.where(col[:1] // 16 < used, id_lane, -1)
    id_sub = jnp.where(row[:, :1] // 16 < used, id_sub, -1)
    same = jnp.logical_and(id_lane == id_sub, row % 16 == col % 16)
    bias[...] = jnp.where(same, 0.0, NEGATIVE)
    for t in range(4):
        for g in range(2):
            tbuf[t, g, used:] = jnp.zeros((16 - used, 16, LW), BF16)

    halves = [slice(0, ROWS // 2), slice(ROWS // 2, ROWS)]
    quarters = [slice(16 * at, 16 * at + 16) for at in range(4)]
    masks = [head_mask(h) for h in range(HEADS_LOC)]

    loads[3].wait()
    for copy in ag_x:
        copy.wait_recv()
    near_g = {}
    for k in (1, 3):
        near_g[k] = remote(
            g_ref, gall.at[m], mp_send.at[1, k - 1], mp_recv.at[1, k - 1], f, lax.rem(m + k, MP)
        )
        near_g[k].start()
        pending.append(near_g[k])
    x_all = xall[...].reshape(LW, D)
    for j in range(3):
        qkvs[j] = dot(x_all, ws[j]).astype(BF16)

    total = jnp.zeros((LW, LW), F32)
    for h in range(HEADS_LOC):
        p = softmax(dot_bt(qkvs[0] * masks[h], qkvs[1]) * HD ** (-0.5))
        probs[h] = p
        total = total + dot(p.astype(BF16), qkvs[2] * masks[h])
    attn = total.astype(BF16)
    attns[...] = attn.reshape(MP, ROWS, LW)

    loads[4].wait()
    for c in range(4):
        cols = pl.ds(c * 256, 256)
        rsend[0, :, :, cols] = dot(attn, wos[:, cols]).astype(BF16).reshape(MP, ROWS, 256)
    rs1 = [scatter_mp(p, 0, rows) for p, rows in zip((2, 8, 16, 17), quarters)]
    own = dot(attns[m], wos[...])
    for c in range(4):
        x_turned[c] = xall[:, :, c * 256 : (c + 1) * 256].reshape(LW, 256).T
    for h in range(HEADS_LOC):
        p_turned[h] = probs[h].astype(BF16).T
    far_g = []
    for k, rows in zip((1, 3), halves):
        near_g[k].wait_recv()
        chunk = gall.at[lax.rem(m + MP - k, MP), rows]
        copy = remote(
            chunk, chunk, mp_send.at[7, k - 1], mp_recv.at[7, k - 1], f, lax.rem(m + k, MP)
        )
        copy.start()
        far_g.append(copy)
    pending.extend(far_g)

    ag_h = []
    for at, rows in enumerate(quarters):
        for copy in rs1[at]:
            copy.wait_recv()
        hidden = x_ref[rows].astype(F32) + own[rows]
        for k in range(3):
            hidden = hidden + rrecv[0, k, rows].astype(F32)
        inv_h = lax.rsqrt(jnp.mean(hidden * hidden, -1, keepdims=True) + EPS)
        hid[rows] = hidden
        nhall[m, rows] = (hidden * inv_h).astype(BF16)
        ag_h += gather_mp((3, 9, 18, 19)[at], nhall.at[m], nhall, rows)

    def plane_send(part, source, target, ssems, rsems):
        copies = []
        for k in range(1, PL):
            to = lax.rem(w + k, PL)
            copy = remote(
                source(to), target, ssems.at[part, k - 1], rsems.at[part, k - 1],
                zpos * PL + to, m,
            )
            copy.start()
            copies.append(copy)
        pending.extend(copies)
        return copies

    def halo_view(part, slots):
        return tbuf.at[3, :, slots] if part == 2 else tbuf.at[:3, part, slots]

    def hand_on(part, frame):
        def to_plane(step, slot):
            return remote(
                halo_view(part, HALO + frame), halo_view(part, slot),
                h_send.at[part], h_recv.at[part], lax.rem(zpos + step, ZS) * PL + w, m,
            )

        @pl.when(frame < HALO)
        def _():
            to_plane(ZS - 1, HALO + PL + frame).start()

        @pl.when(frame >= PL - HALO)
        def _():
            to_plane(1, frame - (PL - HALO)).start()

    def hand_wait(part):
        some = halo_view(part, pl.ds(0, 2 * HALO))
        return remote(some, some, h_send.at[part], h_recv.at[part], f, m)

    def receive(part, copies):
        hand_on(part, w)
        for k in range(1, PL):
            copies[k - 1].wait_recv()
            hand_on(part, lax.rem(w + PL - k, PL))

    loads[5].wait()
    for copy in far_g:
        copy.wait_recv()
    tsend[3] = dot_bt(gall[...].reshape(LW, D), wot[...]).astype(BF16).reshape(2, PL, 16, LW)
    there_up = plane_send(
        2, lambda to: tsend.at[3, :, to], halo_view(2, HALO + w), t_send, t_recv
    )
    for g in range(2):
        tbuf[3, g, HALO + w] = tsend[3, g, w]
    receive(2, there_up)
    loads[6].wait()
    for copy in ag_h:
        copy.wait_recv()
    h_all = nhall[...].reshape(LW, D)
    for j in range(3):
        tsend[j] = dot(h_all, wt[j]).astype(BF16).reshape(2, PL, 16, LW)

    there = [
        plane_send(g, lambda to, g=g: tsend.at[:3, g, to], halo_view(g, HALO + w), t_send, t_recv)
        for g in range(2)
    ]
    for t in range(3):
        for g in range(2):
            tbuf[t, g, HALO + w] = tsend[t, g, w]

    for g in range(2):
        receive(g, there[g])

    zero = jnp.zeros((LW, LW), F32)
    own_slots = slice(HALO, HALO + PL)
    back = []
    for g in range(2):
        hand_wait(g).wait_recv()
        if g == 0:
            hand_wait(2).wait_recv()
        queries, keys, values, upstream = [tbuf[t, g].reshape(LW, LW) for t in range(4)]
        attn_t, d_q, d_k, d_v = zero, zero, zero, zero
        for h in range(HEADS_LOC):
            qm = queries * masks[h]
            om = upstream * masks[h]
            p = softmax(dot_bt(qm, keys) * HD ** (-0.5) + bias[...])
            pb = p.astype(BF16)
            attn_t = attn_t + dot(pb, values * masks[h])
            d_v = d_v + dot_at(pb, om)
            ds = score_grads(p, dot_bt(om, values))
            d_q = d_q + dot(ds, keys * masks[h])
            d_k = d_k + dot_at(ds, qm)
        for t, full in enumerate((d_q, d_k, d_v, attn_t)):
            tres[t, g] = full.astype(BF16).reshape(16, 16, LW)[own_slots]
        back += plane_send(
            g, lambda to, g=g: tres.at[:3, g, to], dqkv.at[:3, g, w], b_send, b_recv
        )
        for t in range(4):
            dqkv[t, g, w] = tres[t, g, w]
    back_attn = plane_send(2, lambda to: tres.at[3, :, to], dqkv.at[3, :, w], b_send, b_recv)

    def project_back(which, grads, weights):
        for c in range(4):
            cols = pl.ds(c * 256, 256)
            part = dot_bt(grads[0], weights[0, cols])
            part = part + dot_bt(grads[1], weights[1, cols])
            part = part + dot_bt(grads[2], weights[2, cols])
            rsend[which, :, :, cols] = part.astype(BF16).reshape(MP, ROWS, 256)

    def own_back(grads, weights):
        part = dot_bt(grads[0], weights[0])
        part = part + dot_bt(grads[1], weights[1])
        return part + dot_bt(grads[2], weights[2])

    def weight_grad(j, left_ref, right):
        for c in range(4):
            left = left_ref[:, :, c * 256 : (c + 1) * 256].reshape(LW, 256)
            gbuf[j, 8 * c : 8 * c + 8] = dot_at(left, right).astype(BF16).reshape(8, 2, 16, LW)

    def weight_grad_x(j, right):
        for c in range(4):
            part = dot(x_turned[c], right)
            gbuf[j, 8 * c : 8 * c + 8] = part.astype(BF16).reshape(8, 2, 16, LW)

    first = [0, 2, 4, 5, 6, 7]
    count = [2, 2, 1, 1, 1, 1]

    def core_send(b):
        some = slice(first[b], first[b] + count[b])
        copy = remote(
            gbuf.at[some, :, 1 - core], grecv1.at[some],
            c_send.at[b], c_recv.at[b], f + 1 - 2 * core, m,
        )
        copy.start()
        pending.append(copy)
        return copy

    def send_x(b, source, target):
        copies = []
        for k in (1, 3, 2):
            to = lax.rem(xpos + k, XS)
            copy = remote(
                source(to), target(k - 1), x_send.at[b, k - 1], x_recv.at[b, k - 1],
                (zpos * XS + to) * 2 + core, m,
            )
            copy.start()
            copies.append(copy)
        pending.extend(copies)
        return copies

    def send_z(b, source, target):
        copies = []
        for k in (4, 3, 5, 2, 6, 1, 7):
            to = lax.rem(zpos + k, ZS)
            copy = remote(
                source(to), target(k - 1), z_send.at[b, k - 1], z_recv.at[b, k - 1],
                (to * XS + xpos) * 2 + core, m,
            )
            copy.start()
            copies.append(copy)
        pending.extend(copies)
        return copies

    def mats(b):
        return slice(first[b], first[b] + count[b])

    def wait_all(copies):
        for copy in copies:
            copy.wait_recv()

    def core_sum(b, copy):
        copy.wait_recv()
        for j in range(first[b], first[b] + count[b]):
            summed = gbuf[j, :, core].astype(F32) + grecv1[j].astype(F32)
            gsum1[j] = summed.astype(BF16).reshape(ZS, XS, 16, LW)

    def core_sum_x_send(b, copy):
        core_sum(b, copy)
        return send_x(b, lambda to: gsum1.at[mats(b), :, to], lambda k: grecv2.at[k, mats(b)])

    def core_sum_z_send(b, copy):
        core_sum(b, copy)
        return send_z(b, lambda to: gsum1.at[mats(b), to], lambda k: hrecv2.at[k, mats(b)])

    def x_sum_z_send(b, copies):
        wait_all(copies)
        for j in range(first[b], first[b] + count[b]):
            summed = gsum1[j, :, xpos].astype(F32)
            for k in range(XS - 1):
                summed = summed + grecv2[k, j].astype(F32)
            gsum2[j] = summed.astype(BF16)
        return send_z(b, lambda to: gsum2.at[mats(b), to], lambda k: grecv3.at[k, mats(b)])

    def z_sum_x_send(b, copies):
        wait_all(copies)
        for j in range(first[b], first[b] + count[b]):
            summed = gsum1[j, zpos].astype(F32)
            for k in range(ZS - 1):
                summed = summed + hrecv2[k, j].astype(F32)
            hsum2[j] = summed.astype(BF16)
        return send_x(b, lambda to: hsum2.at[mats(b), to], lambda k: hrecv3.at[k, mats(b)])

    def z_sum(b, copies, outs):
        wait_all(copies)
        for at, out in enumerate(outs):
            j = first[b] + at
            summed = gsum2[j, zpos].astype(F32)
            for k in range(ZS - 1):
                summed = summed + grecv3[k, j].astype(F32)
            out[...] = summed

    def x_sum(b, copies, outs):
        wait_all(copies)
        for at, out in enumerate(outs):
            j = first[b] + at
            summed = hsum2[j, xpos].astype(F32)
            for k in range(XS - 1):
                summed = summed + hrecv3[k, j].astype(F32)
            out[...] = summed

    rs2 = []
    for phase, rows in zip((4, 10, 12, 13), quarters):
        copies = []
        for k in (1, 3, 2):
            to = lax.rem(m + k, MP)
            copies.append(remote(
                rsend.at[1, to, rows], rrecv.at[1, k - 1, rows],
                mp_send.at[phase, k - 1], mp_recv.at[phase, k - 1], f, to,
            ))
        rs2.append(copies)
        pending.extend(copies)
    for g in range(2):
        wait_all(back[g * (PL - 1) : (g + 1) * (PL - 1)])
        grads = [dqkv[j, g].reshape(LW // 2, LW) for j in range(3)]
        for c in range(4):
            cols = pl.ds(c * 256, 256)
            part = dot_bt(grads[0], wt[0, cols])
            part = part + dot_bt(grads[1], wt[1, cols])
            part = part + dot_bt(grads[2], wt[2, cols])
            rsend[1, 2 * g : 2 * g + 2, :, cols] = part.astype(BF16).reshape(2, ROWS, 256)
        for copies in rs2:
            for k, copy in zip((1, 3, 2), copies):

                @pl.when(lax.rem(m + k, MP) // 2 == g)
                def _():
                    copy.start()

    grads_t = [dqkv[j].reshape(LW, LW) for j in range(3)]
    for j in range(2):
        weight_grad(j, nhall, grads_t[j])
    core_t1 = core_send(0)
    weight_grad(2, nhall, grads_t[2])
    wait_all(back_attn)
    weight_grad(3, gall, dqkv[3].reshape(LW, LW))
    core_t2 = core_send(1)
    quarter = pl.ds(4 * lax.rem(m, 2), 4)
    own = own_back([dqkv[j, m // 2, quarter].reshape(ROWS, LW) for j in range(3)], wt)
    x_t1 = core_sum_x_send(0, core_t1)
    z_t2 = core_sum_z_send(1, core_t2)
    ag_d = []
    for at, rows in enumerate(quarters):
        wait_all(rs2[at])
        d_nh = own[rows]
        for k in range(3):
            d_nh = d_nh + rrecv[1, k, rows].astype(F32)
        hidden = hid[rows]
        inv_h = lax.rsqrt(jnp.mean(hidden * hidden, -1, keepdims=True) + EPS)
        d_hidden = g_ref[rows].astype(F32) + norm_back(hidden, inv_h, d_nh)
        dhid[rows] = d_hidden
        dhall[m, rows] = d_hidden.astype(BF16)
        ag_d += gather_mp((5, 11, 14, 15)[at], dhall.at[m], dhall, rows)
    z_t1 = x_sum_z_send(0, x_t1)
    wait_all(ag_d)

    weight_grad(7, dhall, attns[...].reshape(LW, LW))
    core_o = core_send(5)
    das = dot_bt(dhall[...].reshape(LW, D), wos[...]).astype(BF16)

    def keep(j, grad):
        dqs[j] = grad.astype(BF16).reshape(MP, ROWS, LW)
        weight_grad_x(4 + j, dqs[j].reshape(LW, LW))
        return core_send(2 + j)

    d_v = zero
    for h in range(HEADS_LOC):
        d_v = d_v + dot(p_turned[h], das * masks[h])
    core_v = keep(2, d_v)
    x_o = core_sum_x_send(5, core_o)
    d_q, d_k = zero, zero
    for h in range(HEADS_LOC):
        ds = score_grads(probs[h], dot_bt(das * masks[h], qkvs[2]))
        d_q = d_q + dot(ds, qkvs[1] * masks[h])
        d_k = d_k + dot_at(ds, qkvs[0] * masks[h])
    z_v = core_sum_z_send(4, core_v)
    core_q = keep(0, d_q)
    core_k = keep(1, d_k)
    x_q = core_sum_x_send(2, core_q)
    x_k = core_sum_x_send(3, core_k)
    project_back(2, [dqs[j].reshape(LW, LW) for j in range(3)], ws)
    rs3 = scatter_mp(6, 2)
    stores = []

    def store(source, target):
        copy = pltpu.make_async_copy(source, target, out_sem.at[len(stores)])
        copy.start()
        stores.append(copy)

    x_t2 = z_sum_x_send(1, z_t2)
    z_o = x_sum_z_send(5, x_o)
    z_sum(0, z_t1, [gt_ref.at[0], gt_ref.at[1]])
    d_nx = own_back([dqs[j, m] for j in range(3)], ws)
    z_q = x_sum_z_send(2, x_q)
    x_sum(1, x_t2, [gt_ref.at[2], gto_ref])
    z_k = x_sum_z_send(3, x_k)
    store(gt_ref, gt_out)
    store(gto_ref, gto_out)
    x_v = z_sum_x_send(4, z_v)
    wait_all(rs3)
    for k in range(3):
        d_nx = d_nx + rrecv[2, k].astype(F32)
    x = x_ref[...].astype(F32)
    inv_x = lax.rsqrt(jnp.mean(x * x, -1, keepdims=True) + EPS)
    tok_ref[...] = (dhid[...] + norm_back(x, inv_x, d_nx)).astype(BF16)
    store(tok_ref, tok_out)
    z_sum(5, z_o, [gso_ref])
    store(gso_ref, gso_out)
    x_sum(4, x_v, [gs_ref.at[2]])
    store(gs_ref.at[2], gs_out.at[2])
    z_sum(2, z_q, [gs_ref.at[0]])
    store(gs_ref.at[0], gs_out.at[0])
    z_sum(3, z_k, [gs_ref.at[1]])
    store(gs_ref.at[1], gs_out.at[1])
    for copy in pending:
        copy.wait_send()
    for part in range(3):
        hand_wait(part).wait_send()
    for copy in stores:
        copy.wait()


def deliver(*refs):
    for source, target in zip(refs[:5], refs[5:]):
        target[...] = source[...]


def shards(x, g, ws, wos, wt, wot, clip_frames):
    clips = clip_frames.shape[0]
    vmem = pl.BlockSpec(memory_space=pltpu.VMEM)
    dma = pltpu.SemaphoreType.DMA
    scratch = [
        pltpu.VMEM((ROWS, D), BF16),
        pltpu.VMEM((3, 16, LW), F32),
        pltpu.VMEM((16, LW), F32),
        pltpu.VMEM((3, 16, LW), F32),
        pltpu.VMEM((16, LW), F32),
        dma((7,)),
        pltpu.VMEM((ROWS, D), BF16),
        pltpu.VMEM((ROWS, D), BF16),
        pltpu.VMEM((1, clips), jnp.int32),
        pltpu.VMEM((3, D, LW), BF16),
        pltpu.VMEM((LW, D), BF16),
        pltpu.VMEM((3, D, LW), BF16),
        pltpu.VMEM((LW, D), BF16),
        pltpu.VMEM((MP, ROWS, D), BF16),
        pltpu.VMEM((MP, ROWS, D), BF16),
        pltpu.VMEM((MP, ROWS, D), BF16),
        pltpu.VMEM((MP, ROWS, D), BF16),
        pltpu.VMEM((LW, LW), F32),
        pltpu.VMEM((3, LW, LW), BF16),
        pltpu.VMEM((HEADS_LOC, LW, LW), F32),
        pltpu.VMEM((4, LW, LW), BF16),
        pltpu.VMEM((HEADS_LOC, LW, LW), BF16),
        pltpu.VMEM((MP, ROWS, LW), BF16),
        pltpu.VMEM((ROWS, D), F32),
        pltpu.VMEM((ROWS, D), F32),
        pltpu.VMEM((3, MP, ROWS, D), BF16),
        pltpu.VMEM((3, MP - 1, ROWS, D), BF16),
        pltpu.VMEM((4, 2, PL, 16, LW), BF16),
        pltpu.VMEM((4, 2, 16, 16, LW), BF16),
        pltpu.VMEM((4, 2, PL, 16, LW), BF16),
        pltpu.VMEM((4, 2, PL, 16, LW), BF16),
        pltpu.VMEM((3, MP, ROWS, LW), BF16),
        pltpu.VMEM((8, FR // 2, 2, 16, LW), BF16),
        pltpu.VMEM((8, FR // 2, 16, LW), BF16),
        pltpu.VMEM((8, ZS, XS, 16, LW), BF16),
        pltpu.VMEM((XS - 1, 8, ZS, 16, LW), BF16),
        pltpu.VMEM((8, ZS, 16, LW), BF16),
        pltpu.VMEM((ZS - 1, 8, 16, LW), BF16),
        pltpu.VMEM((ZS - 1, 8, XS, 16, LW), BF16),
        pltpu.VMEM((8, XS, 16, LW), BF16),
        pltpu.VMEM((XS - 1, 8, 16, LW), BF16),
        dma((7,)),
        dma((20, 3)),
        dma((20, 3)),
        dma((3, PL - 1)),
        dma((3, PL - 1)),
        dma((3,)),
        dma((3,)),
        dma((3, PL - 1)),
        dma((3, PL - 1)),
        dma((6,)),
        dma((6,)),
        dma((6, XS - 1)),
        dma((6, XS - 1)),
        dma((6, ZS - 1)),
        dma((6, ZS - 1)),
    ]
    tokens, gs, gso, gt, gto = pl.pallas_call(
        kernel,
        out_shape=(
            jax.ShapeDtypeStruct((ROWS, D), BF16),
            jax.ShapeDtypeStruct((3, 16, LW), F32),
            jax.ShapeDtypeStruct((16, LW), F32),
            jax.ShapeDtypeStruct((3, 16, LW), F32),
            jax.ShapeDtypeStruct((16, LW), F32),
        ),
        in_specs=[pl.BlockSpec(memory_space=pltpu.HBM)] * 7,
        out_specs=[pl.BlockSpec(memory_space=pl.ANY)] * 5,
        scratch_shapes=scratch,
        compiler_params=pltpu.CompilerParams(
            collective_id=0, has_side_effects=True, vmem_limit_bytes=60 * 1024 * 1024
        ),
        cost_estimate=pl.CostEstimate(
            flops=3_500_000_000, bytes_accessed=6_000_000, transcendentals=1_000_000
        ),
    )(
        x.reshape(ROWS, D), g.reshape(ROWS, D), clip_frames.reshape(1, clips), ws, wos, wt, wot,
    )
    results = (tokens, gs, gso, gt, gto)
    tokens, gs, gso, gt, gto = pl.pallas_call(
        deliver,
        out_shape=tuple(jax.ShapeDtypeStruct(r.shape, r.dtype) for r in results),
        in_specs=[vmem] * 5,
        out_specs=[vmem] * 5,
        compiler_params=pltpu.CompilerParams(vmem_limit_bytes=60 * 1024 * 1024),
    )(*results)
    return tokens.reshape(1, ROWS, D), gs, gso.T, gt, gto.T


def solution(mesh):
    placed = (
        P("frames", "mp", None),
        P("frames", "mp", None),
        P(None, None, "mp"),
        P("mp", None),
        P(None, None, "mp"),
        P("mp", None),
        P(),
    )
    return jax.shard_map(
        shards,
        mesh=mesh,
        in_specs=placed,
        out_specs=(
            P("frames", "mp", None),
            P(None, "frames", "mp"),
            P("mp", "frames"),
            P(None, "frames", "mp"),
            P("mp", "frames"),
        ),
        check_vma=False,
    )
```
